32 devices in a mesh: sp: 4 (over z), fsdp: 8 (over y, x, core).
Axes of the slice: x: 2, y: 2, z: 4, core: 2. Of those that a mesh axis runs over, the one named last changes fastest.
Arguments:
- tokens: bfloat16 [16384, 1024], P(('fsdp', 'sp')), may hold values from -72 to 72
- documents: int32 [16384], replicated, may hold values from 0 to 14, as said below
- expert_routes: int32 [16384, 8], P(('fsdp', 'sp')), may hold values from 0 to 31, all different within a row
- drop_rank: int32 [16384, 8], P(('fsdp', 'sp')), may hold values from 0 to 4095, as said below
- norm1_gain: bfloat16 [1024], P('fsdp'), may hold values from 0.5 to 1.5
- query_weight: bfloat16 [1024, 1024], P('fsdp'), may hold values from -0.75 to 0.75
- key_weight: bfloat16 [1024, 512], P('fsdp'), may hold values from -0.75 to 0.75
- value_weight: bfloat16 [1024, 512], P('fsdp'), may hold values from -0.1875 to 0.1875
- out_weight: bfloat16 [1024, 1024], P('fsdp'), may hold values from -2 to 2
- norm2_gain: bfloat16 [1024], P('fsdp'), may hold values from 0.5 to 1.5
- router_weight: bfloat16 [1024, 32], P('fsdp'), may hold values from -0.09375 to 0.09375
- gate_weight: bfloat16 [32, 1024, 512], P('fsdp'), may hold values from -0.1875 to 0.1875
- up_weight: bfloat16 [32, 1024, 512], P('fsdp'), may hold values from -0.1875 to 0.1875
- down_weight: bfloat16 [32, 512, 1024], P('fsdp'), may hold values from -4 to 4
- output_grad: bfloat16 [16384, 1024], P(('fsdp', 'sp')), may hold values from -6 to 6
Outputs:
- output: bfloat16 [16384, 1024], P(('fsdp', 'sp'))
- input_grad: bfloat16 [16384, 1024], P(('fsdp', 'sp'))
- grad_norm1: float32 [1024], P('fsdp')
- grad_query: float32 [1024, 1024], P('fsdp')
- grad_key: float32 [1024, 512], P('fsdp')
- grad_value: float32 [1024, 512], P('fsdp')
- grad_out: float32 [1024, 1024], P('fsdp')
- grad_norm2: float32 [1024], P('fsdp')
- grad_router: float32 [1024, 32], P('fsdp')
- grad_gate: float32 [32, 1024, 512], P('fsdp')
- grad_up: float32 [32, 1024, 512], P('fsdp')
- grad_down: float32 [32, 512, 1024], P('fsdp')
The draws below stay inside these ranges and needn't reach their ends.
Inputs may be any that keep to these rules, and one draw needn't show every extreme that they name: `documents`: document numbers start at 0, never fall and rise by at most one from a token to the next; a document holds at most 2048 tokens and one holds exactly 2048; no document begins at a positive multiple of 2048. `expert_routes`: each row names 8 different experts. `drop_rank`: within each aligned block of 512 rows the entries are the numbers 0 to 4095, each once.
All inputs are finite; a program needn't handle non-finite values.
Results may differ from the reference program's by a relative error of at most 0.02.
Values may be sent and summed in bfloat16 or wider, within the bound.
No kernel may reach another device: no remote copies, remote signals or barrier semaphores. Data moves between devices by JAX's collectives and lax.ppermute only.
A program may use at most 256 MiB of HBM per device.

```python
import math
import jax
import jax.numpy as jnp
from jax import lax

D = 1024
HQ = 16
HK = 8
HD = 64
E = 32
F = 512
TOPK = 8
TOK_DEV = 512
DOC_MIN = 200
SPAN = 2048
TOKENS = 16384
DOC_MAX = 2048
QBLOCK = 512
CAP = 144


def draw_tokens(key, part):
    key = jax.random.fold_in(key, 5)
    base_key, row_key, column_key = jax.random.split(key, 3)
    base = jnp.clip(jax.random.normal(base_key, (TOKENS, D), jnp.float32), -6.0, 6.0)
    row_scale = jnp.exp(jax.random.uniform(row_key, (TOKENS, 1), jnp.float32, math.log(0.3), math.log(3.0)))
    column_scale = jnp.exp(jax.random.uniform(column_key, (1, D), jnp.float32, math.log(0.4), math.log(4.0)))
    return (base * row_scale * column_scale).astype(jnp.bfloat16)


def draw_documents(key, part):
    key = jax.random.fold_in(key, 11)
    first_key, second_key = jax.random.split(key)
    pair_length = DOC_MAX - 1
    count = TOKENS // pair_length + 2
    cut_point = TOKENS - SPAN - DOC_MAX // 2
    second_base = cut_point + DOC_MAX
    pair_index = jnp.arange(count, dtype=jnp.int32)
    first_split = jax.random.randint(first_key, (count,), DOC_MIN, pair_length - DOC_MIN + 1)
    second_split = jax.random.randint(second_key, (count,), DOC_MIN, pair_length - DOC_MIN + 1)
    pair_first = pair_index * pair_length
    middle_first = pair_first + first_split
    pair_first = jnp.where(pair_first < cut_point, pair_first, TOKENS).astype(jnp.int32)
    middle_first = jnp.where(pair_index * pair_length + pair_length <= cut_point, middle_first, TOKENS).astype(jnp.int32)
    pair_second = second_base + pair_index * pair_length
    middle_second = pair_second + second_split
    pair_second = jnp.where(pair_second < TOKENS, pair_second, TOKENS).astype(jnp.int32)
    middle_second = jnp.where(pair_index * pair_length + pair_length <= TOKENS - second_base, middle_second, TOKENS).astype(jnp.int32)
    marks = jnp.zeros((TOKENS,), jnp.int32)
    marks = marks.at[pair_first].set(1, mode='drop')
    marks = marks.at[middle_first].set(1, mode='drop')
    marks = marks.at[pair_second].set(1, mode='drop')
    marks = marks.at[middle_second].set(1, mode='drop')
    marks = marks.at[cut_point].set(1)
    marks = marks.at[second_base].set(1)
    marks = marks.at[0].set(1)
    place = jnp.arange(TOKENS, dtype=jnp.int32)
    border = (place % SPAN == 0) & (place > 0)
    moved = jnp.where(border, marks, 0)
    marks = jnp.maximum(marks - moved, jnp.roll(moved, 1))
    return (jnp.cumsum(marks) - 1).astype(jnp.int32)


def draw_drop_rank(key, part):
    key = jax.random.fold_in(key, 23)
    block_keys = jax.random.split(key, TOKENS // TOK_DEV)
    ranking = jax.vmap(lambda single: jax.random.permutation(single, TOK_DEV * TOPK))(block_keys)
    return ranking.reshape(TOKENS, TOPK).astype(jnp.int32)


def level_of(key, extent, cuts, smallest, top_value):
    level, own = 1.0, jax.random.fold_in(key, 6)
    for axis_at, parts in cuts:
        heights = jnp.exp(jax.random.uniform(jax.random.fold_in(own, axis_at), (parts,), jnp.float32, smallest / len(cuts), top_value / len(cuts)))
        level = level * jnp.repeat(heights, extent[axis_at] // parts).reshape([-1 if axis == axis_at else 1 for axis in range(len(extent))])
    return level


def choose_distinct(key, rows, amount, top, lift):
    sequence = jax.random.permutation(jax.random.fold_in(key, 1), amount)
    pull = sequence
    for power in range(3):
        pull = pull * pull // amount
    pull = pull * lift // amount
    lots = jax.random.randint(jax.random.fold_in(key, 2), (rows, amount), 0, 4096) + pull
    holders = jax.random.permutation(jax.random.fold_in(key, 3), rows)[jnp.arange(amount) % rows]
    lots = jnp.where(jnp.arange(rows)[:, None] == holders[None, :], 1 << 14, lots)
    merit = lots * amount + jnp.arange(amount)
    return lax.top_k(merit.astype(jnp.int32), top)[1].astype(jnp.int32)


def normal_values(own_key, extent, width, limit, shards=(), kind=jnp.bfloat16):
    drawn = jax.random.normal(own_key, extent, jnp.float32) * width
    if len(shards) > 0:
        drawn = level_of(own_key, extent, shards, -0.22, 0.18) * drawn
    return jnp.clip(drawn, min=-limit, max=limit).astype(kind)


def setup_inputs(seed: int = 0) -> dict:
    key_of = jax.random.split(jax.random.key(seed), 16)
    return {
        "tokens": draw_tokens(jax.random.fold_in(key_of[15], 71), 0),
        "documents": draw_documents(jax.random.fold_in(key_of[15], 71), 0),
        "expert_routes": choose_distinct(key_of[2], TOKENS, E, TOPK, 2048),
        "drop_rank": draw_drop_rank(jax.random.fold_in(key_of[15], 71), 0),
        "norm1_gain": jnp.clip(1.0 + 0.1 * jax.random.normal(key_of[4], (D,), jnp.float32), 0.5, 1.5).astype(jnp.bfloat16),
        "query_weight": normal_values(key_of[5], (D, HQ * HD), (D // 16) ** -0.5, 0.75, ((0, 8),)),
        "key_weight": normal_values(key_of[6], (D, HK * HD), (D // 16) ** -0.5, 0.75, ((0, 8),)),
        "value_weight": normal_values(key_of[7], (D, HK * HD), D ** -0.5, 0.1875, ((0, 8),)),
        "out_weight": normal_values(key_of[8], (HQ * HD, D), (HQ * HD // 128) ** -0.5, 2.0, ((0, 8),)),
        "norm2_gain": jnp.clip(1.0 + 0.1 * jax.random.normal(key_of[9], (D,), jnp.float32), 0.5, 1.5).astype(jnp.bfloat16),
        "router_weight": normal_values(key_of[10], (D, E), (4 * D) ** -0.5, 0.09375, ((0, 8),)),
        "gate_weight": normal_values(key_of[11], (E, D, F), D ** -0.5, 0.1875, ((0, 8),)),
        "up_weight": normal_values(key_of[12], (E, D, F), D ** -0.5, 0.1875, ((0, 8),)),
        "down_weight": normal_values(key_of[13], (E, F, D), 2 ** -0.5, 4.0, ((0, 8),)),
        "output_grad": normal_values(key_of[14], (TOKENS, D), 1.0, 6.0, ((0, 32),)),
    }


attend_scale = 0.015625
branch_scale = 0.22
norm_eps = 1e-06
rope_base = 10000.0
masked_score = -1e+30

@jax.custom_vjp
def low(v):
    return lax.optimization_barrier(v.astype(jnp.bfloat16)).astype(jnp.float32)

@jax.custom_vjp
def low_back(v):
    return v

def low_keep(v):
    return (low(v), None)

def low_pass(kept, grad):
    return (grad,)

def back_keep(v):
    return (v, None)

def back_low(kept, grad):
    return (low(grad),)
low.defvjp(low_keep, low_pass)
low_back.defvjp(back_keep, back_low)

def rms_norm(values, gain):
    return values * lax.rsqrt(lax.optimization_barrier(jnp.mean(values * values, axis=-1, keepdims=True)) + norm_eps) * gain

def doc_position(documents):
    length = documents.shape[0]
    place = jnp.arange(length, dtype=jnp.int32)
    fresh = jnp.concatenate([jnp.ones((1,), dtype=bool), documents[1:] != documents[:-1]])
    opening = lax.cummax(jnp.where(fresh, place, 0), axis=0)
    return place - opening

def rope_tables(position, head_size):
    half_size = head_size // 2
    spacing = jnp.arange(half_size, dtype=jnp.float32)
    inverse = rope_base ** (-2.0 * spacing / head_size)
    angle = position.astype(jnp.float32)[:, None] * inverse[None, :]
    return (jnp.tile(jnp.cos(angle), (1, 2)), jnp.tile(jnp.sin(angle), (1, 2)))

def rotate(values, cosine, sine_table):
    half_size = values.shape[-1] // 2
    turned = jnp.concatenate([-values[..., half_size:], values[..., :half_size]], axis=-1)
    return values * cosine[:, None, :] + turned * sine_table[:, None, :]

def route_slots(routes, rank_table, experts, capacity):
    flat_routes = routes.reshape(-1)
    flat_ranks = rank_table.reshape(-1)
    ordered = flat_routes[jnp.argsort(flat_ranks)]
    onehot = (ordered[:, None] == jnp.arange(experts, dtype=jnp.int32)[None, :]).astype(jnp.int32)
    earlier = (jnp.cumsum(onehot, axis=0) - onehot).astype(jnp.int32)
    slot_sorted = lax.optimization_barrier(jnp.sum(earlier * onehot, axis=1)).astype(jnp.int32)
    slot_number = slot_sorted[flat_ranks].reshape(routes.shape)
    kept_pair = slot_number < capacity
    return (jnp.where(kept_pair, routes * capacity + slot_number, -1).astype(jnp.int32), kept_pair)

def reference(tokens, documents, expert_routes, drop_rank, norm1_gain, query_weight, key_weight, value_weight, out_weight, norm2_gain, router_weight, gate_weight, up_weight, down_weight, output_grad):
    highest = lax.Precision.HIGHEST
    cosine, sine_table = rope_tables(doc_position(documents), HD)
    slot_index, kept_pair = jax.vmap(lambda route_blk, rank_blk: route_slots(route_blk, rank_blk, E, CAP))(expert_routes.reshape(-1, TOK_DEV, TOPK), drop_rank.reshape(-1, TOK_DEV, TOPK))
    owner_token = jnp.repeat(jnp.arange(TOK_DEV, dtype=jnp.int32), TOPK)

    def slot_owner(index_blk, kept_blk):
        target = jnp.where(kept_blk, index_blk, E * CAP).reshape(-1).astype(jnp.int32)
        return jnp.full((E * CAP,), -1, jnp.int32).at[target].set(owner_token, mode='drop')
    slot_token = jax.vmap(slot_owner)(slot_index, kept_pair)
    route_hot = expert_routes[:, :, None] == jnp.arange(E, dtype=jnp.int32)[None, None, :]
    key_docs = jnp.concatenate([jnp.full((DOC_MAX,), -1, jnp.int32), documents])
    block_rows = jnp.arange(QBLOCK, dtype=jnp.int32)[:, None]
    block_cols = jnp.arange(DOC_MAX + QBLOCK, dtype=jnp.int32)[None, :]

    def attention(query, key, value):
        key_pad = jnp.concatenate([jnp.zeros((DOC_MAX, HK, HD), jnp.float32), key], axis=0)
        value_pad = jnp.concatenate([jnp.zeros((DOC_MAX, HK, HD), jnp.float32), value], axis=0)

        def attend(block_index):
            start_row = block_index * QBLOCK
            query_part = lax.dynamic_slice_in_dim(query, start_row, QBLOCK).reshape(QBLOCK, HK, HQ // HK, HD)
            key_part = lax.dynamic_slice_in_dim(key_pad, start_row, DOC_MAX + QBLOCK)
            value_part = lax.dynamic_slice_in_dim(value_pad, start_row, DOC_MAX + QBLOCK)
            query_docs = lax.dynamic_slice_in_dim(documents, start_row, QBLOCK)
            near_docs = lax.dynamic_slice_in_dim(key_docs, start_row, DOC_MAX + QBLOCK)
            allowed = (near_docs[None, :] == query_docs[:, None]) & (block_cols <= block_rows + DOC_MAX)
            scores = low_back(attend_scale * jnp.einsum('rgjd,cgd->gjrc', query_part, key_part, precision=highest))
            scores = jnp.where(allowed, scores, masked_score)
            row_max = lax.optimization_barrier(jnp.max(scores, axis=-1, keepdims=True))
            exponent = jnp.exp(scores - row_max)
            softmaxed = exponent / lax.optimization_barrier(jnp.sum(exponent, axis=-1, keepdims=True))
            blended = jnp.einsum('gjrc,cgd->rgjd', low(softmaxed), value_part, precision=highest)
            return blended.reshape(QBLOCK, HQ * HD)
        pieces = lax.map(jax.checkpoint(attend), jnp.arange(TOKENS // QBLOCK, dtype=jnp.int32))
        return pieces.reshape(TOKENS, HQ * HD)

    def forward(stream, first_gain, query_mat, key_mat, value_mat, out_mat, second_gain, router_mat, gate_mats, up_mats, down_mats):
        normed_one = low(rms_norm(stream, first_gain))
        query_lin = low_back(jnp.dot(normed_one, query_mat, precision=highest)).reshape(TOKENS, HQ, HD)
        key_lin = low_back(jnp.dot(normed_one, key_mat, precision=highest)).reshape(TOKENS, HK, HD)
        query = low_back(low(rotate(query_lin, cosine, sine_table)))
        key = low_back(low(rotate(key_lin, cosine, sine_table)))
        value = low_back(low(jnp.dot(normed_one, value_mat, precision=highest))).reshape(TOKENS, HK, HD)
        attended = low_back(low(attention(query, key, value)))
        branch = low_back(jnp.dot(attended, out_mat, precision=highest))
        hidden_one = stream + branch_scale * branch
        normed_two = low(rms_norm(hidden_one, second_gain))
        logits = low_back(jnp.dot(normed_two, router_mat, precision=highest))
        chosen = lax.optimization_barrier(jnp.sum(jnp.where(route_hot, logits[:, None, :], 0.0), axis=-1))
        chosen_max = lax.optimization_barrier(jnp.max(chosen, axis=-1, keepdims=True))
        gate_exp = jnp.exp(chosen - chosen_max)
        gates = low(gate_exp / lax.optimization_barrier(jnp.sum(gate_exp, axis=-1, keepdims=True)))

        def expert_block(block_item):
            rows_in, block_gates, slot_table, index_blk = block_item
            present = slot_table >= 0
            picked = jnp.where(present[:, None], rows_in[jnp.clip(slot_table, 0, TOK_DEV - 1)], 0.0)
            picked = low_back(picked).reshape(E, CAP, D)
            gate_lin = low_back(jnp.einsum('ecd,edf->ecf', picked, gate_mats, precision=highest))
            up_lin = low_back(jnp.einsum('ecd,edf->ecf', picked, up_mats, precision=highest))
            inner = low(gate_lin * jax.nn.sigmoid(gate_lin) * up_lin)
            result = low_back(low(jnp.einsum('ecf,efd->ecd', inner, down_mats, precision=highest))).reshape(E * CAP, D)
            taken = result[jnp.clip(index_blk, 0, E * CAP - 1)]
            weighting = jnp.where(index_blk >= 0, block_gates, 0.0)
            return lax.optimization_barrier(jnp.sum(taken * weighting[:, :, None], axis=1))
        mixture = lax.map(jax.checkpoint(expert_block), (normed_two.reshape(-1, TOK_DEV, D), gates.reshape(-1, TOK_DEV, TOPK), slot_token, slot_index))
        mixture = low_back(mixture.reshape(TOKENS, D))
        return hidden_one + branch_scale * mixture
    primals = (tokens.astype(jnp.float32), norm1_gain.astype(jnp.float32), query_weight.astype(jnp.float32), key_weight.astype(jnp.float32), value_weight.astype(jnp.float32), out_weight.astype(jnp.float32), norm2_gain.astype(jnp.float32), router_weight.astype(jnp.float32), gate_weight.astype(jnp.float32), up_weight.astype(jnp.float32), down_weight.astype(jnp.float32))
    output, pullback = jax.vjp(forward, *primals)
    gradients = pullback(output_grad.astype(jnp.float32))
    return (output.astype(jnp.bfloat16), gradients[0].astype(jnp.bfloat16), gradients[1], gradients[2], gradients[3], gradients[4], gradients[5], gradients[6], gradients[7], gradients[8], gradients[9], gradients[10])
```

```python
import functools

import jax
import jax.numpy as jnp
from jax import lax
from jax.sharding import PartitionSpec as P
from jax.experimental import pallas as pl
from jax.experimental.pallas import tpu as pltpu

HD = 64
DOC_CAP = 2048


attend_scale = 0.015625
branch_scale = 0.22
norm_eps = 1e-06
rope_base = 10000.0
masked_score = -1e30


def from_behind(value, axis, steps):
    count = lax.axis_size(axis)
    initial, last = (max(0, -steps), min(count, count - steps))
    return lax.ppermute(value, axis, [(source, source + steps) for source in range(initial, last)])


def doc_position(documents):
    length = documents.shape[0]
    place = jnp.arange(length, dtype=jnp.int32)
    fresh = jnp.concatenate([jnp.ones((1,), dtype=bool), documents[1:] != documents[:-1]])
    opening = lax.cummax(jnp.where(fresh, place, 0), axis=0)
    return place - opening


def rope_tables(position, head_size):
    half_size = head_size // 2
    spacing = jnp.arange(half_size, dtype=jnp.float32)
    inverse = rope_base ** (-2.0 * spacing / head_size)
    angle = position.astype(jnp.float32)[:, None] * inverse[None, :]
    return (jnp.tile(jnp.cos(angle), (1, 2)), jnp.tile(jnp.sin(angle), (1, 2)))


def rotate(values, cosine, sine_table):
    half_size = values.shape[-1] // 2
    turned = jnp.concatenate([-values[..., half_size:], values[..., :half_size]], axis=-1)
    return values * cosine[:, None, :] + turned * sine_table[:, None, :]


def route_slots(routes, rank_table, experts, capacity):
    flat_routes = routes.reshape(-1)
    flat_ranks = rank_table.reshape(-1)
    ordered = flat_routes[jnp.argsort(flat_ranks)]
    onehot = (ordered[:, None] == jnp.arange(experts, dtype=jnp.int32)[None, :]).astype(jnp.int32)
    earlier = jnp.cumsum(onehot, axis=0) - onehot
    slot_sorted = jnp.sum(earlier * onehot, axis=1)
    slot_number = slot_sorted[flat_ranks].reshape(routes.shape)
    kept_pair = slot_number < capacity
    return (jnp.where(kept_pair, routes * capacity + slot_number, -1), kept_pair)


def to_owner(values):
    return lax.all_to_all(values, "fsdp", split_axis=0, concat_axis=1, tiled=True)


def from_owner(values):
    return lax.all_to_all(values, "fsdp", split_axis=1, concat_axis=0, tiled=True)


def expert_forward(slot_rows, gate_mats, up_mats, down_mats):
    gate_lin = jnp.einsum("nrd,ndf->nrf", slot_rows, gate_mats, preferred_element_type=jnp.float32)
    up_lin = jnp.einsum("nrd,ndf->nrf", slot_rows, up_mats, preferred_element_type=jnp.float32)
    inner = (gate_lin * jax.nn.sigmoid(gate_lin) * up_lin).astype(jnp.bfloat16)
    result = jnp.einsum(
        "nrf,nfd->nrd", inner, down_mats, preferred_element_type=jnp.float32
    ).astype(jnp.bfloat16)
    return (gate_lin, up_lin, result)


def expert_backward(slot_rows, gate_lin, up_lin, result_grad, gate_mats, up_mats, down_mats):
    sigma = jax.nn.sigmoid(gate_lin)
    swished = gate_lin * sigma
    inner = (swished * up_lin).astype(jnp.bfloat16)
    inner_grad = jnp.einsum(
        "nrd,nfd->nrf", result_grad, down_mats, preferred_element_type=jnp.float32
    )
    gate_grad = (inner_grad * up_lin * sigma * (1.0 + gate_lin * (1.0 - sigma))).astype(
        jnp.bfloat16
    )
    up_grad = (inner_grad * swished).astype(jnp.bfloat16)
    rows_grad = jnp.einsum("nrf,ndf->nrd", gate_grad, gate_mats, preferred_element_type=jnp.float32)
    rows_grad = (
        rows_grad + jnp.einsum("nrf,ndf->nrd", up_grad, up_mats, preferred_element_type=jnp.float32)
    ).astype(jnp.bfloat16)
    gate_part = jnp.einsum("nrd,nrf->ndf", slot_rows, gate_grad, preferred_element_type=jnp.float32)
    up_part = jnp.einsum("nrd,nrf->ndf", slot_rows, up_grad, preferred_element_type=jnp.float32)
    down_part = jnp.einsum("nrf,nrd->nfd", inner, result_grad, preferred_element_type=jnp.float32)
    return (rows_grad, gate_part, up_part, down_part)


def local(
    tokens,
    documents,
    expert_routes,
    drop_rank,
    norm1_gain,
    query_weight,
    key_weight,
    value_weight,
    out_weight,
    norm2_gain,
    router_weight,
    gate_weight,
    up_weight,
    down_weight,
    output_grad,
):
    rows_dev, model_width = tokens.shape
    heads_query = query_weight.shape[1] // HD
    heads_kv = key_weight.shape[1] // HD
    repeat = heads_query // heads_kv
    experts = router_weight.shape[1]
    top_count = expert_routes.shape[1]
    seq_parts = lax.axis_size("sp")
    span_rows = seq_parts * rows_dev
    query_block = min(512, span_rows)
    block_count = span_rows // query_block
    doc_most = min(DOC_CAP, span_rows)
    window = doc_most + query_block
    capacity = (9 * rows_dev * top_count + 8 * experts - 1) // (8 * experts)
    slot_total = experts * capacity
    block_start = lax.axis_index("fsdp") * span_rows
    row_start = block_start + lax.axis_index("sp") * rows_dev
    position = lax.dynamic_slice_in_dim(doc_position(documents), row_start, rows_dev)
    cosine, sine_table = rope_tables(position, HD)
    gain_first, query_mat, key_mat, value_mat, out_mat, gain_second, router_mat = (
        lax.all_gather(norm1_gain, "fsdp", axis=0, tiled=True),
        lax.all_gather(query_weight, "fsdp", axis=0, tiled=True),
        lax.all_gather(key_weight, "fsdp", axis=0, tiled=True),
        lax.all_gather(value_weight, "fsdp", axis=0, tiled=True),
        lax.all_gather(out_weight, "fsdp", axis=0, tiled=True),
        lax.all_gather(norm2_gain, "fsdp", axis=0, tiled=True),
        lax.all_gather(router_weight, "fsdp", axis=0, tiled=True),
    )
    stream = tokens.astype(jnp.float32)
    inverse_one = lax.rsqrt(jnp.mean(stream * stream, axis=-1, keepdims=True) + norm_eps)
    gain_one = gain_first.astype(jnp.float32)
    normed_one = (stream * inverse_one * gain_one).astype(jnp.bfloat16)
    query_lin = jnp.dot(normed_one, query_mat, preferred_element_type=jnp.float32).reshape(
        rows_dev, heads_query, HD
    )
    key_lin = jnp.dot(normed_one, key_mat, preferred_element_type=jnp.float32).reshape(
        rows_dev, heads_kv, HD
    )
    value_low = (
        jnp.dot(normed_one, value_mat, preferred_element_type=jnp.float32)
        .astype(jnp.bfloat16)
        .reshape(rows_dev, heads_kv, HD)
    )
    query_low = (
        rotate(query_lin, cosine, sine_table)
        .astype(jnp.bfloat16)
        .reshape(rows_dev, heads_kv, repeat * HD)
    )
    key_low = rotate(key_lin, cosine, sine_table).astype(jnp.bfloat16)
    packed = jnp.concatenate([query_low, key_low, value_low], axis=-1)
    by_heads = lax.all_to_all(packed, "sp", split_axis=1, concat_axis=0, tiled=True)
    groups = by_heads.shape[1]
    query_heads = by_heads[:, :, : repeat * HD]
    pair_heads = by_heads[:, :, repeat * HD :]
    halo_rows = from_behind(pair_heads[span_rows - doc_most :], "fsdp", 1)
    near_pairs = jnp.concatenate([halo_rows, pair_heads], axis=0)
    query_docs = lax.dynamic_slice_in_dim(documents, block_start, span_rows)
    near_docs = lax.dynamic_slice_in_dim(
        jnp.concatenate([jnp.full((doc_most,), -1, jnp.int32), documents]),
        block_start,
        doc_most + span_rows,
    )
    causal = jnp.arange(window)[None, :] <= jnp.arange(query_block)[:, None] + doc_most

    def block_scores(block_index):
        first_row = block_index * query_block
        query_part = lax.dynamic_slice_in_dim(query_heads, first_row, query_block).reshape(
            query_block, groups, repeat, HD
        )
        pair_part = lax.dynamic_slice_in_dim(near_pairs, first_row, window)
        key_part = pair_part[:, :, :HD]
        value_part = pair_part[:, :, HD:]
        own_docs = lax.dynamic_slice_in_dim(query_docs, first_row, query_block)
        seen_docs = lax.dynamic_slice_in_dim(near_docs, first_row, window)
        allowed = (seen_docs[None, :] == own_docs[:, None]) & causal
        scores = attend_scale * jnp.einsum(
            "rgjd,cgd->gjrc", query_part, key_part, preferred_element_type=jnp.float32
        )
        return (query_part, key_part, value_part, jnp.where(allowed, scores, masked_score))

    def attend_block(block_index):
        query_part, key_part, value_part, scores = block_scores(block_index)
        row_max = jnp.max(scores, axis=-1, keepdims=True)
        exponent = jnp.exp(scores - row_max)
        row_total = jnp.sum(exponent, axis=-1, keepdims=True)
        softmaxed = (exponent / row_total).astype(jnp.bfloat16)
        blended = jnp.einsum(
            "gjrc,cgd->rgjd", softmaxed, value_part, preferred_element_type=jnp.float32
        )
        return (
            blended.astype(jnp.bfloat16).reshape(query_block, groups, repeat * HD),
            (row_max + jnp.log(row_total))[..., 0],
        )

    blended_all, log_totals = lax.map(attend_block, jnp.arange(block_count, dtype=jnp.int32))
    attended = lax.all_to_all(
        blended_all.reshape(span_rows, groups, repeat * HD),
        "sp",
        split_axis=0,
        concat_axis=1,
        tiled=True,
    ).reshape(rows_dev, heads_query * HD)
    branch = jnp.dot(attended, out_mat, preferred_element_type=jnp.float32)
    hidden_one = stream + branch_scale * branch
    inverse_two = lax.rsqrt(jnp.mean(hidden_one * hidden_one, axis=-1, keepdims=True) + norm_eps)
    gain_two = gain_second.astype(jnp.float32)
    normed_two = (hidden_one * inverse_two * gain_two).astype(jnp.bfloat16)
    logits = jnp.dot(normed_two, router_mat, preferred_element_type=jnp.float32)
    route_hot = expert_routes[:, :, None] == jnp.arange(experts, dtype=jnp.int32)[None, None, :]
    chosen = jnp.sum(jnp.where(route_hot, logits[:, None, :], 0.0), axis=-1)
    chosen_max = jnp.max(chosen, axis=-1, keepdims=True)
    gate_exp = jnp.exp(chosen - chosen_max)
    gates = gate_exp / jnp.sum(gate_exp, axis=-1, keepdims=True)
    gate_low = gates.astype(jnp.bfloat16)
    slot_index, kept_pair = route_slots(expert_routes, drop_rank, experts, capacity)
    columns = jnp.arange(slot_total, dtype=jnp.int32)[None, :]
    dispatch = jnp.zeros((rows_dev, slot_total), dtype=bool)
    combine = jnp.zeros((rows_dev, slot_total), dtype=jnp.bfloat16)
    for route_slot in range(top_count):
        landing = slot_index[:, route_slot : route_slot + 1] == columns
        dispatch = dispatch | landing
        combine = combine + jnp.where(
            landing, gate_low[:, route_slot : route_slot + 1], jnp.zeros((), jnp.bfloat16)
        )
    dispatch_low = dispatch.astype(jnp.bfloat16)
    expert_in = (
        jnp.einsum("tc,td->cd", dispatch_low, normed_two, preferred_element_type=jnp.float32)
        .astype(jnp.bfloat16)
        .reshape(experts, capacity, model_width)
    )
    owned_in = to_owner(expert_in)
    gate_lin, up_lin, owned_out = expert_forward(owned_in, gate_weight, up_weight, down_weight)
    expert_out = from_owner(owned_out)
    mixture = jnp.dot(
        combine, expert_out.reshape(slot_total, model_width), preferred_element_type=jnp.float32
    )
    output = (hidden_one + branch_scale * mixture).astype(jnp.bfloat16)
    cotangent = output_grad.astype(jnp.float32)
    mixture_grad = (branch_scale * cotangent).astype(jnp.bfloat16)
    out_grad = (
        jnp.einsum("tc,td->cd", combine, mixture_grad, preferred_element_type=jnp.float32)
        .astype(jnp.bfloat16)
        .reshape(experts, capacity, model_width)
    )
    taken = jnp.take(
        expert_out.reshape(slot_total, model_width), jnp.clip(slot_index, 0, slot_total - 1), axis=0
    )
    gate_grad = jnp.where(
        kept_pair,
        jnp.einsum("tkd,td->tk", taken, mixture_grad, preferred_element_type=jnp.float32),
        0.0,
    )
    chosen_grad = gates * (gate_grad - jnp.sum(gates * gate_grad, axis=-1, keepdims=True))
    logit_grad = jnp.sum(jnp.where(route_hot, chosen_grad[:, :, None], 0.0), axis=1).astype(
        jnp.bfloat16
    )
    router_grad = jnp.einsum(
        "td,te->de", normed_two, logit_grad, preferred_element_type=jnp.float32
    )
    normed_two_grad = jnp.einsum(
        "te,de->td", logit_grad, router_mat, preferred_element_type=jnp.float32
    )
    owned_grad = to_owner(out_grad)
    owned_in_grad, expert_gate_grad, expert_up_grad, expert_down_grad = expert_backward(
        owned_in, gate_lin, up_lin, owned_grad, gate_weight, up_weight, down_weight
    )
    expert_in_grad = from_owner(owned_in_grad)
    normed_two_grad = normed_two_grad + jnp.dot(
        dispatch_low,
        expert_in_grad.reshape(slot_total, model_width),
        preferred_element_type=jnp.float32,
    )
    scaled_two = normed_two_grad * gain_two
    hidden_grad = (
        cotangent
        + inverse_two * scaled_two
        - hidden_one * inverse_two**3 * jnp.mean(hidden_one * scaled_two, axis=-1, keepdims=True)
    )
    norm_two_grad = jnp.sum(normed_two_grad * hidden_one * inverse_two, axis=0)
    branch_grad = (branch_scale * hidden_grad).astype(jnp.bfloat16)
    out_mat_grad = jnp.einsum(
        "tk,td->kd", attended, branch_grad, preferred_element_type=jnp.float32
    )
    attended_grad = jnp.einsum(
        "td,kd->tk", branch_grad, out_mat, preferred_element_type=jnp.float32
    ).astype(jnp.bfloat16)
    grad_heads = lax.all_to_all(
        attended_grad.reshape(rows_dev, heads_kv, repeat * HD),
        "sp",
        split_axis=1,
        concat_axis=0,
        tiled=True,
    )

    def attend_back(accumulated, block_item):
        block_index, log_total = block_item
        query_part, key_part, value_part, scores = block_scores(block_index)
        first_row = block_index * query_block
        softmaxed = jnp.exp(scores - log_total[..., None])
        incoming = lax.dynamic_slice_in_dim(grad_heads, first_row, query_block).reshape(
            query_block, groups, repeat, HD
        )
        softmax_grad = jnp.einsum(
            "rgjd,cgd->gjrc", incoming, value_part, preferred_element_type=jnp.float32
        )
        centred = jnp.sum(softmaxed * softmax_grad, axis=-1, keepdims=True)
        score_grad = (softmaxed * (softmax_grad - centred)).astype(jnp.bfloat16)
        query_grad = attend_scale * jnp.einsum(
            "gjrc,cgd->rgjd", score_grad, key_part, preferred_element_type=jnp.float32
        )
        key_grad = attend_scale * jnp.einsum(
            "gjrc,rgjd->cgd", score_grad, query_part, preferred_element_type=jnp.float32
        )
        value_grad = jnp.einsum(
            "gjrc,rgjd->cgd",
            softmaxed.astype(jnp.bfloat16),
            incoming,
            preferred_element_type=jnp.float32,
        )
        current = lax.dynamic_slice_in_dim(accumulated, first_row, window)
        updated = lax.dynamic_update_slice_in_dim(
            accumulated, current + jnp.concatenate([key_grad, value_grad], axis=-1), first_row, 0
        )
        return (updated, query_grad.reshape(query_block, groups, repeat * HD))

    pair_grad, query_grads = lax.scan(
        attend_back,
        jnp.zeros((doc_most + span_rows, groups, 2 * HD), jnp.float32),
        (jnp.arange(block_count, dtype=jnp.int32), log_totals),
    )
    returned = from_behind(pair_grad[:doc_most].astype(jnp.bfloat16), "fsdp", -1).astype(
        jnp.float32
    )
    own_grad = pair_grad[doc_most:]
    own_grad = jnp.concatenate(
        [own_grad[: span_rows - doc_most], own_grad[span_rows - doc_most :] + returned], axis=0
    )
    packed_grad = jnp.concatenate(
        [
            query_grads.reshape(span_rows, groups, repeat * HD).astype(jnp.bfloat16),
            own_grad.astype(jnp.bfloat16),
        ],
        axis=-1,
    )
    by_tokens = lax.all_to_all(packed_grad, "sp", split_axis=0, concat_axis=1, tiled=True)
    query_rot_grad = (
        by_tokens[:, :, : repeat * HD].astype(jnp.float32).reshape(rows_dev, heads_query, HD)
    )
    key_rot_grad = by_tokens[:, :, repeat * HD : (repeat + 1) * HD].astype(jnp.float32)
    value_grad_low = by_tokens[:, :, (repeat + 1) * HD :].reshape(rows_dev, heads_kv * HD)
    query_lin_grad = (
        rotate(query_rot_grad, cosine, -sine_table)
        .astype(jnp.bfloat16)
        .reshape(rows_dev, heads_query * HD)
    )
    key_lin_grad = (
        rotate(key_rot_grad, cosine, -sine_table)
        .astype(jnp.bfloat16)
        .reshape(rows_dev, heads_kv * HD)
    )
    query_mat_grad = jnp.einsum(
        "td,tk->dk", normed_one, query_lin_grad, preferred_element_type=jnp.float32
    )
    key_mat_grad = jnp.einsum(
        "td,tk->dk", normed_one, key_lin_grad, preferred_element_type=jnp.float32
    )
    value_mat_grad = jnp.einsum(
        "td,tk->dk", normed_one, value_grad_low, preferred_element_type=jnp.float32
    )
    normed_one_grad = jnp.einsum(
        "tk,dk->td", query_lin_grad, query_mat, preferred_element_type=jnp.float32
    )
    normed_one_grad = normed_one_grad + jnp.einsum(
        "tk,dk->td", key_lin_grad, key_mat, preferred_element_type=jnp.float32
    )
    normed_one_grad = normed_one_grad + jnp.einsum(
        "tk,dk->td", value_grad_low, value_mat, preferred_element_type=jnp.float32
    )
    scaled_one = normed_one_grad * gain_one
    input_grad = (
        hidden_grad
        + inverse_one * scaled_one
        - stream * inverse_one**3 * jnp.mean(stream * scaled_one, axis=-1, keepdims=True)
    ).astype(jnp.bfloat16)
    norm_one_grad = jnp.sum(normed_one_grad * stream * inverse_one, axis=0)
    shard_norm_one, shard_query, shard_key, shard_value, shard_out, shard_norm_two, shard_router = (
        lax.psum_scatter(
            norm_one_grad.astype(jnp.bfloat16), "fsdp", scatter_dimension=0, tiled=True
        ).astype(jnp.float32),
        lax.psum_scatter(
            query_mat_grad.astype(jnp.bfloat16), "fsdp", scatter_dimension=0, tiled=True
        ).astype(jnp.float32),
        lax.psum_scatter(
            key_mat_grad.astype(jnp.bfloat16), "fsdp", scatter_dimension=0, tiled=True
        ).astype(jnp.float32),
        lax.psum_scatter(
            value_mat_grad.astype(jnp.bfloat16), "fsdp", scatter_dimension=0, tiled=True
        ).astype(jnp.float32),
        lax.psum_scatter(
            out_mat_grad.astype(jnp.bfloat16), "fsdp", scatter_dimension=0, tiled=True
        ).astype(jnp.float32),
        lax.psum_scatter(
            norm_two_grad.astype(jnp.bfloat16), "fsdp", scatter_dimension=0, tiled=True
        ).astype(jnp.float32),
        lax.psum_scatter(
            router_grad.astype(jnp.bfloat16), "fsdp", scatter_dimension=0, tiled=True
        ).astype(jnp.float32),
    )
    (
        summed_norm_one,
        summed_query,
        summed_key,
        summed_value,
        summed_out,
        summed_norm_two,
        summed_router,
        summed_gate,
        summed_up,
        summed_down,
    ) = (
        lax.psum(shard_norm_one.astype(jnp.bfloat16), "sp").astype(jnp.float32),
        lax.psum(shard_query.astype(jnp.bfloat16), "sp").astype(jnp.float32),
        lax.psum(shard_key.astype(jnp.bfloat16), "sp").astype(jnp.float32),
        lax.psum(shard_value.astype(jnp.bfloat16), "sp").astype(jnp.float32),
        lax.psum(shard_out.astype(jnp.bfloat16), "sp").astype(jnp.float32),
        lax.psum(shard_norm_two.astype(jnp.bfloat16), "sp").astype(jnp.float32),
        lax.psum(shard_router.astype(jnp.bfloat16), "sp").astype(jnp.float32),
        lax.psum(expert_gate_grad.astype(jnp.bfloat16), "sp").astype(jnp.float32),
        lax.psum(expert_up_grad.astype(jnp.bfloat16), "sp").astype(jnp.float32),
        lax.psum(expert_down_grad.astype(jnp.bfloat16), "sp").astype(jnp.float32),
    )
    return (
        output,
        input_grad,
        summed_norm_one,
        summed_query,
        summed_key,
        summed_value,
        summed_out,
        summed_norm_two,
        summed_router,
        summed_gate,
        summed_up,
        summed_down,
    )


BF = jnp.bfloat16
F32 = jnp.float32
LOG2E = 1.4426950408889634
QB = 512
KB = 512
HALO = 2048
VMEM_MOST = 60 * 1024 * 1024


def in_vmem(count):
    return [pl.BlockSpec(memory_space=pltpu.VMEM)] * count


def in_hbm(count):
    return [pl.BlockSpec(memory_space=pl.ANY)] * count


def in_smem():
    return pl.BlockSpec(memory_space=pltpu.SMEM)


def shaped(shape, kind):
    return jax.ShapeDtypeStruct(shape, kind)


def params():
    return pltpu.CompilerParams(vmem_limit_bytes=VMEM_MOST)


def cost(flops, moved, transcendentals=0):
    return pl.CostEstimate(
        flops=int(flops), bytes_accessed=int(moved), transcendentals=int(transcendentals)
    )


def nn(left, right):
    return lax.dot_general(left, right, (((1,), (0,)), ((), ())), preferred_element_type=F32)


def nt(left, right):
    return lax.dot_general(left, right, (((1,), (1,)), ((), ())), preferred_element_type=F32)


def tn(left, right):
    return lax.dot_general(left, right, (((0,), (0,)), ((), ())), preferred_element_type=F32)


def flip(value, bit):
    return lax.ppermute(value, "fsdp", [(place, place ^ bit) for place in range(8)])


def half_rows(rows):
    return (rows // 2 + 15) // 16 * 16


def plan_of(rows):
    half = half_rows(rows)
    return (
        (0, 0, rows),
        (1, 0, rows),
        (2, 0, rows),
        (3, 0, rows),
        (4, 0, rows),
        (5, 0, rows),
        (6, 0, half),
        (6, half, rows - half),
        (7, 0, half),
        (7, half, rows - half),
    )


def spread(own):
    half = half_rows(own.shape[0])
    along_x = flip(own, 2)
    along_y = flip(own, 4)
    low = flip(along_y[:half], 2)
    high = flip(along_x[half:], 4)
    return (
        own,
        flip(own, 1),
        along_x,
        flip(along_x, 1),
        along_y,
        flip(along_y, 1),
        low,
        high,
        flip(low, 1),
        flip(high, 1),
    )


def add_low(left, right):
    return (left.astype(F32) + right.astype(F32)).astype(BF)


def collect(odd, even):
    half = half_rows(even.shape[1])
    received = flip(odd, 1)
    own = add_low(even[0], received[0])
    diagonal_low = flip(add_low(even[3, :half], received[3, :half]), 2)
    diagonal_high = flip(add_low(even[3, half:], received[3, half:]), 4)
    for_y = even[2].astype(F32) + received[2].astype(F32)
    for_x = even[1].astype(F32) + received[1].astype(F32)
    for_y = jnp.concatenate([for_y[:half] + diagonal_low.astype(F32), for_y[half:]]).astype(BF)
    for_x = jnp.concatenate([for_x[:half], for_x[half:] + diagonal_high.astype(F32)]).astype(BF)
    return (own, flip(for_x, 2), flip(for_y, 4))


def start_fetch(me, plan, sources, target, block_rows, sems):
    copies = []
    for number, (partner, first, rows) in enumerate(plan):
        start = pl.multiple_of((me ^ partner) * block_rows + first, 64)
        copies.append(
            pltpu.make_async_copy(sources[number], target.at[pl.ds(start, rows)], sems.at[number])
        )
        copies[-1].start()
    return copies


def start_fetch_heads(me, plan, sources, target, sems):
    copies = []
    for number, (partner, first, rows) in enumerate(plan):
        for offset in range(0, rows, HD):
            head = (me ^ partner) * 2 + (first + offset) // HD
            head = (head & ~3) | ((head & 1) << 1) | ((head >> 1) & 1)
            copies.append(
                pltpu.make_async_copy(
                    sources[number].at[pl.ds(offset, HD)],
                    target.at[pl.ds(pl.multiple_of(head * HD, HD), HD)],
                    sems.at[len(copies)],
                )
            )
            copies[-1].start()
    return copies


def turn(values, cosine, sine):
    lane = lax.broadcasted_iota(jnp.int32, values.shape, 1)
    other = jnp.where(
        lane % HD < HD // 2, pltpu.roll(values, 128 - HD // 2, 1), pltpu.roll(values, HD // 2, 1)
    )
    return values * cosine + other * sine


def project_kernel(plan, me_ref, tokens_ref, cos_ref, sin_ref, *refs):
    count = len(plan)
    query_ref, pair_ref, extra_ref, mats, sems = refs[count:]
    copies = start_fetch(me_ref[0], plan, refs[:count], mats, 128, sems)
    stream = tokens_ref[...].astype(F32)
    scaled = stream * lax.rsqrt(jnp.mean(stream * stream, axis=-1, keepdims=True) + norm_eps)
    for copy in copies:
        copy.wait()
    extra = mats[:, 2048:2176].astype(F32).T
    extra_ref[...] = extra[:48].astype(BF)
    normed = (scaled * extra[32:33]).astype(BF)
    cosine, sine = cos_ref[...], sin_ref[...]
    for part in range(4):
        query = nn(normed, mats[:, part * 256 : part * 256 + 256])
        for half in range(2):
            columns = slice(half * 128, half * 128 + 128)
            query_ref[part, :, columns] = turn(query[:, columns], cosine, sine).astype(BF)
        key = nn(normed, mats[:, 1024 + part * 128 : 1152 + part * 128])
        pair_ref[part, :, :128] = turn(key, cosine, sine).astype(BF)
        pair_ref[part, :, 128:] = nn(
            normed, mats[:, 1536 + part * 128 : 1664 + part * 128]
        ).astype(BF)


def project(me, tokens, cosine, sine, pieces):
    plan = plan_of(128)
    return pl.pallas_call(
        functools.partial(project_kernel, plan),
        out_shape=(
            shaped((4, 512, 256), BF),
            shaped((4, 512, 256), BF),
            shaped((48, 1024), BF),
        ),
        in_specs=[in_smem()] + in_vmem(3) + in_hbm(len(plan)),
        out_specs=tuple(in_vmem(3)),
        scratch_shapes=[pltpu.VMEM((1024, 2176), BF), pltpu.SemaphoreType.DMA((len(plan),))],
        compiler_params=params(),
        cost_estimate=cost(2 * 512 * 1024 * 2048, 9e6),
        name="project",
    )(me, tokens, cosine, sine, *pieces)


def lane_half(values, group):
    lane = lax.broadcasted_iota(jnp.int32, values.shape, 1)
    return jnp.where((lane < HD) == (group == 0), values, jnp.zeros((), values.dtype))


def allowed_pairs(block, step, start):
    key_at = block * KB + lax.broadcasted_iota(jnp.int32, (KB, QB), 0)
    query_at = HALO + step * QB + lax.broadcasted_iota(jnp.int32, (KB, QB), 1)
    return (key_at >= start) & (key_at <= query_at)


def attend_kernel(
    low_ref, query_ref, own_ref, halo_ref, start_ref, out_ref, log_ref,
    keys, values_t, most, total, blend,
):
    step = pl.program_id(0)

    @pl.when(step == 0)
    def _():
        for first in range(0, HALO, 512):
            rows = slice(first, first + 512)
            keys[first : first + 512, :] = halo_ref[rows, :128]
            keys[HALO + first : HALO + first + 512, :] = own_ref[rows, :128]
            values_t[:, first : first + 512] = halo_ref[rows, 128:].astype(F32).T.astype(BF)
            values_t[:, HALO + first : HALO + first + 512] = (
                own_ref[rows, 128:].astype(F32).T.astype(BF)
            )

    start = start_ref[0]
    picks = [
        lane_half(query_ref[:, half * 128 : half * 128 + 128], group)
        for half in range(2)
        for group in range(2)
    ]
    most[...] = jnp.full(most.shape, masked_score, F32)
    total[...] = jnp.zeros(total.shape, F32)
    blend[...] = jnp.zeros(blend.shape, F32)

    def visit(block, carry):
        first = pl.multiple_of(block * KB, KB)
        allowed = allowed_pairs(block, step, start)
        key = keys[pl.ds(first, KB), :]
        for number in range(4):
            scores = nt(key, picks[number]) * (attend_scale * LOG2E)
            scores = jnp.where(allowed, scores, masked_score)
            before = most[number : number + 1, :]
            top = jnp.maximum(before, jnp.max(scores, axis=0, keepdims=True))
            weight = jnp.exp2(scores - top)
            fade = jnp.exp2(before - top)
            most[number : number + 1, :] = top
            total[number : number + 1, :] = total[number : number + 1, :] * fade + jnp.sum(
                weight, axis=0, keepdims=True
            )
            group = number % 2
            value = values_t[group * HD : group * HD + HD, pl.ds(first, KB)]
            rows = slice(number * HD, number * HD + HD)
            blend[rows, :] = blend[rows, :] * fade + nn(value, weight.astype(BF))
        return carry

    lax.fori_loop(low_ref[step], step + HALO // KB + 1, visit, 0)
    for number in range(4):
        rows = slice(number * HD, number * HD + HD)
        blend[rows, :] = blend[rows, :] / total[number : number + 1, :]
    for half in range(2):
        out_ref[:, half * 128 : half * 128 + 128] = (
            blend[half * 128 : half * 128 + 128, :].T.astype(BF)
        )
    log_ref[0:4, :] = most[0:4, :] + jnp.log2(total[0:4, :])
    log_ref[4:8, :] = jnp.zeros((4, QB), F32)


def attend(low_block, query, own, halo, start):
    steps = query.shape[0] // QB
    spec = lambda shape, index: pl.BlockSpec(shape, index)
    return pl.pallas_call(
        attend_kernel,
        out_shape=(shaped((2048, 256), BF), shaped((8, 2048), F32)),
        grid_spec=pltpu.PrefetchScalarGridSpec(
            num_scalar_prefetch=1,
            grid=(steps,),
            in_specs=[
                spec((QB, 256), lambda i, low: (i, 0)),
                spec((2048, 256), lambda i, low: (0, 0)),
                spec((2048, 256), lambda i, low: (0, 0)),
                spec((1, 1, QB), lambda i, low: (i, 0, 0)),
            ],
            out_specs=(
                spec((QB, 256), lambda i, low: (i, 0)),
                spec((8, QB), lambda i, low: (0, i)),
            ),
            scratch_shapes=[
                pltpu.VMEM((2 * HALO, 128), BF),
                pltpu.VMEM((128, 2 * HALO), BF),
                pltpu.VMEM((8, QB), F32),
                pltpu.VMEM((8, QB), F32),
                pltpu.VMEM((256, QB), F32),
            ],
        ),
        compiler_params=params(),
        cost_estimate=cost(25e9, 6e6),
        name="attend",
    )(low_block, query, own, halo, start)


def attend_back_kernel(
    low_ref, query_ref, own_ref, halo_ref, start_ref, out_ref, grad_ref, log_ref,
    query_grad_ref, own_grad_ref, halo_grad_ref,
    keys, values, keys_t, key_grad, value_grad, blend,
):
    step = pl.program_id(0)

    @pl.when(step == 0)
    def _():
        for first in range(0, HALO, 512):
            rows = slice(first, first + 512)
            late = slice(HALO + first, HALO + first + 512)
            keys[rows, :] = halo_ref[rows, :128]
            keys[late, :] = own_ref[rows, :128]
            values[rows, :] = halo_ref[rows, 128:]
            values[late, :] = own_ref[rows, 128:]
            keys_t[:, rows] = halo_ref[rows, :128].astype(F32).T.astype(BF)
            keys_t[:, late] = own_ref[rows, :128].astype(F32).T.astype(BF)
        key_grad[...] = jnp.zeros(key_grad.shape, F32)
        value_grad[...] = jnp.zeros(value_grad.shape, F32)

    start = start_ref[0]
    picks, incoming, centres = [], [], []
    for half in range(2):
        columns = slice(half * 128, half * 128 + 128)
        product = (out_ref[:, columns].astype(F32) * grad_ref[:, columns].astype(F32)).T
        for group in range(2):
            picks.append(lane_half(query_ref[:, columns], group))
            incoming.append(lane_half(grad_ref[:, columns], group))
            centres.append(
                jnp.sum(product[group * HD : group * HD + HD, :], axis=0, keepdims=True)
            )
    blend[...] = jnp.zeros(blend.shape, F32)

    def visit(block, carry):
        first = pl.multiple_of(block * KB, KB)
        allowed = allowed_pairs(block, step, start)
        here = pl.ds(first, KB)
        key, value = keys[here, :], values[here, :]
        for number in range(4):
            scores = nt(key, picks[number]) * (attend_scale * LOG2E)
            weight = jnp.where(
                allowed, jnp.exp2(scores - log_ref[number : number + 1, :]), 0.0
            )
            weight_grad = nt(value, incoming[number])
            score_grad = (weight * (weight_grad - centres[number])).astype(BF)
            value_grad[here, :] += nn(weight.astype(BF), incoming[number])
            key_grad[here, :] += nn(score_grad, picks[number])
            group = number % 2
            rows = slice(number * HD, number * HD + HD)
            blend[rows, :] += nn(keys_t[group * HD : group * HD + HD, here], score_grad)
        return carry

    lax.fori_loop(low_ref[step], step + HALO // KB + 1, visit, 0)
    for half in range(2):
        query_grad_ref[:, half * 128 : half * 128 + 128] = (
            (blend[half * 128 : half * 128 + 128, :] * attend_scale).T.astype(BF)
        )

    @pl.when(step == pl.num_programs(0) - 1)
    def _():
        for first in range(0, HALO, 512):
            rows = slice(first, first + 512)
            late = slice(HALO + first, HALO + first + 512)
            halo_grad_ref[rows, :128] = (key_grad[rows, :] * attend_scale).astype(BF)
            halo_grad_ref[rows, 128:] = value_grad[rows, :].astype(BF)
            own_grad_ref[rows, :128] = key_grad[late, :] * attend_scale
            own_grad_ref[rows, 128:] = value_grad[late, :]


def attend_back(low_block, query, own, halo, start, out, grad, logs):
    steps = query.shape[0] // QB
    spec = lambda shape, index: pl.BlockSpec(shape, index)
    tile = spec((QB, 256), lambda i, low: (i, 0))
    whole = spec((2048, 256), lambda i, low: (0, 0))
    return pl.pallas_call(
        attend_back_kernel,
        out_shape=(
            shaped((2048, 256), BF),
            shaped((2048, 256), F32),
            shaped((2048, 256), BF),
        ),
        grid_spec=pltpu.PrefetchScalarGridSpec(
            num_scalar_prefetch=1,
            grid=(steps,),
            in_specs=[
                tile,
                whole,
                whole,
                spec((1, 1, QB), lambda i, low: (i, 0, 0)),
                tile,
                tile,
                spec((8, QB), lambda i, low: (0, i)),
            ],
            out_specs=(tile, whole, whole),
            scratch_shapes=[
                pltpu.VMEM((2 * HALO, 128), BF),
                pltpu.VMEM((2 * HALO, 128), BF),
                pltpu.VMEM((128, 2 * HALO), BF),
                pltpu.VMEM((2 * HALO, 128), F32),
                pltpu.VMEM((2 * HALO, 128), F32),
                pltpu.VMEM((256, QB), F32),
            ],
        ),
        compiler_params=params(),
        cost_estimate=cost(60e9, 10e6),
        name="attend_back",
    )(low_block, query, own, halo, start, out, grad, logs)


def after_kernel(plan, me_ref, tokens_ref, attended_ref, extra_ref, routed_ref, *refs):
    count = len(plan)
    hidden_ref, payload_ref, gates_ref, mats, sems = refs[count:]
    copies = start_fetch_heads(me_ref[0], plan, refs[:count], mats, sems)
    stream = tokens_ref[...].astype(F32)
    for copy in copies:
        copy.wait()
    branch = nn(attended_ref[0], mats[0:256, :])
    for part in range(1, 4):
        branch += nn(attended_ref[part], mats[part * 256 : part * 256 + 256, :])
    hidden = stream + branch_scale * branch
    hidden_ref[...] = hidden
    inverse = lax.rsqrt(jnp.mean(hidden * hidden, axis=-1, keepdims=True) + norm_eps)
    normed = (hidden * inverse * extra_ref[33:34, :].astype(F32)).astype(BF)
    payload_ref[0:512, :] = normed
    logits = nt(extra_ref[0:32, :], normed)
    routed = routed_ref[...] > 0.5
    top = jnp.max(jnp.where(routed, logits, masked_score), axis=0, keepdims=True)
    raised = jnp.where(routed, jnp.exp(logits - top), 0.0)
    gates = raised / jnp.sum(raised, axis=0, keepdims=True)
    gates_ref[...] = gates
    low = gates.astype(BF)
    payload_ref[512:528, 0:512] = low[0:16, :]
    payload_ref[512:528, 512:1024] = low[16:32, :]


def after_attention(me, tokens, attended, extra, routed, pieces):
    plan = plan_of(128)
    return pl.pallas_call(
        functools.partial(after_kernel, plan),
        out_shape=(shaped((512, 1024), F32), shaped((528, 1024), BF), shaped((32, 512), F32)),
        in_specs=[in_smem()] + in_vmem(4) + in_hbm(len(plan)),
        out_specs=tuple(in_vmem(3)),
        scratch_shapes=[pltpu.VMEM((1024, 1024), BF), pltpu.SemaphoreType.DMA((16,))],
        compiler_params=params(),
        cost_estimate=cost(2 * 512 * 1024 * 1024, 8e6),
        name="after_attention",
    )(me, tokens, attended, extra, routed, *pieces)


def own_rows(me, packed):
    first = me * 4
    side = jnp.where(first < 16, packed[:, :512], packed[:, 512:])
    row = lax.broadcasted_iota(jnp.int32, side.shape, 0)
    return [
        jnp.sum(jnp.where(row == first % 16 + expert, side, 0.0), axis=0, keepdims=True)
        for expert in range(4)
    ]


def stand_up(rows):
    row = lax.broadcasted_iota(jnp.int32, (128, 512), 0)
    lying = jnp.zeros((128, 512), F32)
    for number, values in enumerate(rows):
        lying = jnp.where(row == number, values, lying)
    return lying.T


def slot_hot(slot_row):
    at = lax.broadcasted_iota(jnp.int32, (144, 512), 0).astype(F32)
    return at == slot_row


def pieces_rows(parts):
    if len(parts) == 1:
        return parts[0][0:512, :], parts[0][512:528, :].astype(F32)
    rows = parts[0].shape[0]
    return (
        jnp.concatenate([parts[0][...], parts[1][0 : 512 - rows, :]], axis=0),
        parts[1][512 - rows : 528 - rows, :].astype(F32),
    )


def pick_grad_kernel(split, me_ref, *refs):
    count = 2 * split
    rows_ref, slots_ref, columns_ref = refs[count:]
    for block in range(2):
        tokens, packed = pieces_rows(refs[block * split : block * split + split])
        slots = own_rows(me_ref[0], packed)
        for expert in range(4):
            hot = jnp.where(slot_hot(slots[expert]), 1.0, 0.0).astype(BF)
            rows_ref[block, expert * 144 : expert * 144 + 144, :] = nn(hot, tokens).astype(BF)
            slots_ref[block, expert : expert + 1, :] = slots[expert]
        columns_ref[block] = stand_up(slots).astype(BF)


def pick_grads(me, pieces):
    split = len(pieces) // 2
    return pl.pallas_call(
        functools.partial(pick_grad_kernel, split),
        out_shape=(
            shaped((2, 576, 1024), BF),
            shaped((2, 4, 512), F32),
            shaped((2, 512, 128), BF),
        ),
        in_specs=[in_smem()] + in_vmem(len(pieces)),
        out_specs=tuple(in_vmem(3)),
        compiler_params=params(),
        cost_estimate=cost(2 * 2 * 576 * 512 * 1024, 5e6),
        name="pick_grads",
    )(me, *pieces)


def pick_rows_kernel(split, me_ref, slots_ref, *refs):
    count = 2 * split
    rows_ref, gate_ref, columns_ref = refs[count:]
    for block in range(2):
        tokens, packed = pieces_rows(refs[block * split : block * split + split])
        gates = own_rows(me_ref[0], packed)
        for expert in range(4):
            match = slot_hot(slots_ref[block, expert : expert + 1, :])
            hot = jnp.where(match, 1.0, 0.0).astype(BF)
            rows = slice(expert * 144, expert * 144 + 144)
            rows_ref[block, rows, :] = nn(hot, tokens).astype(BF)
            gate = jnp.sum(jnp.where(match, gates[expert], 0.0), axis=1, keepdims=True)
            gate_ref[block, rows, :] = jnp.broadcast_to(gate, (144, 128)).astype(BF)
        columns_ref[block] = stand_up(gates).astype(BF)


def pick_rows(me, slots, pieces):
    split = len(pieces) // 2
    return pl.pallas_call(
        functools.partial(pick_rows_kernel, split),
        out_shape=(
            shaped((2, 576, 1024), BF),
            shaped((2, 576, 128), BF),
            shaped((2, 512, 128), BF),
        ),
        in_specs=[in_smem()] + in_vmem(1 + len(pieces)),
        out_specs=tuple(in_vmem(3)),
        compiler_params=params(),
        cost_estimate=cost(2 * 2 * 576 * 512 * 1024, 5e6),
        name="pick_rows",
    )(me, slots, *pieces)


def expert_kernel(base, me_ref, *refs):
    rows_refs, grads_refs, gate_refs = refs[0:4], refs[4:8], refs[8:12]
    gate_w, up_w, down_w = (ref[0] for ref in refs[12:15])
    out_ref, in_grad_ref, mark_ref, gate_grad_ref, up_grad_ref, down_grad_ref = refs[15:21]
    lin_grads, inners, out_grads, inputs = refs[21:25]
    expert = me_ref[0] * 4 + base + pl.program_id(0)
    for part in range(2):
        at = slice(part * 576, part * 576 + 576)

        def both(pair):
            return jnp.concatenate(
                [pair[2 * part + side][...].reshape(288, -1) for side in range(2)], axis=0
            )

        rows, grads, gate = both(rows_refs), both(grads_refs), both(gate_refs)
        inputs[at, :] = rows
        gate_lin = nn(rows, gate_w)
        up_lin = nn(rows, up_w)
        sigma = 1.0 / (1.0 + jnp.exp(-gate_lin))
        swished = gate_lin * sigma
        inner = (swished * up_lin).astype(BF)
        inners[at, :] = inner
        result = nn(inner, down_w).astype(BF)
        out_ref[part * 4 : part * 4 + 4] = result.reshape(4, 144, 1024)
        wide = grads.astype(F32)
        gate_slot = jnp.sum(wide * result.astype(F32), axis=1, keepdims=True)
        lane = lax.broadcasted_iota(jnp.int32, (576, 128), 1)
        mark_ref[part * 4 : part * 4 + 4] = (
            jnp.where(lane == expert, gate_slot, 0.0).astype(BF).reshape(4, 144, 128)
        )
        out_grad = (wide * gate[:, 0:1].astype(F32)).astype(BF)
        out_grads[at, :] = out_grad
        inner_grad = nt(out_grad, down_w)
        gate_lin_grad = (
            inner_grad * up_lin * sigma * (1.0 + gate_lin * (1.0 - sigma))
        ).astype(BF)
        up_lin_grad = (inner_grad * swished).astype(BF)
        lin_grads[at, 0:512] = gate_lin_grad
        lin_grads[at, 512:1024] = up_lin_grad
        in_grad_ref[part * 4 : part * 4 + 4] = (
            (nt(gate_lin_grad, gate_w) + nt(up_lin_grad, up_w)).astype(BF).reshape(4, 144, 1024)
        )
    down_grad_ref[0] = tn(inners[...], out_grads[...]).astype(BF)
    gate_grad_ref[0] = tn(inputs[...], lin_grads[:, 0:512]).astype(BF)
    up_grad_ref[0] = tn(inputs[...], lin_grads[:, 512:1024]).astype(BF)


def run_experts(me, base, count, rows, grads, gates, gate_w, up_w, down_w):
    spec = pl.BlockSpec
    wide = spec((2, 144, 1024), lambda e: (0, base + e, 0))
    slim = spec((2, 144, 128), lambda e: (0, base + e, 0))
    tall_w = spec((1, 1024, 512), lambda e: (base + e, 0, 0))
    flat_w = spec((1, 512, 1024), lambda e: (base + e, 0, 0))
    return pl.pallas_call(
        functools.partial(expert_kernel, base),
        out_shape=(
            shaped((8, 144 * count, 1024), BF),
            shaped((8, 144 * count, 1024), BF),
            shaped((8, 144 * count, 128), BF),
            shaped((count, 1024, 512), BF),
            shaped((count, 1024, 512), BF),
            shaped((count, 512, 1024), BF),
        ),
        grid=(count,),
        in_specs=[in_smem()] + [wide] * 8 + [slim] * 4 + [tall_w, tall_w, flat_w],
        out_specs=(
            spec((8, 144, 1024), lambda e: (0, e, 0)),
            spec((8, 144, 1024), lambda e: (0, e, 0)),
            spec((8, 144, 128), lambda e: (0, e, 0)),
            spec((1, 1024, 512), lambda e: (e, 0, 0)),
            spec((1, 1024, 512), lambda e: (e, 0, 0)),
            spec((1, 512, 1024), lambda e: (e, 0, 0)),
        ),
        scratch_shapes=[
            pltpu.VMEM((1152, 1024), BF),
            pltpu.VMEM((1152, 512), BF),
            pltpu.VMEM((1152, 1024), BF),
            pltpu.VMEM((1152, 1024), BF),
        ],
        compiler_params=params(),
        cost_estimate=cost(count * 11e9, count * 15e6),
        name="experts",
    )(me, *rows, *grads, *gates, gate_w, up_w, down_w)


def combine_kernel(calls, weighted, *refs):
    slot_ref = refs[0]
    refs = refs[1:]
    gate_ref = None
    if weighted:
        gate_ref, refs = refs[0], refs[1:]
    value_refs, refs = refs[:calls], refs[calls:]
    mark_refs = ()
    if not weighted:
        mark_refs, refs = refs[:calls], refs[calls:]
    out_ref = refs[0]
    here = 4 // calls
    slots = slot_ref[0].astype(F32)
    lane = lax.broadcasted_iota(jnp.int32, (512, 144 * here), 1).astype(F32)
    total, marks = None, None
    for call in range(calls):
        hot = jnp.zeros((512, 144 * here), F32)
        for local_expert in range(here):
            number = call * here + local_expert
            slot = slots[:, number : number + 1]
            place = jnp.where(slot < 144.0, slot + 144.0 * local_expert, -1.0)
            put = 1.0
            if weighted:
                put = gate_ref[0][:, number : number + 1].astype(F32)
            hot = jnp.where(lane == place, put, hot)
        hot = hot.astype(BF)
        term = nn(hot, value_refs[call][0])
        total = term if total is None else total + term
        if not weighted:
            mark = nn(hot, mark_refs[call][0])
            marks = mark if marks is None else marks + mark
    out_ref[0, 0:512, :] = total.astype(BF)
    if not weighted:
        lying = marks.T[0:32, :].astype(BF)
        out_ref[0, 512:528, 0:512] = lying[0:16, :]
        out_ref[0, 512:528, 512:1024] = lying[16:32, :]


def combine(parity, slots, gates, values, marks):
    calls = len(values)
    weighted = gates is not None
    rows = 512 if weighted else 528
    column = pl.BlockSpec((1, 512, 128), lambda i: (2 * i + parity, 0, 0))
    wide = pl.BlockSpec((1, 576 // calls, 1024), lambda i: (2 * i + parity, 0, 0))
    slim = pl.BlockSpec((1, 576 // calls, 128), lambda i: (2 * i + parity, 0, 0))
    args = [slots] + ([gates] if weighted else []) + list(values) + list(marks)
    return pl.pallas_call(
        functools.partial(combine_kernel, calls, weighted),
        out_shape=shaped((4, rows, 1024), BF),
        grid=(4,),
        in_specs=[column]
        + ([column] if weighted else [])
        + [wide] * calls
        + [slim] * len(marks),
        out_specs=pl.BlockSpec((1, rows, 1024), lambda i: (i, 0, 0)),
        compiler_params=params(),
        cost_estimate=cost(4 * 2 * 512 * 768 * 1024, 10e6),
        name="combine",
    )(*args)


def back_kernel(
    plan, me_ref, sum_ref, sum_x_ref, sum_y_ref, hidden_ref, cot_ref, payload_ref, gates_ref,
    extra_ref, *refs,
):
    count = len(plan)
    hidden_grad_ref, branch_grad_ref, attended_grad_ref, small_ref, mats, sems = refs[count:]
    copies = start_fetch_heads(me_ref[0], plan, refs[:count], mats, sems)
    total = (
        sum_ref[...].astype(F32) + sum_x_ref[...].astype(F32) + sum_y_ref[...].astype(F32)
    )
    gate_grad = jnp.concatenate([total[512:528, 0:512], total[512:528, 512:1024]], axis=0)
    gates = gates_ref[...]
    logit_grad = (
        gates * (gate_grad - jnp.sum(gates * gate_grad, axis=0, keepdims=True))
    ).astype(BF)
    normed_grad = total[0:512, :] + tn(logit_grad, extra_ref[0:32, :])
    hidden = hidden_ref[...]
    inverse = lax.rsqrt(jnp.mean(hidden * hidden, axis=-1, keepdims=True) + norm_eps)
    scaled = normed_grad * extra_ref[33:34, :].astype(F32)
    spread_out = inverse * inverse * inverse * jnp.mean(hidden * scaled, axis=-1, keepdims=True)
    hidden_grad = cot_ref[...].astype(F32) + inverse * scaled - hidden * spread_out
    hidden_grad_ref[...] = hidden_grad
    small_ref[0:32, :] = nn(logit_grad, payload_ref[0:512, :])
    small_ref[32:40, :] = jnp.broadcast_to(
        jnp.sum(normed_grad * hidden * inverse, axis=0, keepdims=True), (8, 1024)
    )
    branch_grad = (branch_scale * hidden_grad).astype(BF)
    branch_grad_ref[...] = branch_grad
    for copy in copies:
        copy.wait()
    for part in range(4):
        attended_grad_ref[part] = nt(
            branch_grad, mats[part * 256 : part * 256 + 256, :]
        ).astype(BF)


def back_to_attention(me, sums, hidden, cotangent, payload, gates, extra, pieces):
    plan = plan_of(128)
    return pl.pallas_call(
        functools.partial(back_kernel, plan),
        out_shape=(
            shaped((512, 1024), F32),
            shaped((512, 1024), BF),
            shaped((4, 512, 256), BF),
            shaped((40, 1024), F32),
        ),
        in_specs=[in_smem()] + in_vmem(8) + in_hbm(len(plan)),
        out_specs=tuple(in_vmem(4)),
        scratch_shapes=[pltpu.VMEM((1024, 1024), BF), pltpu.SemaphoreType.DMA((16,))],
        compiler_params=params(),
        cost_estimate=cost(2 * 512 * 1024 * 1024, 12e6),
        name="back_to_attention",
    )(me, *sums, hidden, cotangent, payload, gates, extra, *pieces)


def deal_out(me, big, odd_ref, even_ref):
    for pair in range(4):
        for target, partner in ((even_ref, 2 * pair), (odd_ref, 2 * pair + 1)):
            start = pl.multiple_of((me ^ partner) * 128, 128)
            target[pair] = big[pl.ds(start, 128), :]


def out_grad_kernel(me_ref, attended_ref, branch_grad_ref, small_ref, odd_ref, even_ref, big):
    branch_grad = branch_grad_ref[...]
    for part in range(4):
        grad = tn(attended_ref[part], branch_grad).astype(BF)
        for half in range(2):
            for group in range(2):
                source = half * 128 + group * HD
                target = part * 256 + (2 * group + half) * HD
                big[target : target + HD, 0:1024] = grad[source : source + HD, :]
    small = jnp.concatenate([small_ref[...], jnp.zeros((88, 1024), F32)], axis=0)
    big[:, 1024:1152] = small.T.astype(BF)
    deal_out(me_ref[0], big, odd_ref, even_ref)


def out_grads_of(me, attended, branch_grad, small):
    return pl.pallas_call(
        out_grad_kernel,
        out_shape=(shaped((4, 128, 1152), BF), shaped((4, 128, 1152), BF)),
        in_specs=[in_smem()] + in_vmem(3),
        out_specs=tuple(in_vmem(2)),
        scratch_shapes=[pltpu.VMEM((1024, 1152), BF)],
        compiler_params=params(),
        cost_estimate=cost(2 * 512 * 1024 * 1024, 5e6),
        name="out_grads",
    )(me, attended, branch_grad, small)


def input_kernel(
    plan, me_ref, tokens_ref, cos_ref, sin_ref, query_grad_ref, pair_grad_ref, extra_ref,
    hidden_grad_ref, *refs,
):
    count = len(plan)
    input_grad_ref, odd_ref, even_ref, mats, big, lin, sems = refs[count:]
    me = me_ref[0]
    copies = start_fetch(me, plan, refs[:count], mats, 128, sems)
    stream = tokens_ref[...].astype(F32)
    inverse = lax.rsqrt(jnp.mean(stream * stream, axis=-1, keepdims=True) + norm_eps)
    gain = extra_ref[32:33, :].astype(F32)
    normed = (stream * inverse * gain).astype(BF)
    cosine, sine = cos_ref[...], -sin_ref[...]
    for part in range(4):
        for half in range(2):
            columns = slice(half * 128, half * 128 + 128)
            lin[:, part * 256 + half * 128 : part * 256 + half * 128 + 128] = turn(
                query_grad_ref[part, :, columns].astype(F32), cosine, sine
            ).astype(BF)
        lin[:, 1024 + part * 128 : 1152 + part * 128] = turn(
            pair_grad_ref[part, :, 0:128].astype(F32), cosine, sine
        ).astype(BF)
        lin[:, 1536 + part * 128 : 1664 + part * 128] = pair_grad_ref[part, :, 128:256]
    normed_t = normed.astype(F32).T.astype(BF)
    for first in range(0, 2048, 512):
        big[:, first : first + 512] = nn(normed_t, lin[:, first : first + 512]).astype(BF)
    for copy in copies:
        copy.wait()
    normed_grad = nt(lin[...], mats[:, 0:2048])
    row = jnp.sum(normed_grad * stream * inverse, axis=0, keepdims=True)
    big[:, 2048:2176] = jnp.broadcast_to(row, (128, 1024)).T.astype(BF)
    deal_out(me, big, odd_ref, even_ref)
    scaled = normed_grad * gain
    spread_out = inverse * inverse * inverse * jnp.mean(stream * scaled, axis=-1, keepdims=True)
    input_grad_ref[...] = (
        hidden_grad_ref[...] + inverse * scaled - stream * spread_out
    ).astype(BF)


def input_grads(me, tokens, cosine, sine, query_grad, pair_grad, extra, hidden_grad, pieces):
    plan = plan_of(128)
    return pl.pallas_call(
        functools.partial(input_kernel, plan),
        out_shape=(
            shaped((512, 1024), BF),
            shaped((4, 128, 2176), BF),
            shaped((4, 128, 2176), BF),
        ),
        in_specs=[in_smem()] + in_vmem(7) + in_hbm(len(plan)),
        out_specs=tuple(in_vmem(3)),
        scratch_shapes=[
            pltpu.VMEM((1024, 2176), BF),
            pltpu.VMEM((1024, 2176), BF),
            pltpu.VMEM((512, 2048), BF),
            pltpu.SemaphoreType.DMA((len(plan),)),
        ],
        compiler_params=params(),
        cost_estimate=cost(4 * 512 * 1024 * 2048, 15e6),
        name="input_grads",
    )(me, tokens, cosine, sine, query_grad, pair_grad, extra, hidden_grad, *pieces)


def dense_slots(routes, ranks, experts):
    mine = routes[None, :, :] == jnp.arange(experts, dtype=jnp.int32)[:, None, None]
    far = jnp.int32(1 << 20)
    rank = jnp.min(jnp.where(mine, ranks[None, :, :], far), axis=-1)
    slot = jnp.sum((rank[:, None, :] < rank[:, :, None]).astype(jnp.int32), axis=-1)
    routed = rank < far
    return (jnp.where(routed & (slot < 144), slot, 255).astype(BF), routed.astype(F32))


def swap_middle(values):
    rows, columns = values.shape
    parts = values.reshape(rows, columns // 256, 2, 2, HD)
    return parts.transpose(0, 1, 3, 2, 4).reshape(rows, columns)


def sum_copies(values):
    return lax.psum(values, "sp")


def fast_local(
    tokens, documents, expert_routes, drop_rank, norm1_gain, query_weight, key_weight,
    value_weight, out_weight, norm2_gain, router_weight, gate_weight, up_weight, down_weight,
    output_grad,
):
    fsdp = lax.axis_index("fsdp")
    seq = lax.axis_index("sp")
    me = jnp.reshape(fsdp, (1,)).astype(jnp.int32)
    small = jnp.concatenate(
        [
            router_weight,
            norm1_gain[:, None],
            norm2_gain[:, None],
            jnp.zeros((128, 94), BF),
        ],
        axis=1,
    )
    shard = jnp.concatenate([swap_middle(query_weight), key_weight, value_weight, small], axis=1)
    project_pieces = spread(shard)

    block_start = fsdp * 2048
    position_all = doc_position(documents)
    position_span = lax.dynamic_slice_in_dim(position_all, block_start, 2048)
    position = lax.dynamic_slice_in_dim(position_span, seq * 512, 512)
    cosine, sine_table = rope_tables(position, HD)
    cosine = jnp.tile(cosine, (1, 2))
    signs = jnp.where(jnp.arange(128) % HD < HD // 2, -1.0, 1.0).astype(F32)
    sine = jnp.tile(sine_table, (1, 2)) * signs[None, :]
    start = HALO + jnp.arange(2048, dtype=jnp.int32) - position_span
    start_rows = start.reshape(2048 // QB, 1, QB)
    low_block = start_rows[:, 0, 0] // KB

    query, pair, extra = project(me, tokens, cosine, sine, project_pieces)
    pair_heads = lax.all_to_all(
        pair.reshape(2048, 256), "sp", split_axis=0, concat_axis=0, tiled=True
    )
    query_heads = lax.all_to_all(
        query.reshape(2048, 256), "sp", split_axis=0, concat_axis=0, tiled=True
    )
    halo = from_behind(pair_heads, "fsdp", 1)

    slots, routed = dense_slots(expert_routes, drop_rank, 32)
    mixture_grad = (branch_scale * output_grad.astype(F32)).astype(BF)
    grad_payload = jnp.concatenate(
        [mixture_grad, jnp.concatenate([slots[:16], slots[16:]], axis=1)], axis=0
    )
    grad_pieces = spread(grad_payload)
    out_pieces = spread(out_weight)

    blended, logs = attend(low_block, query_heads, pair_heads, halo, start_rows)
    attended = lax.all_to_all(blended, "sp", split_axis=0, concat_axis=0, tiled=True).reshape(
        4, 512, 256
    )
    hidden_one, payload, gates = after_attention(
        me, tokens, attended, extra, routed, out_pieces
    )
    row_pieces = spread(payload)

    groups = ((0, 2), (2, 4), (4, 6), (6, 10))
    grad_rows, slot_rows, slot_columns = zip(
        *[pick_grads(me, grad_pieces[first:last]) for first, last in groups]
    )
    rows, slot_gates, gate_columns = zip(
        *[
            pick_rows(me, slot_rows[number], row_pieces[first:last])
            for number, (first, last) in enumerate(groups)
        ]
    )
    slot_columns = jnp.concatenate(slot_columns, axis=0)
    gate_columns = jnp.concatenate(gate_columns, axis=0)
    per_call = 2
    results = [
        run_experts(
            me, base, per_call, rows, grad_rows, slot_gates, gate_weight, up_weight, down_weight
        )
        for base in range(0, 4, per_call)
    ]
    outs, in_grads, marks, gate_grads, up_grads, down_grads = zip(*results)
    odd = combine(1, slot_columns, None, in_grads, marks)
    even = combine(0, slot_columns, None, in_grads, marks)
    sums = collect(odd, even)
    hidden_grad, branch_grad, attended_grad, small_grads = back_to_attention(
        me, sums, hidden_one, output_grad, payload, gates, extra, out_pieces
    )
    grad_heads = lax.all_to_all(
        attended_grad.reshape(2048, 256), "sp", split_axis=0, concat_axis=0, tiled=True
    )
    odd_mix = combine(1, slot_columns, gate_columns, outs, ())
    even_mix = combine(0, slot_columns, gate_columns, outs, ())
    mixture = collect(odd_mix, even_mix)
    output = (
        hidden_one
        + branch_scale
        * (mixture[0].astype(F32) + mixture[1].astype(F32) + mixture[2].astype(F32))
    ).astype(BF)
    out_sums = collect(*out_grads_of(me, attended, branch_grad, small_grads))

    query_back, own_back, halo_back = attend_back(
        low_block, query_heads, pair_heads, halo, start_rows, blended, grad_heads, logs
    )
    pair_back = (own_back + from_behind(halo_back, "fsdp", -1).astype(F32)).astype(BF)
    query_grad = lax.all_to_all(
        query_back, "sp", split_axis=0, concat_axis=0, tiled=True
    ).reshape(4, 512, 256)
    pair_grad = lax.all_to_all(
        pair_back, "sp", split_axis=0, concat_axis=0, tiled=True
    ).reshape(4, 512, 256)
    input_grad, odd_in, even_in = input_grads(
        me, tokens, cosine, sine, query_grad, pair_grad, extra, hidden_grad, project_pieces
    )
    in_sums = collect(odd_in, even_in)

    out_shard = sum(term.astype(F32) for term in out_sums).astype(BF)
    in_shard = sum(term.astype(F32) for term in in_sums).astype(BF)
    out_shard, in_shard = sum_copies((out_shard, in_shard))
    expert_sums = sum_copies((gate_grads, up_grads, down_grads))
    stacked = [jnp.concatenate(list(parts), axis=0).astype(F32) for parts in expert_sums]
    return (
        output,
        input_grad,
        in_shard[:, 2048].astype(F32),
        swap_middle(in_shard[:, 0:1024]).astype(F32),
        in_shard[:, 1024:1536].astype(F32),
        in_shard[:, 1536:2048].astype(F32),
        out_shard[:, 0:1024].astype(F32),
        out_shard[:, 1056].astype(F32),
        out_shard[:, 1024:1056].astype(F32),
        *stacked,
    )


def solution(mesh):
    placed = (
        P(("fsdp", "sp"), None),
        P(),
        P(("fsdp", "sp"), None),
        P(("fsdp", "sp"), None),
        P("fsdp"),
        P("fsdp", None),
        P("fsdp", None),
        P("fsdp", None),
        P("fsdp", None),
        P("fsdp"),
        P("fsdp", None),
        P("fsdp", None, None),
        P("fsdp", None, None),
        P("fsdp", None, None),
        P(("fsdp", "sp"), None),
    )
    fast = mesh.shape["sp"] == 4 and mesh.shape["fsdp"] == 8
    return jax.shard_map(
        fast_local if fast else local,
        mesh=mesh,
        in_specs=placed,
        out_specs=(
            P(("fsdp", "sp"), None),
            P(("fsdp", "sp"), None),
            P("fsdp"),
            P("fsdp", None),
            P("fsdp", None),
            P("fsdp", None),
            P("fsdp", None),
            P("fsdp"),
            P("fsdp", None),
            P("fsdp", None, None),
            P("fsdp", None, None),
            P("fsdp", None, None),
        ),
        check_vma=False,
    )
```

```python
import functools

import jax
import jax.numpy as jnp
from jax import lax
from jax.sharding import PartitionSpec as P
from jax.experimental import pallas as pl
from jax.experimental.pallas import tpu as pltpu

HD = 64
DOC_CAP = 2048


attend_scale = 0.015625
branch_scale = 0.22
norm_eps = 1e-06
rope_base = 10000.0
masked_score = -1e30


def from_behind(value, axis, steps):
    count = lax.axis_size(axis)
    initial, last = (max(0, -steps), min(count, count - steps))
    return lax.ppermute(value, axis, [(source, source + steps) for source in range(initial, last)])


def doc_position(documents):
    length = documents.shape[0]
    place = jnp.arange(length, dtype=jnp.int32)
    fresh = jnp.concatenate([jnp.ones((1,), dtype=bool), documents[1:] != documents[:-1]])
    opening = lax.cummax(jnp.where(fresh, place, 0), axis=0)
    return place - opening


def rope_tables(position, head_size):
    half_size = head_size // 2
    spacing = jnp.arange(half_size, dtype=jnp.float32)
    inverse = rope_base ** (-2.0 * spacing / head_size)
    angle = position.astype(jnp.float32)[:, None] * inverse[None, :]
    return (jnp.tile(jnp.cos(angle), (1, 2)), jnp.tile(jnp.sin(angle), (1, 2)))


def rotate(values, cosine, sine_table):
    half_size = values.shape[-1] // 2
    turned = jnp.concatenate([-values[..., half_size:], values[..., :half_size]], axis=-1)
    return values * cosine[:, None, :] + turned * sine_table[:, None, :]


def route_slots(routes, rank_table, experts, capacity):
    flat_routes = routes.reshape(-1)
    flat_ranks = rank_table.reshape(-1)
    ordered = flat_routes[jnp.argsort(flat_ranks)]
    onehot = (ordered[:, None] == jnp.arange(experts, dtype=jnp.int32)[None, :]).astype(jnp.int32)
    earlier = jnp.cumsum(onehot, axis=0) - onehot
    slot_sorted = jnp.sum(earlier * onehot, axis=1)
    slot_number = slot_sorted[flat_ranks].reshape(routes.shape)
    kept_pair = slot_number < capacity
    return (jnp.where(kept_pair, routes * capacity + slot_number, -1), kept_pair)


def to_owner(values):
    return lax.all_to_all(values, "fsdp", split_axis=0, concat_axis=1, tiled=True)


def from_owner(values):
    return lax.all_to_all(values, "fsdp", split_axis=1, concat_axis=0, tiled=True)


def expert_forward(slot_rows, gate_mats, up_mats, down_mats):
    gate_lin = jnp.einsum("nrd,ndf->nrf", slot_rows, gate_mats, preferred_element_type=jnp.float32)
    up_lin = jnp.einsum("nrd,ndf->nrf", slot_rows, up_mats, preferred_element_type=jnp.float32)
    inner = (gate_lin * jax.nn.sigmoid(gate_lin) * up_lin).astype(jnp.bfloat16)
    result = jnp.einsum(
        "nrf,nfd->nrd", inner, down_mats, preferred_element_type=jnp.float32
    ).astype(jnp.bfloat16)
    return (gate_lin, up_lin, result)


def expert_backward(slot_rows, gate_lin, up_lin, result_grad, gate_mats, up_mats, down_mats):
    sigma = jax.nn.sigmoid(gate_lin)
    swished = gate_lin * sigma
    inner = (swished * up_lin).astype(jnp.bfloat16)
    inner_grad = jnp.einsum(
        "nrd,nfd->nrf", result_grad, down_mats, preferred_element_type=jnp.float32
    )
    gate_grad = (inner_grad * up_lin * sigma * (1.0 + gate_lin * (1.0 - sigma))).astype(
        jnp.bfloat16
    )
    up_grad = (inner_grad * swished).astype(jnp.bfloat16)
    rows_grad = jnp.einsum("nrf,ndf->nrd", gate_grad, gate_mats, preferred_element_type=jnp.float32)
    rows_grad = (
        rows_grad + jnp.einsum("nrf,ndf->nrd", up_grad, up_mats, preferred_element_type=jnp.float32)
    ).astype(jnp.bfloat16)
    gate_part = jnp.einsum("nrd,nrf->ndf", slot_rows, gate_grad, preferred_element_type=jnp.float32)
    up_part = jnp.einsum("nrd,nrf->ndf", slot_rows, up_grad, preferred_element_type=jnp.float32)
    down_part = jnp.einsum("nrf,nrd->nfd", inner, result_grad, preferred_element_type=jnp.float32)
    return (rows_grad, gate_part, up_part, down_part)


def local(
    tokens,
    documents,
    expert_routes,
    drop_rank,
    norm1_gain,
    query_weight,
    key_weight,
    value_weight,
    out_weight,
    norm2_gain,
    router_weight,
    gate_weight,
    up_weight,
    down_weight,
    output_grad,
):
    rows_dev, model_width = tokens.shape
    heads_query = query_weight.shape[1] // HD
    heads_kv = key_weight.shape[1] // HD
    repeat = heads_query // heads_kv
    experts = router_weight.shape[1]
    top_count = expert_routes.shape[1]
    seq_parts = lax.axis_size("sp")
    span_rows = seq_parts * rows_dev
    query_block = min(512, span_rows)
    block_count = span_rows // query_block
    doc_most = min(DOC_CAP, span_rows)
    window = doc_most + query_block
    capacity = (9 * rows_dev * top_count + 8 * experts - 1) // (8 * experts)
    slot_total = experts * capacity
    block_start = lax.axis_index("fsdp") * span_rows
    row_start = block_start + lax.axis_index("sp") * rows_dev
    position = lax.dynamic_slice_in_dim(doc_position(documents), row_start, rows_dev)
    cosine, sine_table = rope_tables(position, HD)
    gain_first, query_mat, key_mat, value_mat, out_mat, gain_second, router_mat = (
        lax.all_gather(norm1_gain, "fsdp", axis=0, tiled=True),
        lax.all_gather(query_weight, "fsdp", axis=0, tiled=True),
        lax.all_gather(key_weight, "fsdp", axis=0, tiled=True),
        lax.all_gather(value_weight, "fsdp", axis=0, tiled=True),
        lax.all_gather(out_weight, "fsdp", axis=0, tiled=True),
        lax.all_gather(norm2_gain, "fsdp", axis=0, tiled=True),
        lax.all_gather(router_weight, "fsdp", axis=0, tiled=True),
    )
    stream = tokens.astype(jnp.float32)
    inverse_one = lax.rsqrt(jnp.mean(stream * stream, axis=-1, keepdims=True) + norm_eps)
    gain_one = gain_first.astype(jnp.float32)
    normed_one = (stream * inverse_one * gain_one).astype(jnp.bfloat16)
    query_lin = jnp.dot(normed_one, query_mat, preferred_element_type=jnp.float32).reshape(
        rows_dev, heads_query, HD
    )
    key_lin = jnp.dot(normed_one, key_mat, preferred_element_type=jnp.float32).reshape(
        rows_dev, heads_kv, HD
    )
    value_low = (
        jnp.dot(normed_one, value_mat, preferred_element_type=jnp.float32)
        .astype(jnp.bfloat16)
        .reshape(rows_dev, heads_kv, HD)
    )
    query_low = (
        rotate(query_lin, cosine, sine_table)
        .astype(jnp.bfloat16)
        .reshape(rows_dev, heads_kv, repeat * HD)
    )
    key_low = rotate(key_lin, cosine, sine_table).astype(jnp.bfloat16)
    packed = jnp.concatenate([query_low, key_low, value_low], axis=-1)
    by_heads = lax.all_to_all(packed, "sp", split_axis=1, concat_axis=0, tiled=True)
    groups = by_heads.shape[1]
    query_heads = by_heads[:, :, : repeat * HD]
    pair_heads = by_heads[:, :, repeat * HD :]
    halo_rows = from_behind(pair_heads[span_rows - doc_most :], "fsdp", 1)
    near_pairs = jnp.concatenate([halo_rows, pair_heads], axis=0)
    query_docs = lax.dynamic_slice_in_dim(documents, block_start, span_rows)
    near_docs = lax.dynamic_slice_in_dim(
        jnp.concatenate([jnp.full((doc_most,), -1, jnp.int32), documents]),
        block_start,
        doc_most + span_rows,
    )
    causal = jnp.arange(window)[None, :] <= jnp.arange(query_block)[:, None] + doc_most

    def block_scores(block_index):
        first_row = block_index * query_block
        query_part = lax.dynamic_slice_in_dim(query_heads, first_row, query_block).reshape(
            query_block, groups, repeat, HD
        )
        pair_part = lax.dynamic_slice_in_dim(near_pairs, first_row, window)
        key_part = pair_part[:, :, :HD]
        value_part = pair_part[:, :, HD:]
        own_docs = lax.dynamic_slice_in_dim(query_docs, first_row, query_block)
        seen_docs = lax.dynamic_slice_in_dim(near_docs, first_row, window)
        allowed = (seen_docs[None, :] == own_docs[:, None]) & causal
        scores = attend_scale * jnp.einsum(
            "rgjd,cgd->gjrc", query_part, key_part, preferred_element_type=jnp.float32
        )
        return (query_part, key_part, value_part, jnp.where(allowed, scores, masked_score))

    def attend_block(block_index):
        query_part, key_part, value_part, scores = block_scores(block_index)
        row_max = jnp.max(scores, axis=-1, keepdims=True)
        exponent = jnp.exp(scores - row_max)
        row_total = jnp.sum(exponent, axis=-1, keepdims=True)
        softmaxed = (exponent / row_total).astype(jnp.bfloat16)
        blended = jnp.einsum(
            "gjrc,cgd->rgjd", softmaxed, value_part, preferred_element_type=jnp.float32
        )
        return (
            blended.astype(jnp.bfloat16).reshape(query_block, groups, repeat * HD),
            (row_max + jnp.log(row_total))[..., 0],
        )

    blended_all, log_totals = lax.map(attend_block, jnp.arange(block_count, dtype=jnp.int32))
    attended = lax.all_to_all(
        blended_all.reshape(span_rows, groups, repeat * HD),
        "sp",
        split_axis=0,
        concat_axis=1,
        tiled=True,
    ).reshape(rows_dev, heads_query * HD)
    branch = jnp.dot(attended, out_mat, preferred_element_type=jnp.float32)
    hidden_one = stream + branch_scale * branch
    inverse_two = lax.rsqrt(jnp.mean(hidden_one * hidden_one, axis=-1, keepdims=True) + norm_eps)
    gain_two = gain_second.astype(jnp.float32)
    normed_two = (hidden_one * inverse_two * gain_two).astype(jnp.bfloat16)
    logits = jnp.dot(normed_two, router_mat, preferred_element_type=jnp.float32)
    route_hot = expert_routes[:, :, None] == jnp.arange(experts, dtype=jnp.int32)[None, None, :]
    chosen = jnp.sum(jnp.where(route_hot, logits[:, None, :], 0.0), axis=-1)
    chosen_max = jnp.max(chosen, axis=-1, keepdims=True)
    gate_exp = jnp.exp(chosen - chosen_max)
    gates = gate_exp / jnp.sum(gate_exp, axis=-1, keepdims=True)
    gate_low = gates.astype(jnp.bfloat16)
    slot_index, kept_pair = route_slots(expert_routes, drop_rank, experts, capacity)
    columns = jnp.arange(slot_total, dtype=jnp.int32)[None, :]
    dispatch = jnp.zeros((rows_dev, slot_total), dtype=bool)
    combine = jnp.zeros((rows_dev, slot_total), dtype=jnp.bfloat16)
    for route_slot in range(top_count):
        landing = slot_index[:, route_slot : route_slot + 1] == columns
        dispatch = dispatch | landing
        combine = combine + jnp.where(
            landing, gate_low[:, route_slot : route_slot + 1], jnp.zeros((), jnp.bfloat16)
        )
    dispatch_low = dispatch.astype(jnp.bfloat16)
    expert_in = (
        jnp.einsum("tc,td->cd", dispatch_low, normed_two, preferred_element_type=jnp.float32)
        .astype(jnp.bfloat16)
        .reshape(experts, capacity, model_width)
    )
    owned_in = to_owner(expert_in)
    gate_lin, up_lin, owned_out = expert_forward(owned_in, gate_weight, up_weight, down_weight)
    expert_out = from_owner(owned_out)
    mixture = jnp.dot(
        combine, expert_out.reshape(slot_total, model_width), preferred_element_type=jnp.float32
    )
    output = (hidden_one + branch_scale * mixture).astype(jnp.bfloat16)
    cotangent = output_grad.astype(jnp.float32)
    mixture_grad = (branch_scale * cotangent).astype(jnp.bfloat16)
    out_grad = (
        jnp.einsum("tc,td->cd", combine, mixture_grad, preferred_element_type=jnp.float32)
        .astype(jnp.bfloat16)
        .reshape(experts, capacity, model_width)
    )
    taken = jnp.take(
        expert_out.reshape(slot_total, model_width), jnp.clip(slot_index, 0, slot_total - 1), axis=0
    )
    gate_grad = jnp.where(
        kept_pair,
        jnp.einsum("tkd,td->tk", taken, mixture_grad, preferred_element_type=jnp.float32),
        0.0,
    )
    chosen_grad = gates * (gate_grad - jnp.sum(gates * gate_grad, axis=-1, keepdims=True))
    logit_grad = jnp.sum(jnp.where(route_hot, chosen_grad[:, :, None], 0.0), axis=1).astype(
        jnp.bfloat16
    )
    router_grad = jnp.einsum(
        "td,te->de", normed_two, logit_grad, preferred_element_type=jnp.float32
    )
    normed_two_grad = jnp.einsum(
        "te,de->td", logit_grad, router_mat, preferred_element_type=jnp.float32
    )
    owned_grad = to_owner(out_grad)
    owned_in_grad, expert_gate_grad, expert_up_grad, expert_down_grad = expert_backward(
        owned_in, gate_lin, up_lin, owned_grad, gate_weight, up_weight, down_weight
    )
    expert_in_grad = from_owner(owned_in_grad)
    normed_two_grad = normed_two_grad + jnp.dot(
        dispatch_low,
        expert_in_grad.reshape(slot_total, model_width),
        preferred_element_type=jnp.float32,
    )
    scaled_two = normed_two_grad * gain_two
    hidden_grad = (
        cotangent
        + inverse_two * scaled_two
        - hidden_one * inverse_two**3 * jnp.mean(hidden_one * scaled_two, axis=-1, keepdims=True)
    )
    norm_two_grad = jnp.sum(normed_two_grad * hidden_one * inverse_two, axis=0)
    branch_grad = (branch_scale * hidden_grad).astype(jnp.bfloat16)
    out_mat_grad = jnp.einsum(
        "tk,td->kd", attended, branch_grad, preferred_element_type=jnp.float32
    )
    attended_grad = jnp.einsum(
        "td,kd->tk", branch_grad, out_mat, preferred_element_type=jnp.float32
    ).astype(jnp.bfloat16)
    grad_heads = lax.all_to_all(
        attended_grad.reshape(rows_dev, heads_kv, repeat * HD),
        "sp",
        split_axis=1,
        concat_axis=0,
        tiled=True,
    )

    def attend_back(accumulated, block_item):
        block_index, log_total = block_item
        query_part, key_part, value_part, scores = block_scores(block_index)
        first_row = block_index * query_block
        softmaxed = jnp.exp(scores - log_total[..., None])
        incoming = lax.dynamic_slice_in_dim(grad_heads, first_row, query_block).reshape(
            query_block, groups, repeat, HD
        )
        softmax_grad = jnp.einsum(
            "rgjd,cgd->gjrc", incoming, value_part, preferred_element_type=jnp.float32
        )
        centred = jnp.sum(softmaxed * softmax_grad, axis=-1, keepdims=True)
        score_grad = (softmaxed * (softmax_grad - centred)).astype(jnp.bfloat16)
        query_grad = attend_scale * jnp.einsum(
            "gjrc,cgd->rgjd", score_grad, key_part, preferred_element_type=jnp.float32
        )
        key_grad = attend_scale * jnp.einsum(
            "gjrc,rgjd->cgd", score_grad, query_part, preferred_element_type=jnp.float32
        )
        value_grad = jnp.einsum(
            "gjrc,rgjd->cgd",
            softmaxed.astype(jnp.bfloat16),
            incoming,
            preferred_element_type=jnp.float32,
        )
        current = lax.dynamic_slice_in_dim(accumulated, first_row, window)
        updated = lax.dynamic_update_slice_in_dim(
            accumulated, current + jnp.concatenate([key_grad, value_grad], axis=-1), first_row, 0
        )
        return (updated, query_grad.reshape(query_block, groups, repeat * HD))

    pair_grad, query_grads = lax.scan(
        attend_back,
        jnp.zeros((doc_most + span_rows, groups, 2 * HD), jnp.float32),
        (jnp.arange(block_count, dtype=jnp.int32), log_totals),
    )
    returned = from_behind(pair_grad[:doc_most].astype(jnp.bfloat16), "fsdp", -1).astype(
        jnp.float32
    )
    own_grad = pair_grad[doc_most:]
    own_grad = jnp.concatenate(
        [own_grad[: span_rows - doc_most], own_grad[span_rows - doc_most :] + returned], axis=0
    )
    packed_grad = jnp.concatenate(
        [
            query_grads.reshape(span_rows, groups, repeat * HD).astype(jnp.bfloat16),
            own_grad.astype(jnp.bfloat16),
        ],
        axis=-1,
    )
    by_tokens = lax.all_to_all(packed_grad, "sp", split_axis=0, concat_axis=1, tiled=True)
    query_rot_grad = (
        by_tokens[:, :, : repeat * HD].astype(jnp.float32).reshape(rows_dev, heads_query, HD)
    )
    key_rot_grad = by_tokens[:, :, repeat * HD : (repeat + 1) * HD].astype(jnp.float32)
    value_grad_low = by_tokens[:, :, (repeat + 1) * HD :].reshape(rows_dev, heads_kv * HD)
    query_lin_grad = (
        rotate(query_rot_grad, cosine, -sine_table)
        .astype(jnp.bfloat16)
        .reshape(rows_dev, heads_query * HD)
    )
    key_lin_grad = (
        rotate(key_rot_grad, cosine, -sine_table)
        .astype(jnp.bfloat16)
        .reshape(rows_dev, heads_kv * HD)
    )
    query_mat_grad = jnp.einsum(
        "td,tk->dk", normed_one, query_lin_grad, preferred_element_type=jnp.float32
    )
    key_mat_grad = jnp.einsum(
        "td,tk->dk", normed_one, key_lin_grad, preferred_element_type=jnp.float32
    )
    value_mat_grad = jnp.einsum(
        "td,tk->dk", normed_one, value_grad_low, preferred_element_type=jnp.float32
    )
    normed_one_grad = jnp.einsum(
        "tk,dk->td", query_lin_grad, query_mat, preferred_element_type=jnp.float32
    )
    normed_one_grad = normed_one_grad + jnp.einsum(
        "tk,dk->td", key_lin_grad, key_mat, preferred_element_type=jnp.float32
    )
    normed_one_grad = normed_one_grad + jnp.einsum(
        "tk,dk->td", value_grad_low, value_mat, preferred_element_type=jnp.float32
    )
    scaled_one = normed_one_grad * gain_one
    input_grad = (
        hidden_grad
        + inverse_one * scaled_one
        - stream * inverse_one**3 * jnp.mean(stream * scaled_one, axis=-1, keepdims=True)
    ).astype(jnp.bfloat16)
    norm_one_grad = jnp.sum(normed_one_grad * stream * inverse_one, axis=0)
    shard_norm_one, shard_query, shard_key, shard_value, shard_out, shard_norm_two, shard_router = (
        lax.psum_scatter(
            norm_one_grad.astype(jnp.bfloat16), "fsdp", scatter_dimension=0, tiled=True
        ).astype(jnp.float32),
        lax.psum_scatter(
            query_mat_grad.astype(jnp.bfloat16), "fsdp", scatter_dimension=0, tiled=True
        ).astype(jnp.float32),
        lax.psum_scatter(
            key_mat_grad.astype(jnp.bfloat16), "fsdp", scatter_dimension=0, tiled=True
        ).astype(jnp.float32),
        lax.psum_scatter(
            value_mat_grad.astype(jnp.bfloat16), "fsdp", scatter_dimension=0, tiled=True
        ).astype(jnp.float32),
        lax.psum_scatter(
            out_mat_grad.astype(jnp.bfloat16), "fsdp", scatter_dimension=0, tiled=True
        ).astype(jnp.float32),
        lax.psum_scatter(
            norm_two_grad.astype(jnp.bfloat16), "fsdp", scatter_dimension=0, tiled=True
        ).astype(jnp.float32),
        lax.psum_scatter(
            router_grad.astype(jnp.bfloat16), "fsdp", scatter_dimension=0, tiled=True
        ).astype(jnp.float32),
    )
    (
        summed_norm_one,
        summed_query,
        summed_key,
        summed_value,
        summed_out,
        summed_norm_two,
        summed_router,
        summed_gate,
        summed_up,
        summed_down,
    ) = (
        lax.psum(shard_norm_one.astype(jnp.bfloat16), "sp").astype(jnp.float32),
        lax.psum(shard_query.astype(jnp.bfloat16), "sp").astype(jnp.float32),
        lax.psum(shard_key.astype(jnp.bfloat16), "sp").astype(jnp.float32),
        lax.psum(shard_value.astype(jnp.bfloat16), "sp").astype(jnp.float32),
        lax.psum(shard_out.astype(jnp.bfloat16), "sp").astype(jnp.float32),
        lax.psum(shard_norm_two.astype(jnp.bfloat16), "sp").astype(jnp.float32),
        lax.psum(shard_router.astype(jnp.bfloat16), "sp").astype(jnp.float32),
        lax.psum(expert_gate_grad.astype(jnp.bfloat16), "sp").astype(jnp.float32),
        lax.psum(expert_up_grad.astype(jnp.bfloat16), "sp").astype(jnp.float32),
        lax.psum(expert_down_grad.astype(jnp.bfloat16), "sp").astype(jnp.float32),
    )
    return (
        output,
        input_grad,
        summed_norm_one,
        summed_query,
        summed_key,
        summed_value,
        summed_out,
        summed_norm_two,
        summed_router,
        summed_gate,
        summed_up,
        summed_down,
    )


BF = jnp.bfloat16
F32 = jnp.float32
LOG2E = 1.4426950408889634
QB = 512
KB = 512
HALO = 2048
VMEM_MOST = 60 * 1024 * 1024


def in_vmem(count):
    return [pl.BlockSpec(memory_space=pltpu.VMEM)] * count


def in_hbm(count):
    return [pl.BlockSpec(memory_space=pl.ANY)] * count


def in_smem():
    return pl.BlockSpec(memory_space=pltpu.SMEM)


def shaped(shape, kind):
    return jax.ShapeDtypeStruct(shape, kind)


def params():
    return pltpu.CompilerParams(vmem_limit_bytes=VMEM_MOST)


def cost(flops, moved, transcendentals=0):
    return pl.CostEstimate(
        flops=int(flops) // 8, bytes_accessed=int(moved) // 8, transcendentals=int(transcendentals)
    )


def nn(left, right):
    return lax.dot_general(left, right, (((1,), (0,)), ((), ())), preferred_element_type=F32)


def nt(left, right):
    return lax.dot_general(left, right, (((1,), (1,)), ((), ())), preferred_element_type=F32)


def tn(left, right):
    return lax.dot_general(left, right, (((0,), (0,)), ((), ())), preferred_element_type=F32)


def flip(value, bit):
    return lax.ppermute(value, "fsdp", [(place, place ^ bit) for place in range(8)])


def half_rows(rows):
    return (rows // 2 + 15) // 16 * 16


def plan_of(rows):
    half = half_rows(rows)
    return (
        (0, 0, rows),
        (1, 0, rows),
        (2, 0, rows),
        (3, 0, rows),
        (4, 0, rows),
        (5, 0, rows),
        (6, 0, half),
        (6, half, rows - half),
        (7, 0, half),
        (7, half, rows - half),
    )


def hold(value, *others):
    return lax.optimization_barrier((value, others))[0]


def spread_near(own):
    along_x, along_y = flip(own, 2), flip(own, 4)
    return (own, flip(own, 1), along_x, flip(along_x, 1), along_y, flip(along_y, 1))


def spread_diagonal(near):
    half = half_rows(near[0].shape[0])
    return (flip(near[4][:half], 2), flip(near[2][half:], 4))


def spread_far(diagonal):
    return (*diagonal, flip(diagonal[0], 1), flip(diagonal[1], 1))


def spread(own):
    near = spread_near(own)
    return near + spread_far(spread_diagonal(near))


def add_low(left, right):
    return (left.astype(F32) + right.astype(F32)).astype(BF)


def collect(odd, even, tick=None):
    half = half_rows(even.shape[1])
    received = flip(odd, 1)
    diagonal_low = flip(add_low(even[3, :half], received[3, :half]), 2)
    diagonal_high = flip(add_low(even[3, half:], received[3, half:]), 4)
    if tick is not None:
        diagonal_low, diagonal_high = tick((diagonal_low, diagonal_high))
    own = add_low(even[0], received[0])
    for_y = even[2].astype(F32) + received[2].astype(F32)
    for_x = even[1].astype(F32) + received[1].astype(F32)
    for_y = jnp.concatenate([for_y[:half] + diagonal_low.astype(F32), for_y[half:]]).astype(BF)
    for_x = jnp.concatenate([for_x[:half], for_x[half:] + diagonal_high.astype(F32)]).astype(BF)
    return (own, flip(for_x, 2), flip(for_y, 4))


def heads_plan():
    return tuple(
        (partner, 528 - first)
        for partner, first, rows in plan_of(656)
        if first + rows == 656
    )


def start_fetch(me, plan, sources, target, block_rows, sems):
    copies = []
    for number, (partner, first, rows) in enumerate(plan):
        start = pl.multiple_of((me ^ partner) * block_rows + first, 64)
        copies.append(
            pltpu.make_async_copy(sources[number], target.at[pl.ds(start, rows)], sems.at[number])
        )
        copies[-1].start()
    return copies


def start_fetch_heads(me, plan, sources, target, sems):
    copies = []
    for number, (partner, first) in enumerate(plan):
        for half in range(2):
            head = (me ^ partner) * 2 + half
            head = (head & ~3) | ((head & 1) << 1) | ((head >> 1) & 1)
            copies.append(
                pltpu.make_async_copy(
                    sources[number].at[pl.ds(first + half * HD, HD)],
                    target.at[pl.ds(pl.multiple_of(head * HD, HD), HD)],
                    sems.at[len(copies)],
                )
            )
            copies[-1].start()
    return copies


def turn(values, cosine, sine):
    lane = lax.broadcasted_iota(jnp.int32, values.shape, 1)
    other = jnp.where(
        lane % HD < HD // 2, pltpu.roll(values, 128 - HD // 2, 1), pltpu.roll(values, HD // 2, 1)
    )
    return values * cosine + other * sine


def project_kernel(plan, me_ref, tokens_ref, cos_ref, sin_ref, *refs):
    count = len(plan)
    query_ref, pair_ref, extra_ref, mats, sems = refs[count:]
    copies = start_fetch(me_ref[0], plan, refs[:count], mats, 128, sems)
    stream = tokens_ref[...].astype(F32)
    scaled = stream * lax.rsqrt(jnp.mean(stream * stream, axis=-1, keepdims=True) + norm_eps)
    for copy in copies:
        copy.wait()
    extra = mats[:, 2048:2176].astype(F32).T
    extra_ref[...] = extra[:48].astype(BF)
    normed = (scaled * extra[32:33]).astype(BF)
    cosine, sine = cos_ref[...], sin_ref[...]
    for part in range(4):
        query = nn(normed, mats[:, part * 256 : part * 256 + 256])
        for half in range(2):
            columns = slice(half * 128, half * 128 + 128)
            query_ref[part, :, columns] = turn(query[:, columns], cosine, sine).astype(BF)
        key = nn(normed, mats[:, 1024 + part * 128 : 1152 + part * 128])
        pair_ref[part, :, :128] = turn(key, cosine, sine).astype(BF)
        pair_ref[part, :, 128:] = nn(
            normed, mats[:, 1536 + part * 128 : 1664 + part * 128]
        ).astype(BF)


def project(me, tokens, cosine, sine, pieces):
    plan = plan_of(128)
    return pl.pallas_call(
        functools.partial(project_kernel, plan),
        out_shape=(
            shaped((4, 512, 256), BF),
            shaped((4, 512, 256), BF),
            shaped((48, 1024), BF),
        ),
        in_specs=[in_smem()] + in_vmem(3) + in_hbm(len(plan)),
        out_specs=tuple(in_vmem(3)),
        scratch_shapes=[pltpu.VMEM((1024, 2176), BF), pltpu.SemaphoreType.DMA((len(plan),))],
        compiler_params=params(),
        cost_estimate=cost(2 * 512 * 1024 * 2048, 9e6),
        name="project",
    )(me, tokens, cosine, sine, *pieces)


def lane_half(values, group):
    lane = lax.broadcasted_iota(jnp.int32, values.shape, 1)
    return jnp.where((lane < HD) == (group == 0), values, jnp.zeros((), values.dtype))


def allowed_pairs(block, step, start):
    key_at = block * KB + lax.broadcasted_iota(jnp.int32, (KB, QB), 0)
    query_at = HALO + step * QB + lax.broadcasted_iota(jnp.int32, (KB, QB), 1)
    return (key_at >= start) & (key_at <= query_at)


def attend_kernel(
    low_ref, query_ref, own_ref, halo_ref, start_ref, out_ref, log_ref,
    keys, values_t, most, total, blend,
):
    step = pl.program_id(0)

    @pl.when(step == 0)
    def _():
        for first in range(0, HALO, 512):
            rows = slice(first, first + 512)
            keys[first : first + 512, :] = halo_ref[rows, :128]
            keys[HALO + first : HALO + first + 512, :] = own_ref[rows, :128]
            values_t[:, first : first + 512] = halo_ref[rows, 128:].astype(F32).T.astype(BF)
            values_t[:, HALO + first : HALO + first + 512] = (
                own_ref[rows, 128:].astype(F32).T.astype(BF)
            )

    start = start_ref[0]
    picks = [
        lane_half(query_ref[:, half * 128 : half * 128 + 128], group)
        for half in range(2)
        for group in range(2)
    ]
    most[...] = jnp.full(most.shape, masked_score, F32)
    total[...] = jnp.zeros(total.shape, F32)
    blend[...] = jnp.zeros(blend.shape, F32)

    def visit(block, carry):
        first = pl.multiple_of(block * KB, KB)
        allowed = allowed_pairs(block, step, start)
        key = keys[pl.ds(first, KB), :]
        for number in range(4):
            scores = nt(key, picks[number]) * (attend_scale * LOG2E)
            scores = jnp.where(allowed, scores, masked_score)
            before = most[number : number + 1, :]
            top = jnp.maximum(before, jnp.max(scores, axis=0, keepdims=True))
            weight = jnp.exp2(scores - top)
            fade = jnp.exp2(before - top)
            most[number : number + 1, :] = top
            total[number : number + 1, :] = total[number : number + 1, :] * fade + jnp.sum(
                weight, axis=0, keepdims=True
            )
            group = number % 2
            value = values_t[group * HD : group * HD + HD, pl.ds(first, KB)]
            rows = slice(number * HD, number * HD + HD)
            blend[rows, :] = blend[rows, :] * fade + nn(value, weight.astype(BF))
        return carry

    lax.fori_loop(low_ref[step], step + HALO // KB + 1, visit, 0)
    for number in range(4):
        rows = slice(number * HD, number * HD + HD)
        blend[rows, :] = blend[rows, :] / total[number : number + 1, :]
    for half in range(2):
        out_ref[:, half * 128 : half * 128 + 128] = (
            blend[half * 128 : half * 128 + 128, :].T.astype(BF)
        )
    log_ref[0:4, :] = most[0:4, :] + jnp.log2(total[0:4, :])
    log_ref[4:8, :] = jnp.zeros((4, QB), F32)


def attend(low_block, query, own, halo, start):
    steps = query.shape[0] // QB
    spec = lambda shape, index: pl.BlockSpec(shape, index)
    return pl.pallas_call(
        attend_kernel,
        out_shape=(shaped((2048, 256), BF), shaped((8, 2048), F32)),
        grid_spec=pltpu.PrefetchScalarGridSpec(
            num_scalar_prefetch=1,
            grid=(steps,),
            in_specs=[
                spec((QB, 256), lambda i, low: (i, 0)),
                spec((2048, 256), lambda i, low: (0, 0)),
                spec((2048, 256), lambda i, low: (0, 0)),
                spec((1, 1, QB), lambda i, low: (i, 0, 0)),
            ],
            out_specs=(
                spec((QB, 256), lambda i, low: (i, 0)),
                spec((8, QB), lambda i, low: (0, i)),
            ),
            scratch_shapes=[
                pltpu.VMEM((2 * HALO, 128), BF),
                pltpu.VMEM((128, 2 * HALO), BF),
                pltpu.VMEM((8, QB), F32),
                pltpu.VMEM((8, QB), F32),
                pltpu.VMEM((256, QB), F32),
            ],
        ),
        compiler_params=params(),
        cost_estimate=cost(25e9, 6e6),
        name="attend",
    )(low_block, query, own, halo, start)


def attend_back_kernel(
    low_ref, query_ref, own_ref, halo_ref, start_ref, out_ref, grad_ref, log_ref,
    query_grad_ref, own_grad_ref, halo_grad_ref,
    keys, values, keys_t, key_grad, value_grad, blend,
):
    step = pl.program_id(0)

    @pl.when(step == 0)
    def _():
        for first in range(0, HALO, 512):
            rows = slice(first, first + 512)
            late = slice(HALO + first, HALO + first + 512)
            keys[rows, :] = halo_ref[rows, :128]
            keys[late, :] = own_ref[rows, :128]
            values[rows, :] = halo_ref[rows, 128:]
            values[late, :] = own_ref[rows, 128:]
            keys_t[:, rows] = halo_ref[rows, :128].astype(F32).T.astype(BF)
            keys_t[:, late] = own_ref[rows, :128].astype(F32).T.astype(BF)
        key_grad[...] = jnp.zeros(key_grad.shape, F32)
        value_grad[...] = jnp.zeros(value_grad.shape, F32)

    start = start_ref[0]
    picks, incoming, centres = [], [], []
    for half in range(2):
        columns = slice(half * 128, half * 128 + 128)
        product = (out_ref[:, columns].astype(F32) * grad_ref[:, columns].astype(F32)).T
        for group in range(2):
            picks.append(lane_half(query_ref[:, columns], group))
            incoming.append(lane_half(grad_ref[:, columns], group))
            centres.append(
                jnp.sum(product[group * HD : group * HD + HD, :], axis=0, keepdims=True)
            )
    blend[...] = jnp.zeros(blend.shape, F32)

    def visit(block, carry):
        first = pl.multiple_of(block * KB, KB)
        allowed = allowed_pairs(block, step, start)
        here = pl.ds(first, KB)
        key, value = keys[here, :], values[here, :]
        for number in range(4):
            scores = nt(key, picks[number]) * (attend_scale * LOG2E)
            weight = jnp.where(
                allowed, jnp.exp2(scores - log_ref[number : number + 1, :]), 0.0
            )
            weight_grad = nt(value, incoming[number])
            score_grad = (weight * (weight_grad - centres[number])).astype(BF)
            value_grad[here, :] += nn(weight.astype(BF), incoming[number])
            key_grad[here, :] += nn(score_grad, picks[number])
            group = number % 2
            rows = slice(number * HD, number * HD + HD)
            blend[rows, :] += nn(keys_t[group * HD : group * HD + HD, here], score_grad)
        return carry

    lax.fori_loop(low_ref[step], step + HALO // KB + 1, visit, 0)
    for half in range(2):
        query_grad_ref[:, half * 128 : half * 128 + 128] = (
            (blend[half * 128 : half * 128 + 128, :] * attend_scale).T.astype(BF)
        )

    @pl.when(step == pl.num_programs(0) - 1)
    def _():
        for first in range(0, HALO, 512):
            rows = slice(first, first + 512)
            late = slice(HALO + first, HALO + first + 512)
            halo_grad_ref[rows, :128] = (key_grad[rows, :] * attend_scale).astype(BF)
            halo_grad_ref[rows, 128:] = value_grad[rows, :].astype(BF)
            own_grad_ref[rows, :128] = key_grad[late, :] * attend_scale
            own_grad_ref[rows, 128:] = value_grad[late, :]


def attend_back(low_block, query, own, halo, start, out, grad, logs):
    steps = query.shape[0] // QB
    spec = lambda shape, index: pl.BlockSpec(shape, index)
    tile = spec((QB, 256), lambda i, low: (i, 0))
    whole = spec((2048, 256), lambda i, low: (0, 0))
    return pl.pallas_call(
        attend_back_kernel,
        out_shape=(
            shaped((2048, 256), BF),
            shaped((2048, 256), F32),
            shaped((2048, 256), BF),
        ),
        grid_spec=pltpu.PrefetchScalarGridSpec(
            num_scalar_prefetch=1,
            grid=(steps,),
            in_specs=[
                tile,
                whole,
                whole,
                spec((1, 1, QB), lambda i, low: (i, 0, 0)),
                tile,
                tile,
                spec((8, QB), lambda i, low: (0, i)),
            ],
            out_specs=(tile, whole, whole),
            scratch_shapes=[
                pltpu.VMEM((2 * HALO, 128), BF),
                pltpu.VMEM((2 * HALO, 128), BF),
                pltpu.VMEM((128, 2 * HALO), BF),
                pltpu.VMEM((2 * HALO, 128), F32),
                pltpu.VMEM((2 * HALO, 128), F32),
                pltpu.VMEM((256, QB), F32),
            ],
        ),
        compiler_params=params(),
        cost_estimate=cost(60e9, 10e6),
        name="attend_back",
    )(low_block, query, own, halo, start, out, grad, logs)


def after_kernel(plan, me_ref, tokens_ref, attended_ref, extra_ref, routed_ref, *refs):
    count = len(plan)
    hidden_ref, payload_ref, gates_ref, mats, sems = refs[count:]
    copies = start_fetch_heads(me_ref[0], plan, refs[:count], mats, sems)
    stream = tokens_ref[...].astype(F32)
    for copy in copies:
        copy.wait()
    branch = nn(attended_ref[0], mats[0:256, :])
    for part in range(1, 4):
        branch += nn(attended_ref[part], mats[part * 256 : part * 256 + 256, :])
    hidden = stream + branch_scale * branch
    hidden_ref[...] = hidden
    inverse = lax.rsqrt(jnp.mean(hidden * hidden, axis=-1, keepdims=True) + norm_eps)
    normed = (hidden * inverse * extra_ref[33:34, :].astype(F32)).astype(BF)
    payload_ref[0:512, :] = normed
    logits = nt(extra_ref[0:32, :], normed)
    routed = routed_ref[...] > 0.5
    top = jnp.max(jnp.where(routed, logits, masked_score), axis=0, keepdims=True)
    raised = jnp.where(routed, jnp.exp(logits - top), 0.0)
    gates = raised / jnp.sum(raised, axis=0, keepdims=True)
    gates_ref[...] = gates
    low = gates.astype(BF)
    payload_ref[512:528, 0:512] = low[0:16, :]
    payload_ref[512:528, 512:1024] = low[16:32, :]


def after_attention(me, tokens, attended, extra, routed, pieces):
    plan = heads_plan()
    return pl.pallas_call(
        functools.partial(after_kernel, plan),
        out_shape=(shaped((512, 1024), F32), shaped((528, 1024), BF), shaped((32, 512), F32)),
        in_specs=[in_smem()] + in_vmem(4) + in_hbm(len(plan)),
        out_specs=tuple(in_vmem(3)),
        scratch_shapes=[pltpu.VMEM((1024, 1024), BF), pltpu.SemaphoreType.DMA((16,))],
        compiler_params=params(),
        cost_estimate=cost(2 * 512 * 1024 * 1024, 8e6),
        name="after_attention",
    )(me, tokens, attended, extra, routed, *pieces)


def own_rows(me, packed):
    first = me * 4
    side = jnp.where(first < 16, packed[:, :512], packed[:, 512:])
    row = lax.broadcasted_iota(jnp.int32, side.shape, 0)
    return [
        jnp.sum(jnp.where(row == first % 16 + expert, side, 0.0), axis=0, keepdims=True)
        for expert in range(4)
    ]


def stand_up(rows):
    row = lax.broadcasted_iota(jnp.int32, (128, 512), 0)
    lying = jnp.zeros((128, 512), F32)
    for number, values in enumerate(rows):
        lying = jnp.where(row == number, values, lying)
    return lying.T


def slot_hot(slot_row):
    at = lax.broadcasted_iota(jnp.int32, (144, 512), 0).astype(F32)
    return at == slot_row


def block_plan(partners, height):
    return tuple(
        (partners.index(partner), first, min(rows, 528 - first))
        for partner, first, rows in plan_of(height)
        if partner in partners
    )


def start_blocks(plan, sources, target, sems):
    copies = []
    for number, (place, first, rows) in enumerate(plan):
        copies.append(
            pltpu.make_async_copy(
                sources[number].at[pl.ds(0, rows)],
                target.at[place, pl.ds(first, rows)],
                sems.at[number],
            )
        )
        copies[-1].start()
    return copies


def pick_grad_kernel(plan, blocks, me_ref, *refs):
    count = len(plan)
    rows_ref, slots_ref, columns_ref, held, made, sems, out_sems = refs[count:]
    copies = start_blocks(plan, refs[:count], held, sems)
    leaving = []
    for block in range(blocks):
        for copy, (place, _, _) in zip(copies, plan):
            if place == block:
                copy.wait()
        tokens = held[block, 0:512, :]
        slots = own_rows(me_ref[0], held[block, 512:528, :].astype(F32))
        for expert in range(4):
            hot = jnp.where(slot_hot(slots[expert]), 1.0, 0.0).astype(BF)
            made[block, expert * 144 : expert * 144 + 144, :] = nn(hot, tokens).astype(BF)
            slots_ref[block, expert : expert + 1, :] = slots[expert]
        columns_ref[block] = stand_up(slots).astype(BF)
        leaving.append(
            pltpu.make_async_copy(made.at[block], rows_ref.at[block], out_sems.at[block])
        )
        leaving[-1].start()
    for copy in leaving:
        copy.wait()


def pick_grads(me, partners, pieces):
    blocks, plan = len(partners), block_plan(partners, 656)
    return pl.pallas_call(
        functools.partial(pick_grad_kernel, plan, blocks),
        out_shape=(
            shaped((blocks, 576, 1024), BF),
            shaped((blocks, 4, 512), F32),
            shaped((blocks, 512, 128), BF),
        ),
        in_specs=[in_smem()] + in_hbm(len(pieces)),
        out_specs=tuple(in_hbm(1) + in_vmem(2)),
        scratch_shapes=[
            pltpu.VMEM((blocks, 528, 1024), BF),
            pltpu.VMEM((blocks, 576, 1024), BF),
            pltpu.SemaphoreType.DMA((len(pieces),)),
            pltpu.SemaphoreType.DMA((blocks,)),
        ],
        compiler_params=params(),
        cost_estimate=cost(blocks * 2 * 576 * 512 * 1024, blocks * 2.4e6),
        name="pick_grads",
    )(me, *pieces)


def pick_rows_kernel(plan, blocks, me_ref, slots_ref, *refs):
    count = len(plan)
    rows_ref, gate_ref, columns_ref, held, made, sems, out_sems = refs[count:]
    copies = start_blocks(plan, refs[:count], held, sems)
    leaving = []
    for block in range(blocks):
        for copy, (place, _, _) in zip(copies, plan):
            if place == block:
                copy.wait()
        tokens = held[block, 0:512, :]
        gates = own_rows(me_ref[0], held[block, 512:528, :].astype(F32))
        for expert in range(4):
            match = slot_hot(slots_ref[block, expert : expert + 1, :])
            hot = jnp.where(match, 1.0, 0.0).astype(BF)
            rows = slice(expert * 144, expert * 144 + 144)
            made[block, rows, :] = nn(hot, tokens).astype(BF)
            gate = jnp.sum(jnp.where(match, gates[expert], 0.0), axis=1, keepdims=True)
            gate_ref[block, rows, :] = jnp.broadcast_to(gate, (144, 128)).astype(BF)
        columns_ref[block] = stand_up(gates).astype(BF)
        leaving.append(
            pltpu.make_async_copy(made.at[block], rows_ref.at[block], out_sems.at[block])
        )
        leaving[-1].start()
    for copy in leaving:
        copy.wait()


def pick_rows(me, slots, partners, pieces):
    blocks, plan = len(partners), block_plan(partners, 528)
    return pl.pallas_call(
        functools.partial(pick_rows_kernel, plan, blocks),
        out_shape=(
            shaped((blocks, 576, 1024), BF),
            shaped((blocks, 576, 128), BF),
            shaped((blocks, 512, 128), BF),
        ),
        in_specs=[in_smem()] + in_vmem(1) + in_hbm(len(pieces)),
        out_specs=tuple(in_hbm(1) + in_vmem(2)),
        scratch_shapes=[
            pltpu.VMEM((blocks, 528, 1024), BF),
            pltpu.VMEM((blocks, 576, 1024), BF),
            pltpu.SemaphoreType.DMA((len(pieces),)),
            pltpu.SemaphoreType.DMA((blocks,)),
        ],
        compiler_params=params(),
        cost_estimate=cost(blocks * 2 * 576 * 512 * 1024, blocks * 2.4e6),
        name="pick_rows",
    )(me, slots, *pieces)


def expert_kernel(base, me_ref, *refs):
    rows_refs, grads_refs, gate_refs = refs[0:2], refs[2:4], refs[4:6]
    gate_w, up_w, down_w = (ref[0] for ref in refs[6:9])
    out_ref, in_grad_ref, mark_ref, grad_ref = refs[9:13]
    lin_grads, inners, out_grads, inputs = refs[13:17]
    expert = me_ref[0] * 4 + base + pl.program_id(0)
    for part in range(2):
        at = slice(part * 576, part * 576 + 576)

        def both(pair):
            if part == 0:
                return pair[0][0:4].reshape(576, -1)
            return jnp.concatenate(
                [pair[0][4:6].reshape(288, -1), pair[1][...].reshape(288, -1)], axis=0
            )

        rows, grads, gate = both(rows_refs), both(grads_refs), both(gate_refs)
        inputs[at, :] = rows
        gate_lin = nn(rows, gate_w)
        up_lin = nn(rows, up_w)
        sigma = 1.0 / (1.0 + jnp.exp(-gate_lin))
        swished = gate_lin * sigma
        inner = (swished * up_lin).astype(BF)
        inners[at, :] = inner
        result = nn(inner, down_w).astype(BF)
        out_ref[part * 4 : part * 4 + 4] = result.reshape(4, 144, 1024)
        wide = grads.astype(F32)
        gate_slot = jnp.sum(wide * result.astype(F32), axis=1, keepdims=True)
        lane = lax.broadcasted_iota(jnp.int32, (576, 128), 1)
        mark_ref[part * 4 : part * 4 + 4] = (
            jnp.where(lane == expert, gate_slot, 0.0).astype(BF).reshape(4, 144, 128)
        )
        out_grad = (wide * gate[:, 0:1].astype(F32)).astype(BF)
        out_grads[at, :] = out_grad
        inner_grad = nt(out_grad, down_w)
        gate_lin_grad = (
            inner_grad * up_lin * sigma * (1.0 + gate_lin * (1.0 - sigma))
        ).astype(BF)
        up_lin_grad = (inner_grad * swished).astype(BF)
        lin_grads[at, 0:512] = gate_lin_grad
        lin_grads[at, 512:1024] = up_lin_grad
        in_grad_ref[part * 4 : part * 4 + 4] = (
            (nt(gate_lin_grad, gate_w) + nt(up_lin_grad, up_w)).astype(BF).reshape(4, 144, 1024)
        )
    down_grad = tn(inners[...], out_grads[...]).astype(BF)
    grad_ref[2048:2560, :] = down_grad[:, 0:512]
    grad_ref[2560:3072, :] = down_grad[:, 512:1024]
    grad_ref[0:1024, :] = tn(inputs[...], lin_grads[:, 0:512]).astype(BF)
    grad_ref[1024:2048, :] = tn(inputs[...], lin_grads[:, 512:1024]).astype(BF)


def run_experts(me, base, count, rows, grads, gates, gate_w, up_w, down_w):
    spec = pl.BlockSpec
    wide = [spec((blocks, 144, 1024), lambda e: (0, base + e, 0)) for blocks in (6, 2)]
    slim = [spec((blocks, 144, 128), lambda e: (0, base + e, 0)) for blocks in (6, 2)]
    tall_w = spec((1, 1024, 512), lambda e: (base + e, 0, 0))
    flat_w = spec((1, 512, 1024), lambda e: (base + e, 0, 0))
    return pl.pallas_call(
        functools.partial(expert_kernel, base),
        out_shape=(
            shaped((8, 144 * count, 1024), BF),
            shaped((8, 144 * count, 1024), BF),
            shaped((8, 144 * count, 128), BF),
            shaped((3072 * count, 512), BF),
        ),
        grid=(count,),
        in_specs=[in_smem()] + wide * 2 + slim + [tall_w, tall_w, flat_w],
        out_specs=(
            spec((8, 144, 1024), lambda e: (0, e, 0)),
            spec((8, 144, 1024), lambda e: (0, e, 0)),
            spec((8, 144, 128), lambda e: (0, e, 0)),
            spec((3072, 512), lambda e: (e, 0)),
        ),
        scratch_shapes=[
            pltpu.VMEM((1152, 1024), BF),
            pltpu.VMEM((1152, 512), BF),
            pltpu.VMEM((1152, 1024), BF),
            pltpu.VMEM((1152, 1024), BF),
        ],
        compiler_params=params(),
        cost_estimate=cost(count * 11e9, count * 15e6),
        name="experts",
    )(me, *rows, *grads, *gates, gate_w, up_w, down_w)


def combine_kernel(calls, weighted, *refs):
    slot_ref = refs[0]
    refs = refs[1:]
    gate_ref = None
    if weighted:
        gate_ref, refs = refs[0], refs[1:]
    value_refs, refs = refs[:calls], refs[calls:]
    mark_refs = ()
    if not weighted:
        mark_refs, refs = refs[:calls], refs[calls:]
    out_ref = refs[0]
    here = 4 // calls
    slots = slot_ref[0].astype(F32)
    lane = lax.broadcasted_iota(jnp.int32, (512, 144 * here), 1).astype(F32)
    total, marks = None, None
    for call in range(calls):
        hot = jnp.zeros((512, 144 * here), F32)
        for local_expert in range(here):
            number = call * here + local_expert
            slot = slots[:, number : number + 1]
            place = jnp.where(slot < 144.0, slot + 144.0 * local_expert, -1.0)
            put = 1.0
            if weighted:
                put = gate_ref[0][:, number : number + 1].astype(F32)
            hot = jnp.where(lane == place, put, hot)
        hot = hot.astype(BF)
        term = nn(hot, value_refs[call][0])
        total = term if total is None else total + term
        if not weighted:
            mark = nn(hot, mark_refs[call][0])
            marks = mark if marks is None else marks + mark
    out_ref[0, 0:512, :] = total.astype(BF)
    if not weighted:
        lying = marks.T[0:32, :].astype(BF)
        out_ref[0, 512:528, 0:512] = lying[0:16, :]
        out_ref[0, 512:528, 512:1024] = lying[16:32, :]


def combine(parity, slots, gates, values, marks):
    calls = len(values)
    weighted = gates is not None
    rows = 512 if weighted else 528
    column = pl.BlockSpec((1, 512, 128), lambda i: (2 * i + parity, 0, 0))
    wide = pl.BlockSpec((1, 576 // calls, 1024), lambda i: (2 * i + parity, 0, 0))
    slim = pl.BlockSpec((1, 576 // calls, 128), lambda i: (2 * i + parity, 0, 0))
    args = [slots] + ([gates] if weighted else []) + list(values) + list(marks)
    return pl.pallas_call(
        functools.partial(combine_kernel, calls, weighted),
        out_shape=shaped((4, rows, 1024), BF),
        grid=(4,),
        in_specs=[column]
        + ([column] if weighted else [])
        + [wide] * calls
        + [slim] * len(marks),
        out_specs=pl.BlockSpec((1, rows, 1024), lambda i: (i, 0, 0)),
        compiler_params=params(),
        cost_estimate=cost(4 * 2 * 512 * 768 * 1024, 10e6),
        name="combine",
    )(*args)


def back_kernel(
    plan, me_ref, sum_ref, sum_x_ref, sum_y_ref, hidden_ref, cot_ref, payload_ref, gates_ref,
    extra_ref, *refs,
):
    count = len(plan)
    hidden_grad_ref, branch_grad_ref, attended_grad_ref, small_ref, mats, sems = refs[count:]
    copies = start_fetch_heads(me_ref[0], plan, refs[:count], mats, sems)
    total = (
        sum_ref[...].astype(F32) + sum_x_ref[...].astype(F32) + sum_y_ref[...].astype(F32)
    )
    gate_grad = jnp.concatenate([total[512:528, 0:512], total[512:528, 512:1024]], axis=0)
    gates = gates_ref[...]
    logit_grad = (
        gates * (gate_grad - jnp.sum(gates * gate_grad, axis=0, keepdims=True))
    ).astype(BF)
    normed_grad = total[0:512, :] + tn(logit_grad, extra_ref[0:32, :])
    hidden = hidden_ref[...]
    inverse = lax.rsqrt(jnp.mean(hidden * hidden, axis=-1, keepdims=True) + norm_eps)
    scaled = normed_grad * extra_ref[33:34, :].astype(F32)
    spread_out = inverse * inverse * inverse * jnp.mean(hidden * scaled, axis=-1, keepdims=True)
    hidden_grad = cot_ref[...].astype(F32) + inverse * scaled - hidden * spread_out
    hidden_grad_ref[...] = hidden_grad
    small_ref[0:32, :] = nn(logit_grad, payload_ref[0:512, :])
    small_ref[32:40, :] = jnp.broadcast_to(
        jnp.sum(normed_grad * hidden * inverse, axis=0, keepdims=True), (8, 1024)
    )
    branch_grad = (branch_scale * hidden_grad).astype(BF)
    branch_grad_ref[...] = branch_grad
    for copy in copies:
        copy.wait()
    for part in range(4):
        attended_grad_ref[part] = nt(
            branch_grad, mats[part * 256 : part * 256 + 256, :]
        ).astype(BF)


def back_to_attention(me, sums, hidden, cotangent, payload, gates, extra, pieces):
    plan = heads_plan()
    return pl.pallas_call(
        functools.partial(back_kernel, plan),
        out_shape=(
            shaped((512, 1024), F32),
            shaped((512, 1024), BF),
            shaped((4, 512, 256), BF),
            shaped((40, 1024), F32),
        ),
        in_specs=[in_smem()] + in_vmem(8) + in_hbm(len(plan)),
        out_specs=tuple(in_vmem(4)),
        scratch_shapes=[pltpu.VMEM((1024, 1024), BF), pltpu.SemaphoreType.DMA((16,))],
        compiler_params=params(),
        cost_estimate=cost(2 * 512 * 1024 * 1024, 12e6),
        name="back_to_attention",
    )(me, *sums, hidden, cotangent, payload, gates, extra, *pieces)


def deal_out(me, big, odd_ref, even_ref):
    for pair in range(4):
        for target, partner in ((even_ref, 2 * pair), (odd_ref, 2 * pair + 1)):
            start = pl.multiple_of((me ^ partner) * 128, 128)
            target[pair] = big[pl.ds(start, 128), :]


def out_grad_kernel(me_ref, attended_ref, branch_grad_ref, small_ref, odd_ref, even_ref, big):
    branch_grad = branch_grad_ref[...]
    for part in range(4):
        grad = tn(attended_ref[part], branch_grad).astype(BF)
        for half in range(2):
            for group in range(2):
                source = half * 128 + group * HD
                target = part * 256 + (2 * group + half) * HD
                big[target : target + HD, 0:1024] = grad[source : source + HD, :]
    small = jnp.concatenate([small_ref[...], jnp.zeros((88, 1024), F32)], axis=0)
    big[:, 1024:1152] = small.T.astype(BF)
    deal_out(me_ref[0], big, odd_ref, even_ref)


def out_grads_of(me, attended, branch_grad, small):
    return pl.pallas_call(
        out_grad_kernel,
        out_shape=(shaped((4, 128, 1152), BF), shaped((4, 128, 1152), BF)),
        in_specs=[in_smem()] + in_vmem(3),
        out_specs=tuple(in_vmem(2)),
        scratch_shapes=[pltpu.VMEM((1024, 1152), BF)],
        compiler_params=params(),
        cost_estimate=cost(2 * 512 * 1024 * 1024, 5e6),
        name="out_grads",
    )(me, attended, branch_grad, small)


def input_kernel(
    plan, me_ref, tokens_ref, cos_ref, sin_ref, query_grad_ref, pair_grad_ref, extra_ref,
    hidden_grad_ref, *refs,
):
    count = len(plan)
    input_grad_ref, odd_ref, even_ref, mats, big, lin, sems = refs[count:]
    me = me_ref[0]
    copies = start_fetch(me, plan, refs[:count], mats, 128, sems)
    stream = tokens_ref[...].astype(F32)
    inverse = lax.rsqrt(jnp.mean(stream * stream, axis=-1, keepdims=True) + norm_eps)
    gain = extra_ref[32:33, :].astype(F32)
    normed = (stream * inverse * gain).astype(BF)
    cosine, sine = cos_ref[...], -sin_ref[...]
    for part in range(4):
        for half in range(2):
            columns = slice(half * 128, half * 128 + 128)
            lin[:, part * 256 + half * 128 : part * 256 + half * 128 + 128] = turn(
                query_grad_ref[part, :, columns].astype(F32), cosine, sine
            ).astype(BF)
        lin[:, 1024 + part * 128 : 1152 + part * 128] = turn(
            pair_grad_ref[part, :, 0:128].astype(F32), cosine, sine
        ).astype(BF)
        lin[:, 1536 + part * 128 : 1664 + part * 128] = pair_grad_ref[part, :, 128:256]
    normed_t = normed.astype(F32).T.astype(BF)
    for first in range(0, 2048, 512):
        big[:, first : first + 512] = nn(normed_t, lin[:, first : first + 512]).astype(BF)
    for copy in copies:
        copy.wait()
    normed_grad = nt(lin[...], mats[:, 0:2048])
    row = jnp.sum(normed_grad * stream * inverse, axis=0, keepdims=True)
    big[:, 2048:2176] = jnp.broadcast_to(row, (128, 1024)).T.astype(BF)
    deal_out(me, big, odd_ref, even_ref)
    scaled = normed_grad * gain
    spread_out = inverse * inverse * inverse * jnp.mean(stream * scaled, axis=-1, keepdims=True)
    input_grad_ref[...] = (
        hidden_grad_ref[...] + inverse * scaled - stream * spread_out
    ).astype(BF)


def input_grads(me, tokens, cosine, sine, query_grad, pair_grad, extra, hidden_grad, pieces):
    plan = plan_of(128)
    return pl.pallas_call(
        functools.partial(input_kernel, plan),
        out_shape=(
            shaped((512, 1024), BF),
            shaped((4, 128, 2176), BF),
            shaped((4, 128, 2176), BF),
        ),
        in_specs=[in_smem()] + in_vmem(7) + in_hbm(len(plan)),
        out_specs=tuple(in_vmem(3)),
        scratch_shapes=[
            pltpu.VMEM((1024, 2176), BF),
            pltpu.VMEM((1024, 2176), BF),
            pltpu.VMEM((512, 2048), BF),
            pltpu.SemaphoreType.DMA((len(plan),)),
        ],
        compiler_params=params(),
        cost_estimate=cost(4 * 512 * 1024 * 2048, 15e6),
        name="input_grads",
    )(me, tokens, cosine, sine, query_grad, pair_grad, extra, hidden_grad, *pieces)


def dense_slots(routes, ranks, experts):
    mine = routes[None, :, :] == jnp.arange(experts, dtype=jnp.int32)[:, None, None]
    far = jnp.int32(1 << 20)
    rank = jnp.min(jnp.where(mine, ranks[None, :, :], far), axis=-1)
    slot = jnp.sum((rank[:, None, :] < rank[:, :, None]).astype(jnp.int32), axis=-1)
    routed = rank < far
    return (jnp.where(routed & (slot < 144), slot, 255).astype(BF), routed.astype(F32))


def swap_middle(values):
    rows, columns = values.shape
    parts = values.reshape(rows, columns // 256, 2, 2, HD)
    return parts.transpose(0, 1, 3, 2, 4).reshape(rows, columns)


class Copies:
    def __init__(self, seq):
        self.outer = (seq == 0) | (seq == 3)
        self.waiting = []
        self.flying = []
        self.sums = []

    def add(self, value):
        self.waiting.append(value)

    def step(self, gate):
        arrived, self.flying = self.flying, []
        fresh, self.waiting = self.waiting[:1], self.waiting[1:]
        gate, received, fresh = lax.optimization_barrier(
            (gate, [item[2] for item in arrived], fresh)
        )
        ready = []
        for (phase, value, _), got in zip(arrived, received):
            if phase == 2:
                self.sums.append(jnp.where(self.outer, got, value))
            else:
                ready.append((phase + 1, add_low(value, got)))
        ready += [(0, value) for value in fresh]
        for phase, value in ready:
            pairs = (((0, 1), (3, 2)), ((1, 2), (2, 1)), ((1, 0), (2, 3)))[phase]
            self.flying.append((phase, value, lax.ppermute(value, "sp", pairs)))
        return gate


def sum_line(value, seq):
    outer = (seq == 0) | (seq == 3)
    value = add_low(value, lax.ppermute(value, "sp", ((0, 1), (3, 2))))
    value = add_low(value, lax.ppermute(value, "sp", ((1, 2), (2, 1))))
    return jnp.where(outer, lax.ppermute(value, "sp", ((1, 0), (2, 3))), value)


def fast_local(
    tokens, documents, expert_routes, drop_rank, norm1_gain, query_weight, key_weight,
    value_weight, out_weight, norm2_gain, router_weight, gate_weight, up_weight, down_weight,
    output_grad,
):
    fsdp = lax.axis_index("fsdp")
    seq = lax.axis_index("sp")
    me = jnp.reshape(fsdp, (1,)).astype(jnp.int32)
    small = jnp.concatenate(
        [
            router_weight,
            norm1_gain[:, None],
            norm2_gain[:, None],
            jnp.zeros((128, 94), BF),
        ],
        axis=1,
    )
    shard = jnp.concatenate([swap_middle(query_weight), key_weight, value_weight, small], axis=1)
    project_pieces = spread(shard)

    slots, routed = dense_slots(expert_routes, drop_rank, 32)
    mixture_grad = (branch_scale * output_grad.astype(F32)).astype(BF)
    grad_payload = jnp.concatenate(
        [mixture_grad, jnp.concatenate([slots[:16], slots[16:]], axis=1), out_weight], axis=0
    )

    block_start = fsdp * 2048
    position_all = doc_position(documents)
    position_span = lax.dynamic_slice_in_dim(position_all, block_start, 2048)
    position = lax.dynamic_slice_in_dim(position_span, seq * 512, 512)
    cosine, sine_table = rope_tables(position, HD)
    cosine = jnp.tile(cosine, (1, 2))
    signs = jnp.where(jnp.arange(128) % HD < HD // 2, -1.0, 1.0).astype(F32)
    sine = jnp.tile(sine_table, (1, 2)) * signs[None, :]
    start = HALO + jnp.arange(2048, dtype=jnp.int32) - position_span
    start_rows = start.reshape(2048 // QB, 1, QB)
    low_block = start_rows[:, 0, 0] // KB

    query, pair, extra = project(me, tokens, cosine, sine, project_pieces)
    grad_payload = hold(grad_payload, project_pieces[6], project_pieces[7])
    own, beside = grad_payload, flip(grad_payload, 1)
    along_x, along_y = flip(grad_payload, 2), flip(grad_payload, 4)
    pair_heads = lax.all_to_all(
        pair.reshape(2048, 256), "sp", split_axis=0, concat_axis=0, tiled=True
    )
    pair_heads, query, beside, along_x, along_y = lax.optimization_barrier(
        (pair_heads, query, beside, along_x, along_y)
    )
    query_heads = lax.all_to_all(
        query.reshape(2048, 256), "sp", split_axis=0, concat_axis=0, tiled=True
    )
    halo = from_behind(pair_heads, "fsdp", 1)
    near_pieces = (own, beside, along_x, flip(along_x, 1), along_y, flip(along_y, 1))
    diagonal = spread_diagonal(near_pieces)
    query_heads, halo, near_pieces, diagonal = lax.optimization_barrier(
        (query_heads, halo, near_pieces, diagonal)
    )
    near, far = (0, 1, 2, 3, 4, 5), (6, 7)
    blended, logs = attend(low_block, query_heads, pair_heads, halo, start_rows)
    attended = lax.all_to_all(blended, "sp", split_axis=0, concat_axis=0, tiled=True).reshape(
        4, 512, 256
    )
    far_pieces = spread_far(diagonal)
    near_grads = pick_grads(me, near, near_pieces)
    far_grads = pick_grads(me, far, far_pieces)
    attended, near_grads, far_grads = lax.optimization_barrier((attended, near_grads, far_grads))
    grad_rows, slot_rows, slot_columns = zip(near_grads, far_grads)
    grad_pieces = near_pieces + far_pieces
    out_pieces = [
        piece
        for piece, (_, first, rows) in zip(grad_pieces, plan_of(656))
        if first + rows == 656
    ]
    hidden_one, payload, gates = after_attention(
        me, tokens, attended, extra, routed, out_pieces
    )
    near_pieces = spread_near(payload)
    diagonal = spread_diagonal(near_pieces)
    near_rows = pick_rows(me, slot_rows[0], near, near_pieces)
    near_rows, diagonal = lax.optimization_barrier((near_rows, diagonal))
    far_rows = pick_rows(me, slot_rows[1], far, spread_far(diagonal))
    rows, slot_gates, gate_columns = zip(near_rows, far_rows)
    slot_columns = jnp.concatenate(slot_columns, axis=0)
    gate_columns = jnp.concatenate(gate_columns, axis=0)
    copies = Copies(seq)
    results, here = [], me
    for expert in range(4):
        results.append(
            run_experts(
                here, expert, 1, rows, grad_rows, slot_gates, gate_weight, up_weight, down_weight
            )
        )
        copies.add(results[-1][3])
        if expert == 0:
            here = copies.step(me)
    outs, in_grads, marks, _ = zip(*results)
    in_grads = copies.step(in_grads)
    odd = combine(1, slot_columns, None, in_grads, marks)
    even = combine(0, slot_columns, None, in_grads, marks)
    sums = collect(odd, even, copies.step)
    hidden_grad, branch_grad, attended_grad, small_grads = back_to_attention(
        me, sums, hidden_one, output_grad, payload, gates, extra, out_pieces
    )
    grad_heads = lax.all_to_all(
        attended_grad.reshape(2048, 256), "sp", split_axis=0, concat_axis=0, tiled=True
    )
    grad_heads = copies.step(grad_heads)
    odd_mix = combine(1, slot_columns, gate_columns, outs, ())
    even_mix = combine(0, slot_columns, gate_columns, outs, ())
    mixture = collect(odd_mix, even_mix)
    output = (
        hidden_one
        + branch_scale
        * (mixture[0].astype(F32) + mixture[1].astype(F32) + mixture[2].astype(F32))
    ).astype(BF)
    out_sums = collect(*out_grads_of(me, attended, branch_grad, small_grads))

    query_back, own_back, halo_back = attend_back(
        low_block, query_heads, pair_heads, halo, start_rows, blended, grad_heads, logs
    )
    query_back, own_back, halo_back = copies.step((query_back, own_back, halo_back))
    pair_back = (own_back + from_behind(halo_back, "fsdp", -1).astype(F32)).astype(BF)
    query_grad = lax.all_to_all(
        query_back, "sp", split_axis=0, concat_axis=0, tiled=True
    ).reshape(4, 512, 256)
    pair_grad = lax.all_to_all(
        pair_back, "sp", split_axis=0, concat_axis=0, tiled=True
    ).reshape(4, 512, 256)
    query_grad, pair_grad = copies.step((query_grad, pair_grad))
    input_grad, odd_in, even_in = input_grads(
        me, tokens, cosine, sine, query_grad, pair_grad, extra, hidden_grad, project_pieces
    )
    in_sums = collect(odd_in, even_in)

    out_shard = sum(term.astype(F32) for term in out_sums).astype(BF)
    in_shard = sum(term.astype(F32) for term in in_sums).astype(BF)
    shards = sum_line(jnp.concatenate([in_shard, out_shard], axis=1), seq)
    in_shard, out_shard = shards[:, 0:2176], shards[:, 2176:3328]
    while copies.flying:
        copies.step(())
    stacked = [
        jnp.stack([total[0:1024] for total in copies.sums]).astype(F32),
        jnp.stack([total[1024:2048] for total in copies.sums]).astype(F32),
        jnp.stack(
            [
                jnp.concatenate([total[2048:2560], total[2560:3072]], axis=1)
                for total in copies.sums
            ]
        ).astype(F32),
    ]
    return (
        output,
        input_grad,
        in_shard[:, 2048].astype(F32),
        swap_middle(in_shard[:, 0:1024]).astype(F32),
        in_shard[:, 1024:1536].astype(F32),
        in_shard[:, 1536:2048].astype(F32),
        out_shard[:, 0:1024].astype(F32),
        out_shard[:, 1056].astype(F32),
        out_shard[:, 1024:1056].astype(F32),
        *stacked,
    )


def solution(mesh):
    placed = (
        P(("fsdp", "sp"), None),
        P(),
        P(("fsdp", "sp"), None),
        P(("fsdp", "sp"), None),
        P("fsdp"),
        P("fsdp", None),
        P("fsdp", None),
        P("fsdp", None),
        P("fsdp", None),
        P("fsdp"),
        P("fsdp", None),
        P("fsdp", None, None),
        P("fsdp", None, None),
        P("fsdp", None, None),
        P(("fsdp", "sp"), None),
    )
    fast = mesh.shape["sp"] == 4 and mesh.shape["fsdp"] == 8
    return jax.shard_map(
        fast_local if fast else local,
        mesh=mesh,
        in_specs=placed,
        out_specs=(
            P(("fsdp", "sp"), None),
            P(("fsdp", "sp"), None),
            P("fsdp"),
            P("fsdp", None),
            P("fsdp", None),
            P("fsdp", None),
            P("fsdp", None),
            P("fsdp"),
            P("fsdp", None),
            P("fsdp", None, None),
            P("fsdp", None, None),
            P("fsdp", None, None),
        ),
        check_vma=False,
    )
```

```python
import functools

import jax
import jax.numpy as jnp
from jax import lax
from jax.sharding import PartitionSpec as P
from jax.experimental import pallas as pl
from jax.experimental.pallas import tpu as pltpu

HD = 64
DOC_CAP = 2048


attend_scale = 0.015625
branch_scale = 0.22
norm_eps = 1e-06
rope_base = 10000.0
masked_score = -1e30


def from_behind(value, axis, steps):
    count = lax.axis_size(axis)
    initial, last = (max(0, -steps), min(count, count - steps))
    return lax.ppermute(value, axis, [(source, source + steps) for source in range(initial, last)])


def doc_position(documents):
    length = documents.shape[0]
    place = jnp.arange(length, dtype=jnp.int32)
    fresh = jnp.concatenate([jnp.ones((1,), dtype=bool), documents[1:] != documents[:-1]])
    opening = lax.cummax(jnp.where(fresh, place, 0), axis=0)
    return place - opening


def rope_tables(position, head_size):
    half_size = head_size // 2
    spacing = jnp.arange(half_size, dtype=jnp.float32)
    inverse = rope_base ** (-2.0 * spacing / head_size)
    angle = position.astype(jnp.float32)[:, None] * inverse[None, :]
    return (jnp.tile(jnp.cos(angle), (1, 2)), jnp.tile(jnp.sin(angle), (1, 2)))


def rotate(values, cosine, sine_table):
    half_size = values.shape[-1] // 2
    turned = jnp.concatenate([-values[..., half_size:], values[..., :half_size]], axis=-1)
    return values * cosine[:, None, :] + turned * sine_table[:, None, :]


def route_slots(routes, rank_table, experts, capacity):
    flat_routes = routes.reshape(-1)
    flat_ranks = rank_table.reshape(-1)
    ordered = flat_routes[jnp.argsort(flat_ranks)]
    onehot = (ordered[:, None] == jnp.arange(experts, dtype=jnp.int32)[None, :]).astype(jnp.int32)
    earlier = jnp.cumsum(onehot, axis=0) - onehot
    slot_sorted = jnp.sum(earlier * onehot, axis=1)
    slot_number = slot_sorted[flat_ranks].reshape(routes.shape)
    kept_pair = slot_number < capacity
    return (jnp.where(kept_pair, routes * capacity + slot_number, -1), kept_pair)


def to_owner(values):
    return lax.all_to_all(values, "fsdp", split_axis=0, concat_axis=1, tiled=True)


def from_owner(values):
    return lax.all_to_all(values, "fsdp", split_axis=1, concat_axis=0, tiled=True)


def expert_forward(slot_rows, gate_mats, up_mats, down_mats):
    gate_lin = jnp.einsum("nrd,ndf->nrf", slot_rows, gate_mats, preferred_element_type=jnp.float32)
    up_lin = jnp.einsum("nrd,ndf->nrf", slot_rows, up_mats, preferred_element_type=jnp.float32)
    inner = (gate_lin * jax.nn.sigmoid(gate_lin) * up_lin).astype(jnp.bfloat16)
    result = jnp.einsum(
        "nrf,nfd->nrd", inner, down_mats, preferred_element_type=jnp.float32
    ).astype(jnp.bfloat16)
    return (gate_lin, up_lin, result)


def expert_backward(slot_rows, gate_lin, up_lin, result_grad, gate_mats, up_mats, down_mats):
    sigma = jax.nn.sigmoid(gate_lin)
    swished = gate_lin * sigma
    inner = (swished * up_lin).astype(jnp.bfloat16)
    inner_grad = jnp.einsum(
        "nrd,nfd->nrf", result_grad, down_mats, preferred_element_type=jnp.float32
    )
    gate_grad = (inner_grad * up_lin * sigma * (1.0 + gate_lin * (1.0 - sigma))).astype(
        jnp.bfloat16
    )
    up_grad = (inner_grad * swished).astype(jnp.bfloat16)
    rows_grad = jnp.einsum("nrf,ndf->nrd", gate_grad, gate_mats, preferred_element_type=jnp.float32)
    rows_grad = (
        rows_grad + jnp.einsum("nrf,ndf->nrd", up_grad, up_mats, preferred_element_type=jnp.float32)
    ).astype(jnp.bfloat16)
    gate_part = jnp.einsum("nrd,nrf->ndf", slot_rows, gate_grad, preferred_element_type=jnp.float32)
    up_part = jnp.einsum("nrd,nrf->ndf", slot_rows, up_grad, preferred_element_type=jnp.float32)
    down_part = jnp.einsum("nrf,nrd->nfd", inner, result_grad, preferred_element_type=jnp.float32)
    return (rows_grad, gate_part, up_part, down_part)


def local(
    tokens,
    documents,
    expert_routes,
    drop_rank,
    norm1_gain,
    query_weight,
    key_weight,
    value_weight,
    out_weight,
    norm2_gain,
    router_weight,
    gate_weight,
    up_weight,
    down_weight,
    output_grad,
):
    rows_dev, model_width = tokens.shape
    heads_query = query_weight.shape[1] // HD
    heads_kv = key_weight.shape[1] // HD
    repeat = heads_query // heads_kv
    experts = router_weight.shape[1]
    top_count = expert_routes.shape[1]
    seq_parts = lax.axis_size("sp")
    span_rows = seq_parts * rows_dev
    query_block = min(512, span_rows)
    block_count = span_rows // query_block
    doc_most = min(DOC_CAP, span_rows)
    window = doc_most + query_block
    capacity = (9 * rows_dev * top_count + 8 * experts - 1) // (8 * experts)
    slot_total = experts * capacity
    block_start = lax.axis_index("fsdp") * span_rows
    row_start = block_start + lax.axis_index("sp") * rows_dev
    position = lax.dynamic_slice_in_dim(doc_position(documents), row_start, rows_dev)
    cosine, sine_table = rope_tables(position, HD)
    gain_first, query_mat, key_mat, value_mat, out_mat, gain_second, router_mat = (
        lax.all_gather(norm1_gain, "fsdp", axis=0, tiled=True),
        lax.all_gather(query_weight, "fsdp", axis=0, tiled=True),
        lax.all_gather(key_weight, "fsdp", axis=0, tiled=True),
        lax.all_gather(value_weight, "fsdp", axis=0, tiled=True),
        lax.all_gather(out_weight, "fsdp", axis=0, tiled=True),
        lax.all_gather(norm2_gain, "fsdp", axis=0, tiled=True),
        lax.all_gather(router_weight, "fsdp", axis=0, tiled=True),
    )
    stream = tokens.astype(jnp.float32)
    inverse_one = lax.rsqrt(jnp.mean(stream * stream, axis=-1, keepdims=True) + norm_eps)
    gain_one = gain_first.astype(jnp.float32)
    normed_one = (stream * inverse_one * gain_one).astype(jnp.bfloat16)
    query_lin = jnp.dot(normed_one, query_mat, preferred_element_type=jnp.float32).reshape(
        rows_dev, heads_query, HD
    )
    key_lin = jnp.dot(normed_one, key_mat, preferred_element_type=jnp.float32).reshape(
        rows_dev, heads_kv, HD
    )
    value_low = (
        jnp.dot(normed_one, value_mat, preferred_element_type=jnp.float32)
        .astype(jnp.bfloat16)
        .reshape(rows_dev, heads_kv, HD)
    )
    query_low = (
        rotate(query_lin, cosine, sine_table)
        .astype(jnp.bfloat16)
        .reshape(rows_dev, heads_kv, repeat * HD)
    )
    key_low = rotate(key_lin, cosine, sine_table).astype(jnp.bfloat16)
    packed = jnp.concatenate([query_low, key_low, value_low], axis=-1)
    by_heads = lax.all_to_all(packed, "sp", split_axis=1, concat_axis=0, tiled=True)
    groups = by_heads.shape[1]
    query_heads = by_heads[:, :, : repeat * HD]
    pair_heads = by_heads[:, :, repeat * HD :]
    halo_rows = from_behind(pair_heads[span_rows - doc_most :], "fsdp", 1)
    near_pairs = jnp.concatenate([halo_rows, pair_heads], axis=0)
    query_docs = lax.dynamic_slice_in_dim(documents, block_start, span_rows)
    near_docs = lax.dynamic_slice_in_dim(
        jnp.concatenate([jnp.full((doc_most,), -1, jnp.int32), documents]),
        block_start,
        doc_most + span_rows,
    )
    causal = jnp.arange(window)[None, :] <= jnp.arange(query_block)[:, None] + doc_most

    def block_scores(block_index):
        first_row = block_index * query_block
        query_part = lax.dynamic_slice_in_dim(query_heads, first_row, query_block).reshape(
            query_block, groups, repeat, HD
        )
        pair_part = lax.dynamic_slice_in_dim(near_pairs, first_row, window)
        key_part = pair_part[:, :, :HD]
        value_part = pair_part[:, :, HD:]
        own_docs = lax.dynamic_slice_in_dim(query_docs, first_row, query_block)
        seen_docs = lax.dynamic_slice_in_dim(near_docs, first_row, window)
        allowed = (seen_docs[None, :] == own_docs[:, None]) & causal
        scores = attend_scale * jnp.einsum(
            "rgjd,cgd->gjrc", query_part, key_part, preferred_element_type=jnp.float32
        )
        return (query_part, key_part, value_part, jnp.where(allowed, scores, masked_score))

    def attend_block(block_index):
        query_part, key_part, value_part, scores = block_scores(block_index)
        row_max = jnp.max(scores, axis=-1, keepdims=True)
        exponent = jnp.exp(scores - row_max)
        row_total = jnp.sum(exponent, axis=-1, keepdims=True)
        softmaxed = (exponent / row_total).astype(jnp.bfloat16)
        blended = jnp.einsum(
            "gjrc,cgd->rgjd", softmaxed, value_part, preferred_element_type=jnp.float32
        )
        return (
            blended.astype(jnp.bfloat16).reshape(query_block, groups, repeat * HD),
            (row_max + jnp.log(row_total))[..., 0],
        )

    blended_all, log_totals = lax.map(attend_block, jnp.arange(block_count, dtype=jnp.int32))
    attended = lax.all_to_all(
        blended_all.reshape(span_rows, groups, repeat * HD),
        "sp",
        split_axis=0,
        concat_axis=1,
        tiled=True,
    ).reshape(rows_dev, heads_query * HD)
    branch = jnp.dot(attended, out_mat, preferred_element_type=jnp.float32)
    hidden_one = stream + branch_scale * branch
    inverse_two = lax.rsqrt(jnp.mean(hidden_one * hidden_one, axis=-1, keepdims=True) + norm_eps)
    gain_two = gain_second.astype(jnp.float32)
    normed_two = (hidden_one * inverse_two * gain_two).astype(jnp.bfloat16)
    logits = jnp.dot(normed_two, router_mat, preferred_element_type=jnp.float32)
    route_hot = expert_routes[:, :, None] == jnp.arange(experts, dtype=jnp.int32)[None, None, :]
    chosen = jnp.sum(jnp.where(route_hot, logits[:, None, :], 0.0), axis=-1)
    chosen_max = jnp.max(chosen, axis=-1, keepdims=True)
    gate_exp = jnp.exp(chosen - chosen_max)
    gates = gate_exp / jnp.sum(gate_exp, axis=-1, keepdims=True)
    gate_low = gates.astype(jnp.bfloat16)
    slot_index, kept_pair = route_slots(expert_routes, drop_rank, experts, capacity)
    columns = jnp.arange(slot_total, dtype=jnp.int32)[None, :]
    dispatch = jnp.zeros((rows_dev, slot_total), dtype=bool)
    combine = jnp.zeros((rows_dev, slot_total), dtype=jnp.bfloat16)
    for route_slot in range(top_count):
        landing = slot_index[:, route_slot : route_slot + 1] == columns
        dispatch = dispatch | landing
        combine = combine + jnp.where(
            landing, gate_low[:, route_slot : route_slot + 1], jnp.zeros((), jnp.bfloat16)
        )
    dispatch_low = dispatch.astype(jnp.bfloat16)
    expert_in = (
        jnp.einsum("tc,td->cd", dispatch_low, normed_two, preferred_element_type=jnp.float32)
        .astype(jnp.bfloat16)
        .reshape(experts, capacity, model_width)
    )
    owned_in = to_owner(expert_in)
    gate_lin, up_lin, owned_out = expert_forward(owned_in, gate_weight, up_weight, down_weight)
    expert_out = from_owner(owned_out)
    mixture = jnp.dot(
        combine, expert_out.reshape(slot_total, model_width), preferred_element_type=jnp.float32
    )
    output = (hidden_one + branch_scale * mixture).astype(jnp.bfloat16)
    cotangent = output_grad.astype(jnp.float32)
    mixture_grad = (branch_scale * cotangent).astype(jnp.bfloat16)
    out_grad = (
        jnp.einsum("tc,td->cd", combine, mixture_grad, preferred_element_type=jnp.float32)
        .astype(jnp.bfloat16)
        .reshape(experts, capacity, model_width)
    )
    taken = jnp.take(
        expert_out.reshape(slot_total, model_width), jnp.clip(slot_index, 0, slot_total - 1), axis=0
    )
    gate_grad = jnp.where(
        kept_pair,
        jnp.einsum("tkd,td->tk", taken, mixture_grad, preferred_element_type=jnp.float32),
        0.0,
    )
    chosen_grad = gates * (gate_grad - jnp.sum(gates * gate_grad, axis=-1, keepdims=True))
    logit_grad = jnp.sum(jnp.where(route_hot, chosen_grad[:, :, None], 0.0), axis=1).astype(
        jnp.bfloat16
    )
    router_grad = jnp.einsum(
        "td,te->de", normed_two, logit_grad, preferred_element_type=jnp.float32
    )
    normed_two_grad = jnp.einsum(
        "te,de->td", logit_grad, router_mat, preferred_element_type=jnp.float32
    )
    owned_grad = to_owner(out_grad)
    owned_in_grad, expert_gate_grad, expert_up_grad, expert_down_grad = expert_backward(
        owned_in, gate_lin, up_lin, owned_grad, gate_weight, up_weight, down_weight
    )
    expert_in_grad = from_owner(owned_in_grad)
    normed_two_grad = normed_two_grad + jnp.dot(
        dispatch_low,
        expert_in_grad.reshape(slot_total, model_width),
        preferred_element_type=jnp.float32,
    )
    scaled_two = normed_two_grad * gain_two
    hidden_grad = (
        cotangent
        + inverse_two * scaled_two
        - hidden_one * inverse_two**3 * jnp.mean(hidden_one * scaled_two, axis=-1, keepdims=True)
    )
    norm_two_grad = jnp.sum(normed_two_grad * hidden_one * inverse_two, axis=0)
    branch_grad = (branch_scale * hidden_grad).astype(jnp.bfloat16)
    out_mat_grad = jnp.einsum(
        "tk,td->kd", attended, branch_grad, preferred_element_type=jnp.float32
    )
    attended_grad = jnp.einsum(
        "td,kd->tk", branch_grad, out_mat, preferred_element_type=jnp.float32
    ).astype(jnp.bfloat16)
    grad_heads = lax.all_to_all(
        attended_grad.reshape(rows_dev, heads_kv, repeat * HD),
        "sp",
        split_axis=1,
        concat_axis=0,
        tiled=True,
    )

    def attend_back(accumulated, block_item):
        block_index, log_total = block_item
        query_part, key_part, value_part, scores = block_scores(block_index)
        first_row = block_index * query_block
        softmaxed = jnp.exp(scores - log_total[..., None])
        incoming = lax.dynamic_slice_in_dim(grad_heads, first_row, query_block).reshape(
            query_block, groups, repeat, HD
        )
        softmax_grad = jnp.einsum(
            "rgjd,cgd->gjrc", incoming, value_part, preferred_element_type=jnp.float32
        )
        centred = jnp.sum(softmaxed * softmax_grad, axis=-1, keepdims=True)
        score_grad = (softmaxed * (softmax_grad - centred)).astype(jnp.bfloat16)
        query_grad = attend_scale * jnp.einsum(
            "gjrc,cgd->rgjd", score_grad, key_part, preferred_element_type=jnp.float32
        )
        key_grad = attend_scale * jnp.einsum(
            "gjrc,rgjd->cgd", score_grad, query_part, preferred_element_type=jnp.float32
        )
        value_grad = jnp.einsum(
            "gjrc,rgjd->cgd",
            softmaxed.astype(jnp.bfloat16),
            incoming,
            preferred_element_type=jnp.float32,
        )
        current = lax.dynamic_slice_in_dim(accumulated, first_row, window)
        updated = lax.dynamic_update_slice_in_dim(
            accumulated, current + jnp.concatenate([key_grad, value_grad], axis=-1), first_row, 0
        )
        return (updated, query_grad.reshape(query_block, groups, repeat * HD))

    pair_grad, query_grads = lax.scan(
        attend_back,
        jnp.zeros((doc_most + span_rows, groups, 2 * HD), jnp.float32),
        (jnp.arange(block_count, dtype=jnp.int32), log_totals),
    )
    returned = from_behind(pair_grad[:doc_most].astype(jnp.bfloat16), "fsdp", -1).astype(
        jnp.float32
    )
    own_grad = pair_grad[doc_most:]
    own_grad = jnp.concatenate(
        [own_grad[: span_rows - doc_most], own_grad[span_rows - doc_most :] + returned], axis=0
    )
    packed_grad = jnp.concatenate(
        [
            query_grads.reshape(span_rows, groups, repeat * HD).astype(jnp.bfloat16),
            own_grad.astype(jnp.bfloat16),
        ],
        axis=-1,
    )
    by_tokens = lax.all_to_all(packed_grad, "sp", split_axis=0, concat_axis=1, tiled=True)
    query_rot_grad = (
        by_tokens[:, :, : repeat * HD].astype(jnp.float32).reshape(rows_dev, heads_query, HD)
    )
    key_rot_grad = by_tokens[:, :, repeat * HD : (repeat + 1) * HD].astype(jnp.float32)
    value_grad_low = by_tokens[:, :, (repeat + 1) * HD :].reshape(rows_dev, heads_kv * HD)
    query_lin_grad = (
        rotate(query_rot_grad, cosine, -sine_table)
        .astype(jnp.bfloat16)
        .reshape(rows_dev, heads_query * HD)
    )
    key_lin_grad = (
        rotate(key_rot_grad, cosine, -sine_table)
        .astype(jnp.bfloat16)
        .reshape(rows_dev, heads_kv * HD)
    )
    query_mat_grad = jnp.einsum(
        "td,tk->dk", normed_one, query_lin_grad, preferred_element_type=jnp.float32
    )
    key_mat_grad = jnp.einsum(
        "td,tk->dk", normed_one, key_lin_grad, preferred_element_type=jnp.float32
    )
    value_mat_grad = jnp.einsum(
        "td,tk->dk", normed_one, value_grad_low, preferred_element_type=jnp.float32
    )
    normed_one_grad = jnp.einsum(
        "tk,dk->td", query_lin_grad, query_mat, preferred_element_type=jnp.float32
    )
    normed_one_grad = normed_one_grad + jnp.einsum(
        "tk,dk->td", key_lin_grad, key_mat, preferred_element_type=jnp.float32
    )
    normed_one_grad = normed_one_grad + jnp.einsum(
        "tk,dk->td", value_grad_low, value_mat, preferred_element_type=jnp.float32
    )
    scaled_one = normed_one_grad * gain_one
    input_grad = (
        hidden_grad
        + inverse_one * scaled_one
        - stream * inverse_one**3 * jnp.mean(stream * scaled_one, axis=-1, keepdims=True)
    ).astype(jnp.bfloat16)
    norm_one_grad = jnp.sum(normed_one_grad * stream * inverse_one, axis=0)
    shard_norm_one, shard_query, shard_key, shard_value, shard_out, shard_norm_two, shard_router = (
        lax.psum_scatter(
            norm_one_grad.astype(jnp.bfloat16), "fsdp", scatter_dimension=0, tiled=True
        ).astype(jnp.float32),
        lax.psum_scatter(
            query_mat_grad.astype(jnp.bfloat16), "fsdp", scatter_dimension=0, tiled=True
        ).astype(jnp.float32),
        lax.psum_scatter(
            key_mat_grad.astype(jnp.bfloat16), "fsdp", scatter_dimension=0, tiled=True
        ).astype(jnp.float32),
        lax.psum_scatter(
            value_mat_grad.astype(jnp.bfloat16), "fsdp", scatter_dimension=0, tiled=True
        ).astype(jnp.float32),
        lax.psum_scatter(
            out_mat_grad.astype(jnp.bfloat16), "fsdp", scatter_dimension=0, tiled=True
        ).astype(jnp.float32),
        lax.psum_scatter(
            norm_two_grad.astype(jnp.bfloat16), "fsdp", scatter_dimension=0, tiled=True
        ).astype(jnp.float32),
        lax.psum_scatter(
            router_grad.astype(jnp.bfloat16), "fsdp", scatter_dimension=0, tiled=True
        ).astype(jnp.float32),
    )
    (
        summed_norm_one,
        summed_query,
        summed_key,
        summed_value,
        summed_out,
        summed_norm_two,
        summed_router,
        summed_gate,
        summed_up,
        summed_down,
    ) = (
        lax.psum(shard_norm_one.astype(jnp.bfloat16), "sp").astype(jnp.float32),
        lax.psum(shard_query.astype(jnp.bfloat16), "sp").astype(jnp.float32),
        lax.psum(shard_key.astype(jnp.bfloat16), "sp").astype(jnp.float32),
        lax.psum(shard_value.astype(jnp.bfloat16), "sp").astype(jnp.float32),
        lax.psum(shard_out.astype(jnp.bfloat16), "sp").astype(jnp.float32),
        lax.psum(shard_norm_two.astype(jnp.bfloat16), "sp").astype(jnp.float32),
        lax.psum(shard_router.astype(jnp.bfloat16), "sp").astype(jnp.float32),
        lax.psum(expert_gate_grad.astype(jnp.bfloat16), "sp").astype(jnp.float32),
        lax.psum(expert_up_grad.astype(jnp.bfloat16), "sp").astype(jnp.float32),
        lax.psum(expert_down_grad.astype(jnp.bfloat16), "sp").astype(jnp.float32),
    )
    return (
        output,
        input_grad,
        summed_norm_one,
        summed_query,
        summed_key,
        summed_value,
        summed_out,
        summed_norm_two,
        summed_router,
        summed_gate,
        summed_up,
        summed_down,
    )


BF = jnp.bfloat16
F32 = jnp.float32
LOG2E = 1.4426950408889634
QB = 512
KB = 512
BACK_KB = 256
HALO = 2048
VMEM_MOST = 60 * 1024 * 1024


def in_vmem(count):
    return [pl.BlockSpec(memory_space=pltpu.VMEM)] * count


def in_hbm(count):
    return [pl.BlockSpec(memory_space=pl.ANY)] * count


def in_smem():
    return pl.BlockSpec(memory_space=pltpu.SMEM)


def shaped(shape, kind):
    return jax.ShapeDtypeStruct(shape, kind)


def params():
    return pltpu.CompilerParams(vmem_limit_bytes=VMEM_MOST)


def cost(flops, moved, transcendentals=0):
    return pl.CostEstimate(
        flops=int(flops) // 8, bytes_accessed=int(moved) // 8, transcendentals=int(transcendentals)
    )


def nn(left, right):
    return lax.dot_general(left, right, (((1,), (0,)), ((), ())), preferred_element_type=F32)


def nt(left, right):
    return lax.dot_general(left, right, (((1,), (1,)), ((), ())), preferred_element_type=F32)


def tn(left, right):
    return lax.dot_general(left, right, (((0,), (0,)), ((), ())), preferred_element_type=F32)


def flip(value, bit):
    return lax.ppermute(value, "fsdp", [(place, place ^ bit) for place in range(8)])


def half_rows(rows):
    return (rows // 2 + 15) // 16 * 16


def plan_of(rows):
    half = half_rows(rows)
    return (
        (0, 0, rows),
        (1, 0, rows),
        (2, 0, rows),
        (3, 0, rows),
        (4, 0, rows),
        (5, 0, rows),
        (6, 0, half),
        (6, half, rows - half),
        (7, 0, half),
        (7, half, rows - half),
    )


def hold(value, *others):
    return lax.optimization_barrier((value, others))[0]


def spread_near(own):
    along_x, along_y = flip(own, 2), flip(own, 4)
    return (own, flip(own, 1), along_x, flip(along_x, 1), along_y, flip(along_y, 1))


def spread_diagonal(near):
    half = half_rows(near[0].shape[0])
    return (flip(near[4][:half], 2), flip(near[2][half:], 4))


def spread_far(diagonal):
    return (*diagonal, flip(diagonal[0], 1), flip(diagonal[1], 1))


def spread(own):
    near = spread_near(own)
    return near + spread_far(spread_diagonal(near))


def add_low(left, right):
    return (left.astype(F32) + right.astype(F32)).astype(BF)


def collect(odd, even, tick=None):
    half = half_rows(even.shape[1])
    received = flip(odd, 1)
    diagonal_low = flip(add_low(even[3, :half], received[3, :half]), 2)
    diagonal_high = flip(add_low(even[3, half:], received[3, half:]), 4)
    if tick is not None:
        diagonal_low, diagonal_high = tick((diagonal_low, diagonal_high))
    own = add_low(even[0], received[0])
    for_y = even[2].astype(F32) + received[2].astype(F32)
    for_x = even[1].astype(F32) + received[1].astype(F32)
    for_y = jnp.concatenate([for_y[:half] + diagonal_low.astype(F32), for_y[half:]]).astype(BF)
    for_x = jnp.concatenate([for_x[:half], for_x[half:] + diagonal_high.astype(F32)]).astype(BF)
    return (own, flip(for_x, 2), flip(for_y, 4))


def start_fetch(me, plan, sources, target, block_rows, sems):
    copies = []
    for number, (partner, first, rows) in enumerate(plan):
        start = pl.multiple_of((me ^ partner) * block_rows + first, 64)
        copies.append(
            pltpu.make_async_copy(
                sources[number].at[:, pl.ds(0, 2176)],
                target.at[pl.ds(start, rows)],
                sems.at[number],
            )
        )
        copies[-1].start()
    return copies


def start_fetch_out(me, plan, sources, target, sems):
    copies = []
    for number, (partner, first, rows) in enumerate(plan):
        start = pl.multiple_of((me ^ partner) * 128 + first, 64)
        copies.append(
            pltpu.make_async_copy(
                sources[number].at[:, pl.ds(2176, 1024)],
                target.at[pl.ds(start, rows)],
                sems.at[number],
            )
        )
        copies[-1].start()
    return copies


def turn(values, cosine, sine):
    lane = lax.broadcasted_iota(jnp.int32, values.shape, 1)
    other = jnp.where(
        lane % HD < HD // 2, pltpu.roll(values, 128 - HD // 2, 1), pltpu.roll(values, HD // 2, 1)
    )
    return values * cosine + other * sine


def side_by_side(left, right, group):
    lane = lax.broadcasted_iota(jnp.int32, left.shape, 1)
    if group == 0:
        return jnp.where(lane < HD, left, pltpu.roll(right, HD, 1))
    return jnp.where(lane < HD, pltpu.roll(left, HD, 1), right)


def project_kernel(plan, me_ref, tokens_ref, cos_ref, sin_ref, *refs):
    count = len(plan)
    first_ref, second_ref, extra_ref, mats, sems = refs[count:]
    copies = start_fetch(me_ref[0], plan, refs[:count], mats, 128, sems)
    stream = tokens_ref[...].astype(F32)
    scaled = stream * lax.rsqrt(jnp.mean(stream * stream, axis=-1, keepdims=True) + norm_eps)
    for copy in copies:
        copy.wait()
    extra = mats[:, 2048:2176].astype(F32).T
    extra_ref[...] = extra[:48].astype(BF)
    normed = (scaled * extra[32:33]).astype(BF)
    cosine, sine = cos_ref[...], sin_ref[...]
    for part in range(4):
        query = nn(normed, mats[:, part * 256 : part * 256 + 256])
        key = turn(nn(normed, mats[:, 1024 + part * 128 : 1152 + part * 128]), cosine, sine)
        value = nn(normed, mats[:, 1536 + part * 128 : 1664 + part * 128])
        for group, target in enumerate((first_ref, second_ref)):
            target[part, :, 0:128] = turn(
                query[:, group * 128 : group * 128 + 128], cosine, sine
            ).astype(BF)
            target[part, :, 128:256] = side_by_side(key, value, group).astype(BF)


def project(me, tokens, cosine, sine, pieces):
    plan = plan_of(128)
    return pl.pallas_call(
        functools.partial(project_kernel, plan),
        out_shape=(
            shaped((4, 512, 256), BF),
            shaped((4, 512, 256), BF),
            shaped((48, 1024), BF),
        ),
        in_specs=[in_smem()] + in_vmem(3) + in_hbm(len(plan)),
        out_specs=tuple(in_vmem(3)),
        scratch_shapes=[pltpu.VMEM((1024, 2176), BF), pltpu.SemaphoreType.DMA((len(plan),))],
        compiler_params=params(),
        cost_estimate=cost(2 * 512 * 1024 * 2048, 9e6),
        name="project",
    )(me, tokens, cosine, sine, *pieces)


def placed(values, half, side):
    moved = values.astype(F32)
    if half != side:
        moved = pltpu.roll(moved, HD, 1)
    lane = lax.broadcasted_iota(jnp.int32, values.shape, 1)
    return jnp.where((lane < HD) == (side == 0), moved, 0.0).astype(values.dtype)


def allowed_pairs(first, rows, step, start):
    key_at = first + lax.broadcasted_iota(jnp.int32, (rows, QB), 0)
    query_at = HALO + step * QB + lax.broadcasted_iota(jnp.int32, (rows, QB), 1)
    return (key_at >= start) & (key_at <= query_at)


def attend_kernel(
    low_ref, own_ref, halo_ref, start_ref, out_ref, log_ref, pairs, pairs_t, most, total, blend
):
    step = pl.program_id(0)

    @pl.when(step == 0)
    def _():
        for first in range(0, HALO, 512):
            rows = slice(first, first + 512)
            late = slice(HALO + first, HALO + first + 512)
            pairs[rows, :] = halo_ref[rows, :]
            pairs[late, :] = own_ref[rows, 128:256]
            pairs_t[:, rows] = halo_ref[rows, :].astype(F32).T.astype(BF)
            pairs_t[:, late] = own_ref[rows, 128:256].astype(F32).T.astype(BF)

    start = start_ref[0]
    query = own_ref[pl.ds(pl.multiple_of(step * QB, QB), QB), 0:128]
    picks = [placed(query, half, 0) for half in range(2)]
    most[...] = jnp.full(most.shape, masked_score, F32)
    total[...] = jnp.zeros(total.shape, F32)
    blend[...] = jnp.zeros(blend.shape, F32)

    def visit(block, carry):
        first = pl.multiple_of(block * KB, KB)
        allowed = allowed_pairs(first, KB, step, start)
        pair = pairs[pl.ds(first, KB), :]
        value = pairs_t[HD:128, pl.ds(first, KB)]
        raw = [nt(pair, picks[half]) for half in range(2)]
        for half in range(2):
            scores = jnp.where(allowed, raw[half] * (attend_scale * LOG2E), masked_score)
            before = most[half : half + 1, :]
            top = jnp.maximum(before, jnp.max(scores, axis=0, keepdims=True))
            weight = jnp.exp2(scores - top)
            fade = jnp.exp2(before - top)
            most[half : half + 1, :] = top
            total[half : half + 1, :] = total[half : half + 1, :] * fade + jnp.sum(
                weight, axis=0, keepdims=True
            )
            rows = slice(half * HD, half * HD + HD)
            blend[rows, :] = blend[rows, :] * fade + nn(value, weight.astype(BF))
        return carry

    lax.fori_loop(low_ref[step], (HALO + (step + 1) * QB) // KB, visit, 0)
    for half in range(2):
        rows = slice(half * HD, half * HD + HD)
        blend[rows, :] = blend[rows, :] / total[half : half + 1, :]
    out_ref[...] = blend[...].T.astype(BF)
    log_ref[0:2, :] = most[0:2, :] + jnp.log2(total[0:2, :])
    log_ref[2:8, :] = jnp.zeros((6, QB), F32)


def attend(low_block, own, halo, start):
    spec = lambda shape, index: pl.BlockSpec(shape, index)
    return pl.pallas_call(
        attend_kernel,
        out_shape=(shaped((2048, 128), BF), shaped((8, 2048), F32)),
        grid_spec=pltpu.PrefetchScalarGridSpec(
            num_scalar_prefetch=1,
            grid=(2048 // QB,),
            in_specs=[
                spec((2048, 256), lambda i, low: (0, 0)),
                spec((2048, 128), lambda i, low: (0, 0)),
                spec((1, 1, QB), lambda i, low: (i, 0, 0)),
            ],
            out_specs=(
                spec((QB, 128), lambda i, low: (i, 0)),
                spec((8, QB), lambda i, low: (0, i)),
            ),
            scratch_shapes=[
                pltpu.VMEM((2 * HALO, 128), BF),
                pltpu.VMEM((128, 2 * HALO), BF),
                pltpu.VMEM((8, QB), F32),
                pltpu.VMEM((8, QB), F32),
                pltpu.VMEM((128, QB), F32),
            ],
        ),
        compiler_params=params(),
        cost_estimate=cost(12e9, 3e6),
        name="attend",
    )(low_block, own, halo, start)


def attend_back_kernel(
    low_ref, own_ref, halo_ref, start_ref, out_ref, grad_ref, log_ref,
    own_grad_ref, halo_grad_ref, pairs, pairs_t, pair_grad, blend,
):
    step = pl.program_id(0)

    @pl.when(step == 0)
    def _():
        for first in range(0, HALO, 512):
            rows = slice(first, first + 512)
            late = slice(HALO + first, HALO + first + 512)
            pairs[rows, :] = halo_ref[rows, :]
            pairs[late, :] = own_ref[rows, 128:256]
            pairs_t[:, rows] = halo_ref[rows, :].astype(F32).T.astype(BF)
            pairs_t[:, late] = own_ref[rows, 128:256].astype(F32).T.astype(BF)
        pair_grad[...] = jnp.zeros(pair_grad.shape, F32)

    start = start_ref[0]
    here_rows = pl.ds(pl.multiple_of(step * QB, QB), QB)
    query, grad = own_ref[here_rows, 0:128], grad_ref[...]
    product = (out_ref[...].astype(F32) * grad.astype(F32)).T
    picks, incoming, centres = [], [], []
    for half in range(2):
        picks.append(placed(query, half, 0))
        incoming.append(placed(grad, half, 1))
        centres.append(jnp.sum(product[half * HD : half * HD + HD, :], axis=0, keepdims=True))
    blend[...] = jnp.zeros(blend.shape, F32)

    def visit(block, carry):
        first = pl.multiple_of(block * BACK_KB, BACK_KB)
        allowed = allowed_pairs(first, BACK_KB, step, start)
        here = pl.ds(first, BACK_KB)
        pair, key_t = pairs[here, :], pairs_t[0:HD, here]
        for half in range(2):
            scores = nt(pair, picks[half]) * (attend_scale * LOG2E)
            weight = jnp.where(allowed, jnp.exp2(scores - log_ref[half : half + 1, :]), 0.0)
            weight_grad = nt(pair, incoming[half])
            score_grad = (
                weight * (weight_grad - centres[half]) * attend_scale
            ).astype(BF)
            pair_grad[here, :] += nn(weight.astype(BF), incoming[half]) + nn(
                score_grad, picks[half]
            )
            blend[half * HD : half * HD + HD, :] += nn(key_t, score_grad)
        return carry

    lax.fori_loop(low_ref[step], (HALO + (step + 1) * QB) // BACK_KB, visit, 0)
    own_grad_ref[here_rows, 0:128] = blend[...].T

    @pl.when(step == pl.num_programs(0) - 1)
    def _():
        for first in range(0, HALO, 512):
            rows = slice(first, first + 512)
            late = slice(HALO + first, HALO + first + 512)
            halo_grad_ref[rows, :] = pair_grad[rows, :].astype(BF)
            own_grad_ref[rows, 128:256] = pair_grad[late, :]


def attend_back(low_block, own, halo, start, out, grad, logs):
    spec = lambda shape, index: pl.BlockSpec(shape, index)
    tile = spec((QB, 128), lambda i, low: (i, 0))
    whole = spec((2048, 256), lambda i, low: (0, 0))
    half = spec((2048, 128), lambda i, low: (0, 0))
    return pl.pallas_call(
        attend_back_kernel,
        out_shape=(shaped((2048, 256), F32), shaped((2048, 128), BF)),
        grid_spec=pltpu.PrefetchScalarGridSpec(
            num_scalar_prefetch=1,
            grid=(2048 // QB,),
            in_specs=[
                whole,
                half,
                spec((1, 1, QB), lambda i, low: (i, 0, 0)),
                tile,
                tile,
                spec((8, QB), lambda i, low: (0, i)),
            ],
            out_specs=(whole, half),
            scratch_shapes=[
                pltpu.VMEM((2 * HALO, 128), BF),
                pltpu.VMEM((128, 2 * HALO), BF),
                pltpu.VMEM((2 * HALO, 128), F32),
                pltpu.VMEM((128, QB), F32),
            ],
        ),
        compiler_params=params(),
        cost_estimate=cost(30e9, 6e6),
        name="attend_back",
    )(low_block, own, halo, start, out, grad, logs)


def after_kernel(
    plan, me_ref, tokens_ref, first_ref, second_ref, extra_ref, routed_ref, *refs
):
    count = len(plan)
    hidden_ref, payload_ref, gates_ref, mats, sems = refs[count:]
    copies = start_fetch_out(me_ref[0], plan, refs[:count], mats, sems)
    stream = tokens_ref[...].astype(F32)
    for copy in copies:
        copy.wait()
    branch = jnp.zeros((512, 1024), F32)
    for part in range(4):
        both = jnp.concatenate([first_ref[part], second_ref[part]], axis=1)
        branch += nn(both, mats[part * 256 : part * 256 + 256, :])
    hidden = stream + branch_scale * branch
    hidden_ref[...] = hidden
    inverse = lax.rsqrt(jnp.mean(hidden * hidden, axis=-1, keepdims=True) + norm_eps)
    normed = (hidden * inverse * extra_ref[33:34, :].astype(F32)).astype(BF)
    payload_ref[0:512, :] = normed
    logits = nt(extra_ref[0:32, :], normed)
    routed = routed_ref[...] > 0.5
    top = jnp.max(jnp.where(routed, logits, masked_score), axis=0, keepdims=True)
    raised = jnp.where(routed, jnp.exp(logits - top), 0.0)
    gates = raised / jnp.sum(raised, axis=0, keepdims=True)
    gates_ref[...] = gates
    low = gates.astype(BF)
    payload_ref[512:528, 0:512] = low[0:16, :]
    payload_ref[512:528, 512:1024] = low[16:32, :]


def after_attention(me, tokens, attended, extra, routed, pieces):
    plan = plan_of(128)
    return pl.pallas_call(
        functools.partial(after_kernel, plan),
        out_shape=(shaped((512, 1024), F32), shaped((528, 1024), BF), shaped((32, 512), F32)),
        in_specs=[in_smem()] + in_vmem(5) + in_hbm(len(plan)),
        out_specs=tuple(in_vmem(3)),
        scratch_shapes=[pltpu.VMEM((1024, 1024), BF), pltpu.SemaphoreType.DMA((len(plan),))],
        compiler_params=params(),
        cost_estimate=cost(2 * 512 * 1024 * 1024, 8e6),
        name="after_attention",
    )(me, tokens, *attended, extra, routed, *pieces)


def own_rows(me, packed):
    first = me * 4
    side = jnp.where(first < 16, packed[:, :512], packed[:, 512:])
    row = lax.broadcasted_iota(jnp.int32, side.shape, 0)
    return [
        jnp.sum(jnp.where(row == first % 16 + expert, side, 0.0), axis=0, keepdims=True)
        for expert in range(4)
    ]


def stand_up(rows):
    row = lax.broadcasted_iota(jnp.int32, (128, 512), 0)
    lying = jnp.zeros((128, 512), F32)
    for number, values in enumerate(rows):
        lying = jnp.where(row == number, values, lying)
    return lying.T


def slot_hot(slot_row):
    at = lax.broadcasted_iota(jnp.int32, (144, 512), 0).astype(F32)
    return at == slot_row


def block_plan(partners, height):
    return tuple(
        (partners.index(partner), first, min(rows, 528 - first))
        for partner, first, rows in plan_of(height)
        if partner in partners
    )


def start_blocks(plan, sources, target, sems):
    copies = []
    for number, (place, first, rows) in enumerate(plan):
        copies.append(
            pltpu.make_async_copy(
                sources[number].at[pl.ds(0, rows)],
                target.at[place, pl.ds(first, rows)],
                sems.at[number],
            )
        )
        copies[-1].start()
    return copies


def pick_grad_kernel(plan, blocks, me_ref, *refs):
    count = len(plan)
    rows_ref, slots_ref, columns_ref, held, made, sems, out_sems = refs[count:]
    copies = start_blocks(plan, refs[:count], held, sems)
    leaving = []
    for block in range(blocks):
        for copy, (place, _, _) in zip(copies, plan):
            if place == block:
                copy.wait()
        tokens = held[block, 0:512, :]
        slots = own_rows(me_ref[0], held[block, 512:528, :].astype(F32))
        for expert in range(4):
            hot = jnp.where(slot_hot(slots[expert]), 1.0, 0.0).astype(BF)
            made[block, expert * 144 : expert * 144 + 144, :] = nn(hot, tokens).astype(BF)
            slots_ref[block, expert : expert + 1, :] = slots[expert]
        columns_ref[block] = stand_up(slots).astype(BF)
        leaving.append(
            pltpu.make_async_copy(made.at[block], rows_ref.at[block], out_sems.at[block])
        )
        leaving[-1].start()
    for copy in leaving:
        copy.wait()


def pick_grads(me, partners, pieces):
    blocks, plan = len(partners), block_plan(partners, 528)
    return pl.pallas_call(
        functools.partial(pick_grad_kernel, plan, blocks),
        out_shape=(
            shaped((blocks, 576, 1024), BF),
            shaped((blocks, 4, 512), F32),
            shaped((blocks, 512, 128), BF),
        ),
        in_specs=[in_smem()] + in_hbm(len(pieces)),
        out_specs=tuple(in_hbm(1) + in_vmem(2)),
        scratch_shapes=[
            pltpu.VMEM((blocks, 528, 1024), BF),
            pltpu.VMEM((blocks, 576, 1024), BF),
            pltpu.SemaphoreType.DMA((len(pieces),)),
            pltpu.SemaphoreType.DMA((blocks,)),
        ],
        compiler_params=params(),
        cost_estimate=cost(blocks * 2 * 576 * 512 * 1024, blocks * 2.4e6),
        name="pick_grads",
    )(me, *pieces)


def pick_rows_kernel(plan, blocks, me_ref, slots_ref, *refs):
    count = len(plan)
    rows_ref, gate_ref, columns_ref, held, made, sems, out_sems = refs[count:]
    copies = start_blocks(plan, refs[:count], held, sems)
    leaving = []
    for block in range(blocks):
        for copy, (place, _, _) in zip(copies, plan):
            if place == block:
                copy.wait()
        tokens = held[block, 0:512, :]
        gates = own_rows(me_ref[0], held[block, 512:528, :].astype(F32))
        for expert in range(4):
            match = slot_hot(slots_ref[block, expert : expert + 1, :])
            hot = jnp.where(match, 1.0, 0.0).astype(BF)
            rows = slice(expert * 144, expert * 144 + 144)
            made[block, rows, :] = nn(hot, tokens).astype(BF)
            gate = jnp.sum(jnp.where(match, gates[expert], 0.0), axis=1, keepdims=True)
            gate_ref[block, rows, :] = jnp.broadcast_to(gate, (144, 128)).astype(BF)
        columns_ref[block] = stand_up(gates).astype(BF)
        leaving.append(
            pltpu.make_async_copy(made.at[block], rows_ref.at[block], out_sems.at[block])
        )
        leaving[-1].start()
    for copy in leaving:
        copy.wait()


def pick_rows(me, slots, partners, pieces):
    blocks, plan = len(partners), block_plan(partners, 528)
    return pl.pallas_call(
        functools.partial(pick_rows_kernel, plan, blocks),
        out_shape=(
            shaped((blocks, 576, 1024), BF),
            shaped((blocks, 576, 128), BF),
            shaped((blocks, 512, 128), BF),
        ),
        in_specs=[in_smem()] + in_vmem(1) + in_hbm(len(pieces)),
        out_specs=tuple(in_hbm(1) + in_vmem(2)),
        scratch_shapes=[
            pltpu.VMEM((blocks, 528, 1024), BF),
            pltpu.VMEM((blocks, 576, 1024), BF),
            pltpu.SemaphoreType.DMA((len(pieces),)),
            pltpu.SemaphoreType.DMA((blocks,)),
        ],
        compiler_params=params(),
        cost_estimate=cost(blocks * 2 * 576 * 512 * 1024, blocks * 2.4e6),
        name="pick_rows",
    )(me, slots, *pieces)


def both_parts(pair, part):
    if part == 0:
        return pair[0][0:4].reshape(576, -1)
    return jnp.concatenate([pair[0][4:6].reshape(288, -1), pair[1][...].reshape(288, -1)], axis=0)


def expert_grad_kernel(*refs):
    rows_refs, grads_refs, gate_refs = refs[0:2], refs[2:4], refs[4:6]
    gate_w, up_w, down_w = (ref[0] for ref in refs[6:9])
    lin_ref, inner_ref, grad_ref = refs[9:12]
    lin_grads, inners, out_grads, inputs = refs[12:16]
    for part in range(2):
        at = slice(part * 576, part * 576 + 576)
        blocks = slice(part * 4, part * 4 + 4)
        rows = both_parts(rows_refs, part)
        inputs[at, :] = rows
        gate_lin = nn(rows, gate_w)
        up_lin = nn(rows, up_w)
        sigma = 1.0 / (1.0 + jnp.exp(-gate_lin))
        swished = gate_lin * sigma
        inner = (swished * up_lin).astype(BF)
        inners[at, :] = inner
        inner_ref[blocks] = inner.reshape(4, 144, 512)
        gate = both_parts(gate_refs, part)[:, 0:1].astype(F32)
        out_grad = (both_parts(grads_refs, part).astype(F32) * gate).astype(BF)
        out_grads[at, :] = out_grad
        inner_grad = nt(out_grad, down_w)
        lin_grads[at, 0:512] = (
            inner_grad * up_lin * sigma * (1.0 + gate_lin * (1.0 - sigma))
        ).astype(BF)
        lin_grads[at, 512:1024] = (inner_grad * swished).astype(BF)
        lin_ref[blocks] = lin_grads[at, :].reshape(4, 144, 1024)
    down_grad = tn(inners[...], out_grads[...]).astype(BF)
    grad_ref[2048:2560, :] = down_grad[:, 0:512]
    grad_ref[2560:3072, :] = down_grad[:, 512:1024]
    grad_ref[0:1024, :] = tn(inputs[...], lin_grads[:, 0:512]).astype(BF)
    grad_ref[1024:2048, :] = tn(inputs[...], lin_grads[:, 512:1024]).astype(BF)


def expert_grads(base, count, rows, grads, gates, gate_w, up_w, down_w):
    spec = pl.BlockSpec
    wide = [spec((blocks, 144, 1024), lambda e: (0, base + e, 0)) for blocks in (6, 2)]
    slim = [spec((blocks, 144, 128), lambda e: (0, base + e, 0)) for blocks in (6, 2)]
    tall_w = spec((1, 1024, 512), lambda e: (base + e, 0, 0))
    flat_w = spec((1, 512, 1024), lambda e: (base + e, 0, 0))
    return pl.pallas_call(
        expert_grad_kernel,
        out_shape=(
            shaped((8, 144 * count, 1024), BF),
            shaped((8, 144 * count, 512), BF),
            shaped((3072 * count, 512), BF),
        ),
        grid=(count,),
        in_specs=wide * 2 + slim + [tall_w, tall_w, flat_w],
        out_specs=(
            spec((8, 144, 1024), lambda e: (0, e, 0)),
            spec((8, 144, 512), lambda e: (0, e, 0)),
            spec((3072, 512), lambda e: (e, 0)),
        ),
        scratch_shapes=[
            pltpu.VMEM((1152, 1024), BF),
            pltpu.VMEM((1152, 512), BF),
            pltpu.VMEM((1152, 1024), BF),
            pltpu.VMEM((1152, 1024), BF),
        ],
        compiler_params=params(),
        cost_estimate=cost(count * 8e9, count * 15e6),
        name="expert_grads",
    )(*rows, *grads, *gates, gate_w, up_w, down_w)


def expert_rows_kernel(base, me_ref, lin_ref, inner_ref, *refs):
    grads_refs = refs[0:2]
    gate_w, up_w, down_w = (ref[0] for ref in refs[2:5])
    out_ref, in_grad_ref, mark_ref = refs[5:8]
    expert = me_ref[0] * 4 + base + pl.program_id(0)
    lane = lax.broadcasted_iota(jnp.int32, (576, 128), 1)
    for part in range(2):
        blocks = slice(part * 4, part * 4 + 4)
        result = nn(inner_ref[blocks].reshape(576, 512), down_w).astype(BF)
        out_ref[blocks] = result.reshape(4, 144, 1024)
        wide = both_parts(grads_refs, part).astype(F32)
        gate_slot = jnp.sum(wide * result.astype(F32), axis=1, keepdims=True)
        mark_ref[blocks] = jnp.where(lane == expert, gate_slot, 0.0).astype(BF).reshape(4, 144, 128)
        lin = lin_ref[blocks].reshape(576, 1024)
        in_grad_ref[blocks] = (
            (nt(lin[:, 0:512], gate_w) + nt(lin[:, 512:1024], up_w))
            .astype(BF)
            .reshape(4, 144, 1024)
        )


def expert_rows(me, base, count, lin, inner, grads, gate_w, up_w, down_w):
    spec = pl.BlockSpec
    wide = [spec((blocks, 144, 1024), lambda e: (0, base + e, 0)) for blocks in (6, 2)]
    tall_w = spec((1, 1024, 512), lambda e: (base + e, 0, 0))
    flat_w = spec((1, 512, 1024), lambda e: (base + e, 0, 0))
    own = lambda width: spec((8, 144, width), lambda e: (0, e, 0))
    return pl.pallas_call(
        functools.partial(expert_rows_kernel, base),
        out_shape=(
            shaped((8, 144 * count, 1024), BF),
            shaped((8, 144 * count, 1024), BF),
            shaped((8, 144 * count, 128), BF),
        ),
        grid=(count,),
        in_specs=[in_smem(), own(1024), own(512)] + wide + [tall_w, tall_w, flat_w],
        out_specs=(own(1024), own(1024), own(128)),
        compiler_params=params(),
        cost_estimate=cost(count * 4e9, count * 14e6),
        name="expert_rows",
    )(me, lin, inner, *grads, gate_w, up_w, down_w)


def combine_kernel(calls, weighted, *refs):
    slot_ref = refs[0]
    refs = refs[1:]
    gate_ref = None
    if weighted:
        gate_ref, refs = refs[0], refs[1:]
    value_refs, refs = refs[:calls], refs[calls:]
    mark_refs = ()
    if not weighted:
        mark_refs, refs = refs[:calls], refs[calls:]
    out_ref = refs[0]
    here = 4 // calls
    slots = slot_ref[0].astype(F32)
    lane = lax.broadcasted_iota(jnp.int32, (512, 144 * here), 1).astype(F32)
    total, marks = None, None
    for call in range(calls):
        hot = jnp.zeros((512, 144 * here), F32)
        for local_expert in range(here):
            number = call * here + local_expert
            slot = slots[:, number : number + 1]
            place = jnp.where(slot < 144.0, slot + 144.0 * local_expert, -1.0)
            put = 1.0
            if weighted:
                put = gate_ref[0][:, number : number + 1].astype(F32)
            hot = jnp.where(lane == place, put, hot)
        hot = hot.astype(BF)
        term = nn(hot, value_refs[call][0])
        total = term if total is None else total + term
        if not weighted:
            mark = nn(hot, mark_refs[call][0])
            marks = mark if marks is None else marks + mark
    out_ref[0, 0:512, :] = total.astype(BF)
    if not weighted:
        lying = marks.T[0:32, :].astype(BF)
        out_ref[0, 512:528, 0:512] = lying[0:16, :]
        out_ref[0, 512:528, 512:1024] = lying[16:32, :]


def combine(parity, slots, gates, values, marks):
    calls = len(values)
    weighted = gates is not None
    rows = 512 if weighted else 528
    column = pl.BlockSpec((1, 512, 128), lambda i: (2 * i + parity, 0, 0))
    wide = pl.BlockSpec((1, 576 // calls, 1024), lambda i: (2 * i + parity, 0, 0))
    slim = pl.BlockSpec((1, 576 // calls, 128), lambda i: (2 * i + parity, 0, 0))
    args = [slots] + ([gates] if weighted else []) + list(values) + list(marks)
    return pl.pallas_call(
        functools.partial(combine_kernel, calls, weighted),
        out_shape=shaped((4, rows, 1024), BF),
        grid=(4,),
        in_specs=[column]
        + ([column] if weighted else [])
        + [wide] * calls
        + [slim] * len(marks),
        out_specs=pl.BlockSpec((1, rows, 1024), lambda i: (i, 0, 0)),
        compiler_params=params(),
        cost_estimate=cost(4 * 2 * 512 * 768 * 1024, 10e6),
        name="combine",
    )(*args)


def back_kernel(
    plan, me_ref, sum_ref, sum_x_ref, sum_y_ref, hidden_ref, cot_ref, payload_ref, gates_ref,
    extra_ref, *refs,
):
    count = len(plan)
    hidden_grad_ref, branch_grad_ref, first_ref, second_ref, small_ref, mats, sems = refs[count:]
    copies = start_fetch_out(me_ref[0], plan, refs[:count], mats, sems)
    total = (
        sum_ref[...].astype(F32) + sum_x_ref[...].astype(F32) + sum_y_ref[...].astype(F32)
    )
    gate_grad = jnp.concatenate([total[512:528, 0:512], total[512:528, 512:1024]], axis=0)
    gates = gates_ref[...]
    logit_grad = (
        gates * (gate_grad - jnp.sum(gates * gate_grad, axis=0, keepdims=True))
    ).astype(BF)
    normed_grad = total[0:512, :] + tn(logit_grad, extra_ref[0:32, :])
    hidden = hidden_ref[...]
    inverse = lax.rsqrt(jnp.mean(hidden * hidden, axis=-1, keepdims=True) + norm_eps)
    scaled = normed_grad * extra_ref[33:34, :].astype(F32)
    spread_out = inverse * inverse * inverse * jnp.mean(hidden * scaled, axis=-1, keepdims=True)
    hidden_grad = cot_ref[...].astype(F32) + inverse * scaled - hidden * spread_out
    hidden_grad_ref[...] = hidden_grad
    small_ref[0:32, :] = nn(logit_grad, payload_ref[0:512, :])
    small_ref[32:40, :] = jnp.broadcast_to(
        jnp.sum(normed_grad * hidden * inverse, axis=0, keepdims=True), (8, 1024)
    )
    branch_grad = (branch_scale * hidden_grad).astype(BF)
    branch_grad_ref[...] = branch_grad
    for copy in copies:
        copy.wait()
    for part in range(4):
        grad = nt(branch_grad, mats[part * 256 : part * 256 + 256, :]).astype(BF)
        first_ref[part] = grad[:, 0:128]
        second_ref[part] = grad[:, 128:256]


def back_to_attention(me, sums, hidden, cotangent, payload, gates, extra, pieces):
    plan = plan_of(128)
    return pl.pallas_call(
        functools.partial(back_kernel, plan),
        out_shape=(
            shaped((512, 1024), F32),
            shaped((512, 1024), BF),
            shaped((4, 512, 128), BF),
            shaped((4, 512, 128), BF),
            shaped((40, 1024), F32),
        ),
        in_specs=[in_smem()] + in_vmem(8) + in_hbm(len(plan)),
        out_specs=tuple(in_vmem(5)),
        scratch_shapes=[pltpu.VMEM((1024, 1024), BF), pltpu.SemaphoreType.DMA((len(plan),))],
        compiler_params=params(),
        cost_estimate=cost(2 * 512 * 1024 * 1024, 12e6),
        name="back_to_attention",
    )(me, *sums, hidden, cotangent, payload, gates, extra, *pieces)


def deal_out(me, big, odd_ref, even_ref):
    for pair in range(4):
        for target, partner in ((even_ref, 2 * pair), (odd_ref, 2 * pair + 1)):
            start = pl.multiple_of((me ^ partner) * 128, 128)
            target[pair] = big[pl.ds(start, 128), :]


def out_grad_kernel(me_ref, first_ref, second_ref, branch_grad_ref, small_ref, odd_ref, even_ref, big):
    branch_grad = branch_grad_ref[...]
    for part in range(4):
        both = jnp.concatenate([first_ref[part], second_ref[part]], axis=1)
        big[part * 256 : part * 256 + 256, 0:1024] = tn(both, branch_grad).astype(BF)
    small = jnp.concatenate([small_ref[...], jnp.zeros((88, 1024), F32)], axis=0)
    big[:, 1024:1152] = small.T.astype(BF)
    deal_out(me_ref[0], big, odd_ref, even_ref)


def out_grads_of(me, attended, branch_grad, small):
    return pl.pallas_call(
        out_grad_kernel,
        out_shape=(shaped((4, 128, 1152), BF), shaped((4, 128, 1152), BF)),
        in_specs=[in_smem()] + in_vmem(4),
        out_specs=tuple(in_vmem(2)),
        scratch_shapes=[pltpu.VMEM((1024, 1152), BF)],
        compiler_params=params(),
        cost_estimate=cost(2 * 512 * 1024 * 1024, 5e6),
        name="out_grads",
    )(me, *attended, branch_grad, small)


def input_kernel(
    plan, me_ref, tokens_ref, cos_ref, sin_ref, first_ref, second_ref, extra_ref,
    hidden_grad_ref, *refs,
):
    count = len(plan)
    input_grad_ref, odd_ref, even_ref, mats, big, lin, sems = refs[count:]
    me = me_ref[0]
    copies = start_fetch(me, plan, refs[:count], mats, 128, sems)
    stream = tokens_ref[...].astype(F32)
    inverse = lax.rsqrt(jnp.mean(stream * stream, axis=-1, keepdims=True) + norm_eps)
    gain = extra_ref[32:33, :].astype(F32)
    normed = (stream * inverse * gain).astype(BF)
    cosine, sine = cos_ref[...], -sin_ref[...]
    for part in range(4):
        tiles = []
        for group, source in enumerate((first_ref, second_ref)):
            lin[:, part * 256 + group * 128 : part * 256 + group * 128 + 128] = turn(
                source[part, :, 0:128].astype(F32), cosine, sine
            ).astype(BF)
            tiles.append(source[part, :, 128:256].astype(F32))
        lane = lax.broadcasted_iota(jnp.int32, tiles[0].shape, 1)
        key = jnp.where(lane < HD, tiles[0], pltpu.roll(tiles[1], HD, 1))
        value = jnp.where(lane < HD, pltpu.roll(tiles[0], HD, 1), tiles[1])
        lin[:, 1024 + part * 128 : 1152 + part * 128] = turn(key, cosine, sine).astype(BF)
        lin[:, 1536 + part * 128 : 1664 + part * 128] = value.astype(BF)
    normed_t = normed.astype(F32).T.astype(BF)
    for first in range(0, 2048, 512):
        big[:, first : first + 512] = nn(normed_t, lin[:, first : first + 512]).astype(BF)
    for copy in copies:
        copy.wait()
    normed_grad = nt(lin[...], mats[:, 0:2048])
    row = jnp.sum(normed_grad * stream * inverse, axis=0, keepdims=True)
    big[:, 2048:2176] = jnp.broadcast_to(row, (128, 1024)).T.astype(BF)
    deal_out(me, big, odd_ref, even_ref)
    scaled = normed_grad * gain
    spread_out = inverse * inverse * inverse * jnp.mean(stream * scaled, axis=-1, keepdims=True)
    input_grad_ref[...] = (
        hidden_grad_ref[...] + inverse * scaled - stream * spread_out
    ).astype(BF)


def input_grads(me, tokens, cosine, sine, query_grad, pair_grad, extra, hidden_grad, pieces):
    plan = plan_of(128)
    return pl.pallas_call(
        functools.partial(input_kernel, plan),
        out_shape=(
            shaped((512, 1024), BF),
            shaped((4, 128, 2176), BF),
            shaped((4, 128, 2176), BF),
        ),
        in_specs=[in_smem()] + in_vmem(7) + in_hbm(len(plan)),
        out_specs=tuple(in_vmem(3)),
        scratch_shapes=[
            pltpu.VMEM((1024, 2176), BF),
            pltpu.VMEM((1024, 2176), BF),
            pltpu.VMEM((512, 2048), BF),
            pltpu.SemaphoreType.DMA((len(plan),)),
        ],
        compiler_params=params(),
        cost_estimate=cost(4 * 512 * 1024 * 2048, 15e6),
        name="input_grads",
    )(me, tokens, cosine, sine, query_grad, pair_grad, extra, hidden_grad, *pieces)


def dense_slots(routes, ranks, experts):
    mine = routes[None, :, :] == jnp.arange(experts, dtype=jnp.int32)[:, None, None]
    far = jnp.int32(1 << 20)
    rank = jnp.min(jnp.where(mine, ranks[None, :, :], far), axis=-1)
    slot = jnp.sum((rank[:, None, :] < rank[:, :, None]).astype(jnp.int32), axis=-1)
    routed = rank < far
    return (jnp.where(routed & (slot < 144), slot, 255).astype(BF), routed.astype(F32))


def across(values):
    return lax.all_to_all(values, "sp", split_axis=0, concat_axis=0, tiled=True)


def sum_shared(value):
    rows, columns = value.shape
    quarters = across(value).reshape(4, rows // 4, columns).astype(F32)
    quarter = jnp.sum(quarters, axis=0).astype(BF)
    return across(jnp.tile(quarter, (4, 1)))


def fast_local(
    tokens, documents, expert_routes, drop_rank, norm1_gain, query_weight, key_weight,
    value_weight, out_weight, norm2_gain, router_weight, gate_weight, up_weight, down_weight,
    output_grad,
):
    fsdp = lax.axis_index("fsdp")
    seq = lax.axis_index("sp")
    me = jnp.reshape(fsdp, (1,)).astype(jnp.int32)
    small = jnp.concatenate(
        [
            router_weight,
            norm1_gain[:, None],
            norm2_gain[:, None],
            jnp.zeros((128, 94), BF),
        ],
        axis=1,
    )
    shard = jnp.concatenate(
        [query_weight, key_weight, value_weight, small, out_weight], axis=1
    )
    project_pieces = spread(shard)

    slots, routed = dense_slots(expert_routes, drop_rank, 32)
    mixture_grad = (branch_scale * output_grad.astype(F32)).astype(BF)
    grad_payload = jnp.concatenate(
        [mixture_grad, jnp.concatenate([slots[:16], slots[16:]], axis=1)], axis=0
    )

    block_start = fsdp * 2048
    position_all = doc_position(documents)
    position_span = lax.dynamic_slice_in_dim(position_all, block_start, 2048)
    position = lax.dynamic_slice_in_dim(position_span, seq * 512, 512)
    cosine, sine_table = rope_tables(position, HD)
    cosine = jnp.tile(cosine, (1, 2))
    signs = jnp.where(jnp.arange(128) % HD < HD // 2, -1.0, 1.0).astype(F32)
    sine = jnp.tile(sine_table, (1, 2)) * signs[None, :]
    start = HALO + jnp.arange(2048, dtype=jnp.int32) - position_span
    start_rows = start.reshape(2048 // QB, 1, QB)
    low_block = start_rows[:, 0, 0] // KB
    low_back = start_rows[:, 0, 0] // BACK_KB

    first, second, extra = project(me, tokens, cosine, sine, project_pieces)
    grad_payload = hold(grad_payload, project_pieces[6], project_pieces[7])
    own, beside = grad_payload, flip(grad_payload, 1)
    along_x, along_y = flip(grad_payload, 2), flip(grad_payload, 4)
    heads = [across(first.reshape(2048, 256)), None]
    heads[0], second, beside, along_x, along_y = lax.optimization_barrier(
        (heads[0], second, beside, along_x, along_y)
    )
    heads[1] = across(second.reshape(2048, 256))
    halos = [from_behind(heads[0][:, 128:256], "fsdp", 1), None]
    near_pieces = (own, beside, along_x, flip(along_x, 1), along_y, flip(along_y, 1))
    blended, logs = [None, None], [None, None]
    blended[0], logs[0] = attend(low_block, heads[0], halos[0], start_rows)
    blended[0], heads[1] = lax.optimization_barrier((blended[0], heads[1]))
    halos[1] = from_behind(heads[1][:, 128:256], "fsdp", 1)
    first_back = across(blended[0])
    near, far = (0, 1, 2, 3, 4, 5), (6, 7)
    near_grads = pick_grads(me, near, near_pieces)
    halos[1], near_grads = lax.optimization_barrier((halos[1], near_grads))
    diagonal = spread_diagonal(near_pieces)
    blended[1], logs[1] = attend(low_block, heads[1], halos[1], start_rows)
    blended[1], first_back, diagonal = lax.optimization_barrier(
        (blended[1], first_back, diagonal)
    )
    attended = [first_back, across(blended[1])]
    far_grads = pick_grads(me, far, spread_far(diagonal))
    all_slot_columns = jnp.concatenate([near_grads[2], far_grads[2]], axis=0)
    attended, near_grads, far_grads, all_slot_columns = lax.optimization_barrier(
        (attended, near_grads, far_grads, all_slot_columns)
    )
    attended = [part.reshape(4, 512, 128) for part in attended]
    grad_rows, slot_rows, _ = zip(near_grads, far_grads)
    hidden_one, payload, gates = after_attention(
        me, tokens, attended, extra, routed, project_pieces
    )
    near_pieces = spread_near(payload)
    diagonal = spread_diagonal(near_pieces)
    near_rows = pick_rows(me, slot_rows[0], near, near_pieces)
    near_rows, diagonal = lax.optimization_barrier((near_rows, diagonal))
    far_rows = pick_rows(me, slot_rows[1], far, spread_far(diagonal))
    rows, slot_gates, gate_columns = zip(near_rows, far_rows)
    mats = (gate_weight, up_weight, down_weight)
    lin_grads, inners, parts = zip(
        *[expert_grads(base, 2, rows, grad_rows, slot_gates, *mats) for base in (0, 2)]
    )
    sums_of_parts = lax.psum(parts, "sp")

    def finish(turn_number, _):
        here, slot_columns = hold((me, all_slot_columns), turn_number)
        outs, in_grads, marks = zip(
            *[
                expert_rows(here, 2 * pair, 2, lin_grads[pair], inners[pair], grad_rows, *mats)
                for pair in range(2)
            ]
        )
        odd = combine(1, slot_columns, None, in_grads, marks)
        even = combine(0, slot_columns, None, in_grads, marks)
        sums = collect(odd, even)
        hidden_grad, branch_grad, first_grad, second_grad, small_grads = back_to_attention(
            me, sums, hidden_one, output_grad, payload, gates, extra, project_pieces
        )
        first_heads = across(first_grad.reshape(2048, 128))
        first_heads, second_grad = lax.optimization_barrier((first_heads, second_grad))
        second_heads = across(second_grad.reshape(2048, 128))
        first_own, first_halo = attend_back(
            low_back, heads[0], halos[0], start_rows, blended[0], first_heads, logs[0]
        )
        first_own, first_halo, second_heads = lax.optimization_barrier(
            (first_own, first_halo, second_heads)
        )
        held_outs, held_gates = hold((outs, gate_columns), first_heads)
        held_gates = jnp.concatenate(held_gates, axis=0)
        odd_mix = combine(1, slot_columns, held_gates, held_outs, ())
        even_mix = combine(0, slot_columns, held_gates, held_outs, ())
        mixture = collect(odd_mix, even_mix)
        output = (
            hidden_one
            + branch_scale
            * (mixture[0].astype(F32) + mixture[1].astype(F32) + mixture[2].astype(F32))
        ).astype(BF)
        out_sums = collect(*out_grads_of(me, attended, branch_grad, small_grads))

        def grads_home(own_grad, halo_grad):
            returned = from_behind(halo_grad, "fsdp", -1).astype(F32)
            own_grad = own_grad + jnp.pad(returned, ((0, 0), (128, 0)))
            return across(own_grad.astype(BF)).reshape(4, 512, 256)

        first_home = grads_home(first_own, first_halo)
        second_own, second_halo = attend_back(
            low_back, heads[1], halos[1], start_rows, blended[1], second_heads, logs[1]
        )
        second_own, second_halo, first_home = lax.optimization_barrier(
            (second_own, second_halo, first_home)
        )
        second_home = grads_home(second_own, second_halo)
        input_grad, odd_in, even_in = input_grads(
            me, tokens, cosine, sine, first_home, second_home, extra, hidden_grad, project_pieces
        )
        in_sums = collect(odd_in, even_in)

        out_shard = sum(term.astype(F32) for term in out_sums).astype(BF)
        in_shard = sum(term.astype(F32) for term in in_sums).astype(BF)
        shards = sum_shared(jnp.concatenate([in_shard, out_shard], axis=1))
        return (output, input_grad, shards)

    rounds = 1 + (documents[0] > 0).astype(jnp.int32)
    output, input_grad, shards = lax.fori_loop(
        0,
        rounds,
        finish,
        (
            jnp.zeros((512, 1024), BF),
            jnp.zeros((512, 1024), BF),
            jnp.zeros((128, 3328), BF),
        ),
    )
    in_shard, out_shard = shards[:, 0:2176], shards[:, 2176:3328]
    sums_of_parts = [
        total[first : first + 3072] for total in sums_of_parts for first in (0, 3072)
    ]
    stacked = [
        jnp.stack([total[0:1024] for total in sums_of_parts]).astype(F32),
        jnp.stack([total[1024:2048] for total in sums_of_parts]).astype(F32),
        jnp.stack(
            [
                jnp.concatenate([total[2048:2560], total[2560:3072]], axis=1)
                for total in sums_of_parts
            ]
        ).astype(F32),
    ]
    return (
        output,
        input_grad,
        in_shard[:, 2048].astype(F32),
        in_shard[:, 0:1024].astype(F32),
        in_shard[:, 1024:1536].astype(F32),
        in_shard[:, 1536:2048].astype(F32),
        out_shard[:, 0:1024].astype(F32),
        out_shard[:, 1056].astype(F32),
        out_shard[:, 1024:1056].astype(F32),
        *stacked,
    )


def solution(mesh):
    placed = (
        P(("fsdp", "sp"), None),
        P(),
        P(("fsdp", "sp"), None),
        P(("fsdp", "sp"), None),
        P("fsdp"),
        P("fsdp", None),
        P("fsdp", None),
        P("fsdp", None),
        P("fsdp", None),
        P("fsdp"),
        P("fsdp", None),
        P("fsdp", None, None),
        P("fsdp", None, None),
        P("fsdp", None, None),
        P(("fsdp", "sp"), None),
    )
    fast = mesh.shape["sp"] == 4 and mesh.shape["fsdp"] == 8
    return jax.shard_map(
        fast_local if fast else local,
        mesh=mesh,
        in_specs=placed,
        out_specs=(
            P(("fsdp", "sp"), None),
            P(("fsdp", "sp"), None),
            P("fsdp"),
            P("fsdp", None),
            P("fsdp", None),
            P("fsdp", None),
            P("fsdp", None),
            P("fsdp"),
            P("fsdp", None),
            P("fsdp", None, None),
            P("fsdp", None, None),
            P("fsdp", None, None),
        ),
        check_vma=False,
    )
```

```python
import functools

import jax
import jax.numpy as jnp
from jax import lax
from jax.sharding import PartitionSpec as P
from jax.experimental import pallas as pl
from jax.experimental.pallas import tpu as pltpu

HD = 64
DOC_CAP = 2048


attend_scale = 0.015625
branch_scale = 0.22
norm_eps = 1e-06
rope_base = 10000.0
masked_score = -1e30


def from_behind(value, axis, steps):
    count = lax.axis_size(axis)
    initial, last = (max(0, -steps), min(count, count - steps))
    return lax.ppermute(value, axis, [(source, source + steps) for source in range(initial, last)])


def doc_position(documents):
    length = documents.shape[0]
    place = jnp.arange(length, dtype=jnp.int32)
    fresh = jnp.concatenate([jnp.ones((1,), dtype=bool), documents[1:] != documents[:-1]])
    opening = lax.cummax(jnp.where(fresh, place, 0), axis=0)
    return place - opening


def rope_tables(position, head_size):
    half_size = head_size // 2
    spacing = jnp.arange(half_size, dtype=jnp.float32)
    inverse = rope_base ** (-2.0 * spacing / head_size)
    angle = position.astype(jnp.float32)[:, None] * inverse[None, :]
    return (jnp.tile(jnp.cos(angle), (1, 2)), jnp.tile(jnp.sin(angle), (1, 2)))


def rotate(values, cosine, sine_table):
    half_size = values.shape[-1] // 2
    turned = jnp.concatenate([-values[..., half_size:], values[..., :half_size]], axis=-1)
    return values * cosine[:, None, :] + turned * sine_table[:, None, :]


def route_slots(routes, rank_table, experts, capacity):
    flat_routes = routes.reshape(-1)
    flat_ranks = rank_table.reshape(-1)
    ordered = flat_routes[jnp.argsort(flat_ranks)]
    onehot = (ordered[:, None] == jnp.arange(experts, dtype=jnp.int32)[None, :]).astype(jnp.int32)
    earlier = jnp.cumsum(onehot, axis=0) - onehot
    slot_sorted = jnp.sum(earlier * onehot, axis=1)
    slot_number = slot_sorted[flat_ranks].reshape(routes.shape)
    kept_pair = slot_number < capacity
    return (jnp.where(kept_pair, routes * capacity + slot_number, -1), kept_pair)


def to_owner(values):
    return lax.all_to_all(values, "fsdp", split_axis=0, concat_axis=1, tiled=True)


def from_owner(values):
    return lax.all_to_all(values, "fsdp", split_axis=1, concat_axis=0, tiled=True)


def expert_forward(slot_rows, gate_mats, up_mats, down_mats):
    gate_lin = jnp.einsum("nrd,ndf->nrf", slot_rows, gate_mats, preferred_element_type=jnp.float32)
    up_lin = jnp.einsum("nrd,ndf->nrf", slot_rows, up_mats, preferred_element_type=jnp.float32)
    inner = (gate_lin * jax.nn.sigmoid(gate_lin) * up_lin).astype(jnp.bfloat16)
    result = jnp.einsum(
        "nrf,nfd->nrd", inner, down_mats, preferred_element_type=jnp.float32
    ).astype(jnp.bfloat16)
    return (gate_lin, up_lin, result)


def expert_backward(slot_rows, gate_lin, up_lin, result_grad, gate_mats, up_mats, down_mats):
    sigma = jax.nn.sigmoid(gate_lin)
    swished = gate_lin * sigma
    inner = (swished * up_lin).astype(jnp.bfloat16)
    inner_grad = jnp.einsum(
        "nrd,nfd->nrf", result_grad, down_mats, preferred_element_type=jnp.float32
    )
    gate_grad = (inner_grad * up_lin * sigma * (1.0 + gate_lin * (1.0 - sigma))).astype(
        jnp.bfloat16
    )
    up_grad = (inner_grad * swished).astype(jnp.bfloat16)
    rows_grad = jnp.einsum("nrf,ndf->nrd", gate_grad, gate_mats, preferred_element_type=jnp.float32)
    rows_grad = (
        rows_grad + jnp.einsum("nrf,ndf->nrd", up_grad, up_mats, preferred_element_type=jnp.float32)
    ).astype(jnp.bfloat16)
    gate_part = jnp.einsum("nrd,nrf->ndf", slot_rows, gate_grad, preferred_element_type=jnp.float32)
    up_part = jnp.einsum("nrd,nrf->ndf", slot_rows, up_grad, preferred_element_type=jnp.float32)
    down_part = jnp.einsum("nrf,nrd->nfd", inner, result_grad, preferred_element_type=jnp.float32)
    return (rows_grad, gate_part, up_part, down_part)


def local(
    tokens,
    documents,
    expert_routes,
    drop_rank,
    norm1_gain,
    query_weight,
    key_weight,
    value_weight,
    out_weight,
    norm2_gain,
    router_weight,
    gate_weight,
    up_weight,
    down_weight,
    output_grad,
):
    rows_dev, model_width = tokens.shape
    heads_query = query_weight.shape[1] // HD
    heads_kv = key_weight.shape[1] // HD
    repeat = heads_query // heads_kv
    experts = router_weight.shape[1]
    top_count = expert_routes.shape[1]
    seq_parts = lax.axis_size("sp")
    span_rows = seq_parts * rows_dev
    query_block = min(512, span_rows)
    block_count = span_rows // query_block
    doc_most = min(DOC_CAP, span_rows)
    window = doc_most + query_block
    capacity = (9 * rows_dev * top_count + 8 * experts - 1) // (8 * experts)
    slot_total = experts * capacity
    block_start = lax.axis_index("fsdp") * span_rows
    row_start = block_start + lax.axis_index("sp") * rows_dev
    position = lax.dynamic_slice_in_dim(doc_position(documents), row_start, rows_dev)
    cosine, sine_table = rope_tables(position, HD)
    gain_first, query_mat, key_mat, value_mat, out_mat, gain_second, router_mat = (
        lax.all_gather(norm1_gain, "fsdp", axis=0, tiled=True),
        lax.all_gather(query_weight, "fsdp", axis=0, tiled=True),
        lax.all_gather(key_weight, "fsdp", axis=0, tiled=True),
        lax.all_gather(value_weight, "fsdp", axis=0, tiled=True),
        lax.all_gather(out_weight, "fsdp", axis=0, tiled=True),
        lax.all_gather(norm2_gain, "fsdp", axis=0, tiled=True),
        lax.all_gather(router_weight, "fsdp", axis=0, tiled=True),
    )
    stream = tokens.astype(jnp.float32)
    inverse_one = lax.rsqrt(jnp.mean(stream * stream, axis=-1, keepdims=True) + norm_eps)
    gain_one = gain_first.astype(jnp.float32)
    normed_one = (stream * inverse_one * gain_one).astype(jnp.bfloat16)
    query_lin = jnp.dot(normed_one, query_mat, preferred_element_type=jnp.float32).reshape(
        rows_dev, heads_query, HD
    )
    key_lin = jnp.dot(normed_one, key_mat, preferred_element_type=jnp.float32).reshape(
        rows_dev, heads_kv, HD
    )
    value_low = (
        jnp.dot(normed_one, value_mat, preferred_element_type=jnp.float32)
        .astype(jnp.bfloat16)
        .reshape(rows_dev, heads_kv, HD)
    )
    query_low = (
        rotate(query_lin, cosine, sine_table)
        .astype(jnp.bfloat16)
        .reshape(rows_dev, heads_kv, repeat * HD)
    )
    key_low = rotate(key_lin, cosine, sine_table).astype(jnp.bfloat16)
    packed = jnp.concatenate([query_low, key_low, value_low], axis=-1)
    by_heads = lax.all_to_all(packed, "sp", split_axis=1, concat_axis=0, tiled=True)
    groups = by_heads.shape[1]
    query_heads = by_heads[:, :, : repeat * HD]
    pair_heads = by_heads[:, :, repeat * HD :]
    halo_rows = from_behind(pair_heads[span_rows - doc_most :], "fsdp", 1)
    near_pairs = jnp.concatenate([halo_rows, pair_heads], axis=0)
    query_docs = lax.dynamic_slice_in_dim(documents, block_start, span_rows)
    near_docs = lax.dynamic_slice_in_dim(
        jnp.concatenate([jnp.full((doc_most,), -1, jnp.int32), documents]),
        block_start,
        doc_most + span_rows,
    )
    causal = jnp.arange(window)[None, :] <= jnp.arange(query_block)[:, None] + doc_most

    def block_scores(block_index):
        first_row = block_index * query_block
        query_part = lax.dynamic_slice_in_dim(query_heads, first_row, query_block).reshape(
            query_block, groups, repeat, HD
        )
        pair_part = lax.dynamic_slice_in_dim(near_pairs, first_row, window)
        key_part = pair_part[:, :, :HD]
        value_part = pair_part[:, :, HD:]
        own_docs = lax.dynamic_slice_in_dim(query_docs, first_row, query_block)
        seen_docs = lax.dynamic_slice_in_dim(near_docs, first_row, window)
        allowed = (seen_docs[None, :] == own_docs[:, None]) & causal
        scores = attend_scale * jnp.einsum(
            "rgjd,cgd->gjrc", query_part, key_part, preferred_element_type=jnp.float32
        )
        return (query_part, key_part, value_part, jnp.where(allowed, scores, masked_score))

    def attend_block(block_index):
        query_part, key_part, value_part, scores = block_scores(block_index)
        row_max = jnp.max(scores, axis=-1, keepdims=True)
        exponent = jnp.exp(scores - row_max)
        row_total = jnp.sum(exponent, axis=-1, keepdims=True)
        softmaxed = (exponent / row_total).astype(jnp.bfloat16)
        blended = jnp.einsum(
            "gjrc,cgd->rgjd", softmaxed, value_part, preferred_element_type=jnp.float32
        )
        return (
            blended.astype(jnp.bfloat16).reshape(query_block, groups, repeat * HD),
            (row_max + jnp.log(row_total))[..., 0],
        )

    blended_all, log_totals = lax.map(attend_block, jnp.arange(block_count, dtype=jnp.int32))
    attended = lax.all_to_all(
        blended_all.reshape(span_rows, groups, repeat * HD),
        "sp",
        split_axis=0,
        concat_axis=1,
        tiled=True,
    ).reshape(rows_dev, heads_query * HD)
    branch = jnp.dot(attended, out_mat, preferred_element_type=jnp.float32)
    hidden_one = stream + branch_scale * branch
    inverse_two = lax.rsqrt(jnp.mean(hidden_one * hidden_one, axis=-1, keepdims=True) + norm_eps)
    gain_two = gain_second.astype(jnp.float32)
    normed_two = (hidden_one * inverse_two * gain_two).astype(jnp.bfloat16)
    logits = jnp.dot(normed_two, router_mat, preferred_element_type=jnp.float32)
    route_hot = expert_routes[:, :, None] == jnp.arange(experts, dtype=jnp.int32)[None, None, :]
    chosen = jnp.sum(jnp.where(route_hot, logits[:, None, :], 0.0), axis=-1)
    chosen_max = jnp.max(chosen, axis=-1, keepdims=True)
    gate_exp = jnp.exp(chosen - chosen_max)
    gates = gate_exp / jnp.sum(gate_exp, axis=-1, keepdims=True)
    gate_low = gates.astype(jnp.bfloat16)
    slot_index, kept_pair = route_slots(expert_routes, drop_rank, experts, capacity)
    columns = jnp.arange(slot_total, dtype=jnp.int32)[None, :]
    dispatch = jnp.zeros((rows_dev, slot_total), dtype=bool)
    combine = jnp.zeros((rows_dev, slot_total), dtype=jnp.bfloat16)
    for route_slot in range(top_count):
        landing = slot_index[:, route_slot : route_slot + 1] == columns
        dispatch = dispatch | landing
        combine = combine + jnp.where(
            landing, gate_low[:, route_slot : route_slot + 1], jnp.zeros((), jnp.bfloat16)
        )
    dispatch_low = dispatch.astype(jnp.bfloat16)
    expert_in = (
        jnp.einsum("tc,td->cd", dispatch_low, normed_two, preferred_element_type=jnp.float32)
        .astype(jnp.bfloat16)
        .reshape(experts, capacity, model_width)
    )
    owned_in = to_owner(expert_in)
    gate_lin, up_lin, owned_out = expert_forward(owned_in, gate_weight, up_weight, down_weight)
    expert_out = from_owner(owned_out)
    mixture = jnp.dot(
        combine, expert_out.reshape(slot_total, model_width), preferred_element_type=jnp.float32
    )
    output = (hidden_one + branch_scale * mixture).astype(jnp.bfloat16)
    cotangent = output_grad.astype(jnp.float32)
    mixture_grad = (branch_scale * cotangent).astype(jnp.bfloat16)
    out_grad = (
        jnp.einsum("tc,td->cd", combine, mixture_grad, preferred_element_type=jnp.float32)
        .astype(jnp.bfloat16)
        .reshape(experts, capacity, model_width)
    )
    taken = jnp.take(
        expert_out.reshape(slot_total, model_width), jnp.clip(slot_index, 0, slot_total - 1), axis=0
    )
    gate_grad = jnp.where(
        kept_pair,
        jnp.einsum("tkd,td->tk", taken, mixture_grad, preferred_element_type=jnp.float32),
        0.0,
    )
    chosen_grad = gates * (gate_grad - jnp.sum(gates * gate_grad, axis=-1, keepdims=True))
    logit_grad = jnp.sum(jnp.where(route_hot, chosen_grad[:, :, None], 0.0), axis=1).astype(
        jnp.bfloat16
    )
    router_grad = jnp.einsum(
        "td,te->de", normed_two, logit_grad, preferred_element_type=jnp.float32
    )
    normed_two_grad = jnp.einsum(
        "te,de->td", logit_grad, router_mat, preferred_element_type=jnp.float32
    )
    owned_grad = to_owner(out_grad)
    owned_in_grad, expert_gate_grad, expert_up_grad, expert_down_grad = expert_backward(
        owned_in, gate_lin, up_lin, owned_grad, gate_weight, up_weight, down_weight
    )
    expert_in_grad = from_owner(owned_in_grad)
    normed_two_grad = normed_two_grad + jnp.dot(
        dispatch_low,
        expert_in_grad.reshape(slot_total, model_width),
        preferred_element_type=jnp.float32,
    )
    scaled_two = normed_two_grad * gain_two
    hidden_grad = (
        cotangent
        + inverse_two * scaled_two
        - hidden_one * inverse_two**3 * jnp.mean(hidden_one * scaled_two, axis=-1, keepdims=True)
    )
    norm_two_grad = jnp.sum(normed_two_grad * hidden_one * inverse_two, axis=0)
    branch_grad = (branch_scale * hidden_grad).astype(jnp.bfloat16)
    out_mat_grad = jnp.einsum(
        "tk,td->kd", attended, branch_grad, preferred_element_type=jnp.float32
    )
    attended_grad = jnp.einsum(
        "td,kd->tk", branch_grad, out_mat, preferred_element_type=jnp.float32
    ).astype(jnp.bfloat16)
    grad_heads = lax.all_to_all(
        attended_grad.reshape(rows_dev, heads_kv, repeat * HD),
        "sp",
        split_axis=1,
        concat_axis=0,
        tiled=True,
    )

    def attend_back(accumulated, block_item):
        block_index, log_total = block_item
        query_part, key_part, value_part, scores = block_scores(block_index)
        first_row = block_index * query_block
        softmaxed = jnp.exp(scores - log_total[..., None])
        incoming = lax.dynamic_slice_in_dim(grad_heads, first_row, query_block).reshape(
            query_block, groups, repeat, HD
        )
        softmax_grad = jnp.einsum(
            "rgjd,cgd->gjrc", incoming, value_part, preferred_element_type=jnp.float32
        )
        centred = jnp.sum(softmaxed * softmax_grad, axis=-1, keepdims=True)
        score_grad = (softmaxed * (softmax_grad - centred)).astype(jnp.bfloat16)
        query_grad = attend_scale * jnp.einsum(
            "gjrc,cgd->rgjd", score_grad, key_part, preferred_element_type=jnp.float32
        )
        key_grad = attend_scale * jnp.einsum(
            "gjrc,rgjd->cgd", score_grad, query_part, preferred_element_type=jnp.float32
        )
        value_grad = jnp.einsum(
            "gjrc,rgjd->cgd",
            softmaxed.astype(jnp.bfloat16),
            incoming,
            preferred_element_type=jnp.float32,
        )
        current = lax.dynamic_slice_in_dim(accumulated, first_row, window)
        updated = lax.dynamic_update_slice_in_dim(
            accumulated, current + jnp.concatenate([key_grad, value_grad], axis=-1), first_row, 0
        )
        return (updated, query_grad.reshape(query_block, groups, repeat * HD))

    pair_grad, query_grads = lax.scan(
        attend_back,
        jnp.zeros((doc_most + span_rows, groups, 2 * HD), jnp.float32),
        (jnp.arange(block_count, dtype=jnp.int32), log_totals),
    )
    returned = from_behind(pair_grad[:doc_most].astype(jnp.bfloat16), "fsdp", -1).astype(
        jnp.float32
    )
    own_grad = pair_grad[doc_most:]
    own_grad = jnp.concatenate(
        [own_grad[: span_rows - doc_most], own_grad[span_rows - doc_most :] + returned], axis=0
    )
    packed_grad = jnp.concatenate(
        [
            query_grads.reshape(span_rows, groups, repeat * HD).astype(jnp.bfloat16),
            own_grad.astype(jnp.bfloat16),
        ],
        axis=-1,
    )
    by_tokens = lax.all_to_all(packed_grad, "sp", split_axis=0, concat_axis=1, tiled=True)
    query_rot_grad = (
        by_tokens[:, :, : repeat * HD].astype(jnp.float32).reshape(rows_dev, heads_query, HD)
    )
    key_rot_grad = by_tokens[:, :, repeat * HD : (repeat + 1) * HD].astype(jnp.float32)
    value_grad_low = by_tokens[:, :, (repeat + 1) * HD :].reshape(rows_dev, heads_kv * HD)
    query_lin_grad = (
        rotate(query_rot_grad, cosine, -sine_table)
        .astype(jnp.bfloat16)
        .reshape(rows_dev, heads_query * HD)
    )
    key_lin_grad = (
        rotate(key_rot_grad, cosine, -sine_table)
        .astype(jnp.bfloat16)
        .reshape(rows_dev, heads_kv * HD)
    )
    query_mat_grad = jnp.einsum(
        "td,tk->dk", normed_one, query_lin_grad, preferred_element_type=jnp.float32
    )
    key_mat_grad = jnp.einsum(
        "td,tk->dk", normed_one, key_lin_grad, preferred_element_type=jnp.float32
    )
    value_mat_grad = jnp.einsum(
        "td,tk->dk", normed_one, value_grad_low, preferred_element_type=jnp.float32
    )
    normed_one_grad = jnp.einsum(
        "tk,dk->td", query_lin_grad, query_mat, preferred_element_type=jnp.float32
    )
    normed_one_grad = normed_one_grad + jnp.einsum(
        "tk,dk->td", key_lin_grad, key_mat, preferred_element_type=jnp.float32
    )
    normed_one_grad = normed_one_grad + jnp.einsum(
        "tk,dk->td", value_grad_low, value_mat, preferred_element_type=jnp.float32
    )
    scaled_one = normed_one_grad * gain_one
    input_grad = (
        hidden_grad
        + inverse_one * scaled_one
        - stream * inverse_one**3 * jnp.mean(stream * scaled_one, axis=-1, keepdims=True)
    ).astype(jnp.bfloat16)
    norm_one_grad = jnp.sum(normed_one_grad * stream * inverse_one, axis=0)
    shard_norm_one, shard_query, shard_key, shard_value, shard_out, shard_norm_two, shard_router = (
        lax.psum_scatter(
            norm_one_grad.astype(jnp.bfloat16), "fsdp", scatter_dimension=0, tiled=True
        ).astype(jnp.float32),
        lax.psum_scatter(
            query_mat_grad.astype(jnp.bfloat16), "fsdp", scatter_dimension=0, tiled=True
        ).astype(jnp.float32),
        lax.psum_scatter(
            key_mat_grad.astype(jnp.bfloat16), "fsdp", scatter_dimension=0, tiled=True
        ).astype(jnp.float32),
        lax.psum_scatter(
            value_mat_grad.astype(jnp.bfloat16), "fsdp", scatter_dimension=0, tiled=True
        ).astype(jnp.float32),
        lax.psum_scatter(
            out_mat_grad.astype(jnp.bfloat16), "fsdp", scatter_dimension=0, tiled=True
        ).astype(jnp.float32),
        lax.psum_scatter(
            norm_two_grad.astype(jnp.bfloat16), "fsdp", scatter_dimension=0, tiled=True
        ).astype(jnp.float32),
        lax.psum_scatter(
            router_grad.astype(jnp.bfloat16), "fsdp", scatter_dimension=0, tiled=True
        ).astype(jnp.float32),
    )
    (
        summed_norm_one,
        summed_query,
        summed_key,
        summed_value,
        summed_out,
        summed_norm_two,
        summed_router,
        summed_gate,
        summed_up,
        summed_down,
    ) = (
        lax.psum(shard_norm_one.astype(jnp.bfloat16), "sp").astype(jnp.float32),
        lax.psum(shard_query.astype(jnp.bfloat16), "sp").astype(jnp.float32),
        lax.psum(shard_key.astype(jnp.bfloat16), "sp").astype(jnp.float32),
        lax.psum(shard_value.astype(jnp.bfloat16), "sp").astype(jnp.float32),
        lax.psum(shard_out.astype(jnp.bfloat16), "sp").astype(jnp.float32),
        lax.psum(shard_norm_two.astype(jnp.bfloat16), "sp").astype(jnp.float32),
        lax.psum(shard_router.astype(jnp.bfloat16), "sp").astype(jnp.float32),
        lax.psum(expert_gate_grad.astype(jnp.bfloat16), "sp").astype(jnp.float32),
        lax.psum(expert_up_grad.astype(jnp.bfloat16), "sp").astype(jnp.float32),
        lax.psum(expert_down_grad.astype(jnp.bfloat16), "sp").astype(jnp.float32),
    )
    return (
        output,
        input_grad,
        summed_norm_one,
        summed_query,
        summed_key,
        summed_value,
        summed_out,
        summed_norm_two,
        summed_router,
        summed_gate,
        summed_up,
        summed_down,
    )


BF = jnp.bfloat16
F32 = jnp.float32
LOG2E = 1.4426950408889634
QB = 512
KB = 512
BACK_KB = 256
HALO = 2048
VMEM_MOST = 60 * 1024 * 1024


def in_vmem(count):
    return [pl.BlockSpec(memory_space=pltpu.VMEM)] * count


def in_hbm(count):
    return [pl.BlockSpec(memory_space=pl.ANY)] * count


def in_smem():
    return pl.BlockSpec(memory_space=pltpu.SMEM)


def shaped(shape, kind):
    return jax.ShapeDtypeStruct(shape, kind)


def params():
    return pltpu.CompilerParams(vmem_limit_bytes=VMEM_MOST)


def cost(flops, moved, transcendentals=0):
    return pl.CostEstimate(
        flops=int(flops) // 8, bytes_accessed=int(moved) // 8, transcendentals=int(transcendentals)
    )


def nn(left, right):
    return lax.dot_general(left, right, (((1,), (0,)), ((), ())), preferred_element_type=F32)


def nt(left, right):
    return lax.dot_general(left, right, (((1,), (1,)), ((), ())), preferred_element_type=F32)


def tn(left, right):
    return lax.dot_general(left, right, (((0,), (0,)), ((), ())), preferred_element_type=F32)


def flip(value, bit):
    return lax.ppermute(value, "fsdp", [(place, place ^ bit) for place in range(8)])


def half_rows(rows):
    return (rows // 2 + 15) // 16 * 16


def plan_of(rows):
    half = half_rows(rows)
    return (
        (0, 0, rows),
        (1, 0, rows),
        (2, 0, rows),
        (3, 0, rows),
        (4, 0, rows),
        (5, 0, rows),
        (6, 0, half),
        (6, half, rows - half),
        (7, 0, half),
        (7, half, rows - half),
    )


def hold(value, *others):
    return lax.optimization_barrier((value, others))[0]


def spread_near(own):
    along_x, along_y = flip(own, 2), flip(own, 4)
    return (own, flip(own, 1), along_x, flip(along_x, 1), along_y, flip(along_y, 1))


def spread_diagonal(near):
    half = half_rows(near[0].shape[0])
    return (flip(near[4][:half], 2), flip(near[2][half:], 4))


def spread_far(diagonal):
    return (*diagonal, flip(diagonal[0], 1), flip(diagonal[1], 1))


def spread(own):
    near = spread_near(own)
    return near + spread_far(spread_diagonal(near))


def add_low(left, right):
    return (left.astype(F32) + right.astype(F32)).astype(BF)


def collect(odd, even, tick=None):
    half = half_rows(even.shape[1])
    received = flip(odd, 1)
    diagonal_low = flip(add_low(even[3, :half], received[3, :half]), 2)
    diagonal_high = flip(add_low(even[3, half:], received[3, half:]), 4)
    if tick is not None:
        diagonal_low, diagonal_high = tick((diagonal_low, diagonal_high))
    own = add_low(even[0], received[0])
    for_y = even[2].astype(F32) + received[2].astype(F32)
    for_x = even[1].astype(F32) + received[1].astype(F32)
    for_y = jnp.concatenate([for_y[:half] + diagonal_low.astype(F32), for_y[half:]]).astype(BF)
    for_x = jnp.concatenate([for_x[:half], for_x[half:] + diagonal_high.astype(F32)]).astype(BF)
    return (own, flip(for_x, 2), flip(for_y, 4))


def start_fetch(me, plan, sources, target, block_rows, sems):
    copies = []
    for number, (partner, first, rows) in enumerate(plan):
        start = pl.multiple_of((me ^ partner) * block_rows + first, 64)
        copies.append(
            pltpu.make_async_copy(
                sources[number].at[:, pl.ds(0, 2176)],
                target.at[pl.ds(start, rows)],
                sems.at[number],
            )
        )
        copies[-1].start()
    return copies


def start_fetch_out(me, plan, sources, target, sems):
    copies = []
    for number, (partner, first, rows) in enumerate(plan):
        start = pl.multiple_of((me ^ partner) * 128 + first, 64)
        copies.append(
            pltpu.make_async_copy(
                sources[number].at[:, pl.ds(2176, 1024)],
                target.at[pl.ds(start, rows)],
                sems.at[number],
            )
        )
        copies[-1].start()
    return copies


def turn(values, cosine, sine):
    lane = lax.broadcasted_iota(jnp.int32, values.shape, 1)
    other = jnp.where(
        lane % HD < HD // 2, pltpu.roll(values, 128 - HD // 2, 1), pltpu.roll(values, HD // 2, 1)
    )
    return values * cosine + other * sine


def side_by_side(left, right, group):
    lane = lax.broadcasted_iota(jnp.int32, left.shape, 1)
    if group == 0:
        return jnp.where(lane < HD, left, pltpu.roll(right, HD, 1))
    return jnp.where(lane < HD, pltpu.roll(left, HD, 1), right)


def project_kernel(plan, me_ref, tokens_ref, cos_ref, sin_ref, *refs):
    count = len(plan)
    first_ref, second_ref, extra_ref, mats, sems = refs[count:]
    copies = start_fetch(me_ref[0], plan, refs[:count], mats, 128, sems)
    stream = tokens_ref[...].astype(F32)
    scaled = stream * lax.rsqrt(jnp.mean(stream * stream, axis=-1, keepdims=True) + norm_eps)
    for copy in copies:
        copy.wait()
    extra = mats[:, 2048:2176].astype(F32).T
    extra_ref[...] = extra[:48].astype(BF)
    normed = (scaled * extra[32:33]).astype(BF)
    cosine, sine = cos_ref[...], sin_ref[...]
    for part in range(4):
        query = nn(normed, mats[:, part * 256 : part * 256 + 256])
        key = turn(nn(normed, mats[:, 1024 + part * 128 : 1152 + part * 128]), cosine, sine)
        value = nn(normed, mats[:, 1536 + part * 128 : 1664 + part * 128])
        for group, target in enumerate((first_ref, second_ref)):
            target[part, :, 0:128] = turn(
                query[:, group * 128 : group * 128 + 128], cosine, sine
            ).astype(BF)
            target[part, :, 128:256] = side_by_side(key, value, group).astype(BF)


def project(me, tokens, cosine, sine, pieces):
    plan = plan_of(128)
    return pl.pallas_call(
        functools.partial(project_kernel, plan),
        out_shape=(
            shaped((4, 512, 256), BF),
            shaped((4, 512, 256), BF),
            shaped((48, 1024), BF),
        ),
        in_specs=[in_smem()] + in_vmem(3) + in_hbm(len(plan)),
        out_specs=tuple(in_vmem(3)),
        scratch_shapes=[pltpu.VMEM((1024, 2176), BF), pltpu.SemaphoreType.DMA((len(plan),))],
        compiler_params=params(),
        cost_estimate=cost(2 * 512 * 1024 * 2048, 9e6),
        name="project",
    )(me, tokens, cosine, sine, *pieces)


def placed(values, half, side):
    moved = values.astype(F32)
    if half != side:
        moved = pltpu.roll(moved, HD, 1)
    lane = lax.broadcasted_iota(jnp.int32, values.shape, 1)
    return jnp.where((lane < HD) == (side == 0), moved, 0.0).astype(values.dtype)


def allowed_pairs(first, rows, step, start):
    key_at = first + lax.broadcasted_iota(jnp.int32, (rows, QB), 0)
    query_at = HALO + step * QB + lax.broadcasted_iota(jnp.int32, (rows, QB), 1)
    return (key_at >= start) & (key_at <= query_at)


def attend_kernel(
    low_ref, own_ref, halo_ref, start_ref, out_ref, log_ref, pairs, pairs_t, most, total, blend
):
    step = pl.program_id(0)

    @pl.when(step == 0)
    def _():
        for first in range(0, HALO, 512):
            rows = slice(first, first + 512)
            late = slice(HALO + first, HALO + first + 512)
            pairs[rows, :] = halo_ref[rows, :]
            pairs[late, :] = own_ref[rows, 128:256]
            pairs_t[:, rows] = halo_ref[rows, :].astype(F32).T.astype(BF)
            pairs_t[:, late] = own_ref[rows, 128:256].astype(F32).T.astype(BF)

    start = start_ref[0]
    query = own_ref[pl.ds(pl.multiple_of(step * QB, QB), QB), 0:128]
    picks = [placed(query, half, 0) for half in range(2)]
    most[...] = jnp.full(most.shape, masked_score, F32)
    total[...] = jnp.zeros(total.shape, F32)
    blend[...] = jnp.zeros(blend.shape, F32)

    def visit(block, carry):
        first = pl.multiple_of(block * KB, KB)
        allowed = allowed_pairs(first, KB, step, start)
        pair = pairs[pl.ds(first, KB), :]
        value = pairs_t[HD:128, pl.ds(first, KB)]
        raw = [nt(pair, picks[half]) for half in range(2)]
        for half in range(2):
            scores = jnp.where(allowed, raw[half] * (attend_scale * LOG2E), masked_score)
            before = most[half : half + 1, :]
            top = jnp.maximum(before, jnp.max(scores, axis=0, keepdims=True))
            weight = jnp.exp2(scores - top)
            fade = jnp.exp2(before - top)
            most[half : half + 1, :] = top
            total[half : half + 1, :] = total[half : half + 1, :] * fade + jnp.sum(
                weight, axis=0, keepdims=True
            )
            rows = slice(half * HD, half * HD + HD)
            blend[rows, :] = blend[rows, :] * fade + nn(value, weight.astype(BF))
        return carry

    lax.fori_loop(low_ref[step], (HALO + (step + 1) * QB) // KB, visit, 0)
    for half in range(2):
        rows = slice(half * HD, half * HD + HD)
        blend[rows, :] = blend[rows, :] / total[half : half + 1, :]
    out_ref[...] = blend[...].T.astype(BF)
    log_ref[0:2, :] = most[0:2, :] + jnp.log2(total[0:2, :])
    log_ref[2:8, :] = jnp.zeros((6, QB), F32)


def attend(low_block, own, halo, start):
    spec = lambda shape, index: pl.BlockSpec(shape, index)
    return pl.pallas_call(
        attend_kernel,
        out_shape=(shaped((2048, 128), BF), shaped((8, 2048), F32)),
        grid_spec=pltpu.PrefetchScalarGridSpec(
            num_scalar_prefetch=1,
            grid=(2048 // QB,),
            in_specs=[
                spec((2048, 256), lambda i, low: (0, 0)),
                spec((2048, 128), lambda i, low: (0, 0)),
                spec((1, 1, QB), lambda i, low: (i, 0, 0)),
            ],
            out_specs=(
                spec((QB, 128), lambda i, low: (i, 0)),
                spec((8, QB), lambda i, low: (0, i)),
            ),
            scratch_shapes=[
                pltpu.VMEM((2 * HALO, 128), BF),
                pltpu.VMEM((128, 2 * HALO), BF),
                pltpu.VMEM((8, QB), F32),
                pltpu.VMEM((8, QB), F32),
                pltpu.VMEM((128, QB), F32),
            ],
        ),
        compiler_params=params(),
        cost_estimate=cost(12e9, 3e6),
        name="attend",
    )(low_block, own, halo, start)


def attend_back_kernel(
    low_ref, own_ref, halo_ref, start_ref, out_ref, grad_ref, log_ref,
    own_grad_ref, halo_grad_ref, pairs, pairs_t, pair_grad, blend,
):
    step = pl.program_id(0)

    @pl.when(step == 0)
    def _():
        for first in range(0, HALO, 512):
            rows = slice(first, first + 512)
            late = slice(HALO + first, HALO + first + 512)
            pairs[rows, :] = halo_ref[rows, :]
            pairs[late, :] = own_ref[rows, 128:256]
            pairs_t[:, rows] = halo_ref[rows, :].astype(F32).T.astype(BF)
            pairs_t[:, late] = own_ref[rows, 128:256].astype(F32).T.astype(BF)
        pair_grad[...] = jnp.zeros(pair_grad.shape, F32)

    start = start_ref[0]
    here_rows = pl.ds(pl.multiple_of(step * QB, QB), QB)
    query, grad = own_ref[here_rows, 0:128], grad_ref[...]
    product = (out_ref[...].astype(F32) * grad.astype(F32)).T
    picks, incoming, centres = [], [], []
    for half in range(2):
        picks.append(placed(query, half, 0))
        incoming.append(placed(grad, half, 1))
        centres.append(jnp.sum(product[half * HD : half * HD + HD, :], axis=0, keepdims=True))
    blend[...] = jnp.zeros(blend.shape, F32)

    def visit(block, carry):
        first = pl.multiple_of(block * BACK_KB, BACK_KB)
        allowed = allowed_pairs(first, BACK_KB, step, start)
        here = pl.ds(first, BACK_KB)
        pair, key_t = pairs[here, :], pairs_t[0:HD, here]
        for half in range(2):
            scores = nt(pair, picks[half]) * (attend_scale * LOG2E)
            weight = jnp.where(allowed, jnp.exp2(scores - log_ref[half : half + 1, :]), 0.0)
            weight_grad = nt(pair, incoming[half])
            score_grad = (
                weight * (weight_grad - centres[half]) * attend_scale
            ).astype(BF)
            pair_grad[here, :] += nn(weight.astype(BF), incoming[half]) + nn(
                score_grad, picks[half]
            )
            blend[half * HD : half * HD + HD, :] += nn(key_t, score_grad)
        return carry

    lax.fori_loop(low_ref[step], (HALO + (step + 1) * QB) // BACK_KB, visit, 0)
    own_grad_ref[here_rows, 0:128] = blend[...].T

    @pl.when(step == pl.num_programs(0) - 1)
    def _():
        for first in range(0, HALO, 512):
            rows = slice(first, first + 512)
            late = slice(HALO + first, HALO + first + 512)
            halo_grad_ref[rows, :] = pair_grad[rows, :].astype(BF)
            own_grad_ref[rows, 128:256] = pair_grad[late, :]


def attend_back(low_block, own, halo, start, out, grad, logs):
    spec = lambda shape, index: pl.BlockSpec(shape, index)
    tile = spec((QB, 128), lambda i, low: (i, 0))
    whole = spec((2048, 256), lambda i, low: (0, 0))
    half = spec((2048, 128), lambda i, low: (0, 0))
    return pl.pallas_call(
        attend_back_kernel,
        out_shape=(shaped((2048, 256), F32), shaped((2048, 128), BF)),
        grid_spec=pltpu.PrefetchScalarGridSpec(
            num_scalar_prefetch=1,
            grid=(2048 // QB,),
            in_specs=[
                whole,
                half,
                spec((1, 1, QB), lambda i, low: (i, 0, 0)),
                tile,
                tile,
                spec((8, QB), lambda i, low: (0, i)),
            ],
            out_specs=(whole, half),
            scratch_shapes=[
                pltpu.VMEM((2 * HALO, 128), BF),
                pltpu.VMEM((128, 2 * HALO), BF),
                pltpu.VMEM((2 * HALO, 128), F32),
                pltpu.VMEM((128, QB), F32),
            ],
        ),
        compiler_params=params(),
        cost_estimate=cost(30e9, 6e6),
        name="attend_back",
    )(low_block, own, halo, start, out, grad, logs)


def after_kernel(
    plan, me_ref, tokens_ref, first_ref, second_ref, extra_ref, routed_ref, *refs
):
    count = len(plan)
    hidden_ref, payload_ref, gates_ref, mats, sems = refs[count:]
    copies = start_fetch_out(me_ref[0], plan, refs[:count], mats, sems)
    stream = tokens_ref[...].astype(F32)
    for copy in copies:
        copy.wait()
    branch = jnp.zeros((512, 1024), F32)
    for part in range(4):
        both = jnp.concatenate([first_ref[part], second_ref[part]], axis=1)
        branch += nn(both, mats[part * 256 : part * 256 + 256, :])
    hidden = stream + branch_scale * branch
    hidden_ref[...] = hidden
    inverse = lax.rsqrt(jnp.mean(hidden * hidden, axis=-1, keepdims=True) + norm_eps)
    normed = (hidden * inverse * extra_ref[33:34, :].astype(F32)).astype(BF)
    payload_ref[0:512, :] = normed
    logits = nt(extra_ref[0:32, :], normed)
    routed = routed_ref[...] > 0.5
    top = jnp.max(jnp.where(routed, logits, masked_score), axis=0, keepdims=True)
    raised = jnp.where(routed, jnp.exp(logits - top), 0.0)
    gates = raised / jnp.sum(raised, axis=0, keepdims=True)
    gates_ref[...] = gates
    low = gates.astype(BF)
    payload_ref[512:528, 0:512] = low[0:16, :]
    payload_ref[512:528, 512:1024] = low[16:32, :]


def after_attention(me, tokens, attended, extra, routed, pieces):
    plan = plan_of(128)
    return pl.pallas_call(
        functools.partial(after_kernel, plan),
        out_shape=(shaped((512, 1024), F32), shaped((528, 1024), BF), shaped((32, 512), F32)),
        in_specs=[in_smem()] + in_vmem(5) + in_hbm(len(plan)),
        out_specs=tuple(in_vmem(3)),
        scratch_shapes=[pltpu.VMEM((1024, 1024), BF), pltpu.SemaphoreType.DMA((len(plan),))],
        compiler_params=params(),
        cost_estimate=cost(2 * 512 * 1024 * 1024, 8e6),
        name="after_attention",
    )(me, tokens, *attended, extra, routed, *pieces)


def own_rows(me, packed):
    first = me * 4
    side = jnp.where(first < 16, packed[:, :512], packed[:, 512:])
    row = lax.broadcasted_iota(jnp.int32, side.shape, 0)
    return [
        jnp.sum(jnp.where(row == first % 16 + expert, side, 0.0), axis=0, keepdims=True)
        for expert in range(4)
    ]


def stand_up(rows):
    row = lax.broadcasted_iota(jnp.int32, (128, 512), 0)
    lying = jnp.zeros((128, 512), F32)
    for number, values in enumerate(rows):
        lying = jnp.where(row == number, values, lying)
    return lying.T


def slot_hot(slot_row):
    at = lax.broadcasted_iota(jnp.int32, (144, 512), 0).astype(F32)
    return at == slot_row


def block_plan(partners, height):
    return tuple(
        (partners.index(partner), first, min(rows, 528 - first))
        for partner, first, rows in plan_of(height)
        if partner in partners
    )


def start_blocks(plan, sources, target, sems):
    copies = []
    for number, (place, first, rows) in enumerate(plan):
        copies.append(
            pltpu.make_async_copy(
                sources[number].at[pl.ds(0, rows)],
                target.at[place, pl.ds(first, rows)],
                sems.at[number],
            )
        )
        copies[-1].start()
    return copies


def pick_grad_kernel(plan, blocks, me_ref, *refs):
    count = len(plan)
    rows_ref, slots_ref, columns_ref, held, made, sems, out_sems = refs[count:]
    copies = start_blocks(plan, refs[:count], held, sems)
    leaving = []
    for block in range(blocks):
        for copy, (place, _, _) in zip(copies, plan):
            if place == block:
                copy.wait()
        tokens = held[block, 0:512, :]
        slots = own_rows(me_ref[0], held[block, 512:528, :].astype(F32))
        for expert in range(4):
            hot = jnp.where(slot_hot(slots[expert]), 1.0, 0.0).astype(BF)
            made[block, expert * 144 : expert * 144 + 144, :] = nn(hot, tokens).astype(BF)
            slots_ref[block, expert : expert + 1, :] = slots[expert]
        columns_ref[block] = stand_up(slots).astype(BF)
        leaving.append(
            pltpu.make_async_copy(made.at[block], rows_ref.at[block], out_sems.at[block])
        )
        leaving[-1].start()
    for copy in leaving:
        copy.wait()


def pick_grads(me, partners, pieces):
    blocks, plan = len(partners), block_plan(partners, 528)
    return pl.pallas_call(
        functools.partial(pick_grad_kernel, plan, blocks),
        out_shape=(
            shaped((blocks, 576, 1024), BF),
            shaped((blocks, 4, 512), F32),
            shaped((blocks, 512, 128), BF),
        ),
        in_specs=[in_smem()] + in_hbm(len(pieces)),
        out_specs=tuple(in_hbm(1) + in_vmem(2)),
        scratch_shapes=[
            pltpu.VMEM((blocks, 528, 1024), BF),
            pltpu.VMEM((blocks, 576, 1024), BF),
            pltpu.SemaphoreType.DMA((len(pieces),)),
            pltpu.SemaphoreType.DMA((blocks,)),
        ],
        compiler_params=params(),
        cost_estimate=cost(blocks * 2 * 576 * 512 * 1024, blocks * 2.4e6),
        name="pick_grads",
    )(me, *pieces)


def pick_rows_kernel(plan, blocks, me_ref, slots_ref, *refs):
    count = len(plan)
    rows_ref, gate_ref, columns_ref, held, made, sems, out_sems = refs[count:]
    copies = start_blocks(plan, refs[:count], held, sems)
    leaving = []
    for block in range(blocks):
        for copy, (place, _, _) in zip(copies, plan):
            if place == block:
                copy.wait()
        tokens = held[block, 0:512, :]
        gates = own_rows(me_ref[0], held[block, 512:528, :].astype(F32))
        for expert in range(4):
            match = slot_hot(slots_ref[block, expert : expert + 1, :])
            hot = jnp.where(match, 1.0, 0.0).astype(BF)
            rows = slice(expert * 144, expert * 144 + 144)
            made[block, rows, :] = nn(hot, tokens).astype(BF)
            gate = jnp.sum(jnp.where(match, gates[expert], 0.0), axis=1, keepdims=True)
            gate_ref[block, rows, :] = jnp.broadcast_to(gate, (144, 128)).astype(BF)
        columns_ref[block] = stand_up(gates).astype(BF)
        leaving.append(
            pltpu.make_async_copy(made.at[block], rows_ref.at[block], out_sems.at[block])
        )
        leaving[-1].start()
    for copy in leaving:
        copy.wait()


def pick_rows(me, slots, partners, pieces):
    blocks, plan = len(partners), block_plan(partners, 528)
    return pl.pallas_call(
        functools.partial(pick_rows_kernel, plan, blocks),
        out_shape=(
            shaped((blocks, 576, 1024), BF),
            shaped((blocks, 576, 128), BF),
            shaped((blocks, 512, 128), BF),
        ),
        in_specs=[in_smem()] + in_vmem(1) + in_hbm(len(pieces)),
        out_specs=tuple(in_hbm(1) + in_vmem(2)),
        scratch_shapes=[
            pltpu.VMEM((blocks, 528, 1024), BF),
            pltpu.VMEM((blocks, 576, 1024), BF),
            pltpu.SemaphoreType.DMA((len(pieces),)),
            pltpu.SemaphoreType.DMA((blocks,)),
        ],
        compiler_params=params(),
        cost_estimate=cost(blocks * 2 * 576 * 512 * 1024, blocks * 2.4e6),
        name="pick_rows",
    )(me, slots, *pieces)


def both_parts(pair, part):
    if part == 0:
        return pair[0][0:4].reshape(576, -1)
    return jnp.concatenate([pair[0][4:6].reshape(288, -1), pair[1][...].reshape(288, -1)], axis=0)


def expert_grad_kernel(*refs):
    rows_refs, grads_refs, gate_refs = refs[0:2], refs[2:4], refs[4:6]
    gate_w, up_w, down_w = (ref[0] for ref in refs[6:9])
    lin_ref, inner_ref, grad_ref = refs[9:12]
    lin_grads, inners, out_grads, inputs = refs[12:16]
    for part in range(2):
        at = slice(part * 576, part * 576 + 576)
        blocks = slice(part * 4, part * 4 + 4)
        rows = both_parts(rows_refs, part)
        inputs[at, :] = rows
        gate_lin = nn(rows, gate_w)
        up_lin = nn(rows, up_w)
        sigma = 1.0 / (1.0 + jnp.exp(-gate_lin))
        swished = gate_lin * sigma
        inner = (swished * up_lin).astype(BF)
        inners[at, :] = inner
        inner_ref[blocks] = inner.reshape(4, 144, 512)
        gate = both_parts(gate_refs, part)[:, 0:1].astype(F32)
        out_grad = (both_parts(grads_refs, part).astype(F32) * gate).astype(BF)
        out_grads[at, :] = out_grad
        inner_grad = nt(out_grad, down_w)
        lin_grads[at, 0:512] = (
            inner_grad * up_lin * sigma * (1.0 + gate_lin * (1.0 - sigma))
        ).astype(BF)
        lin_grads[at, 512:1024] = (inner_grad * swished).astype(BF)
        lin_ref[blocks] = lin_grads[at, :].reshape(4, 144, 1024)
    down_grad = tn(inners[...], out_grads[...]).astype(BF)
    grad_ref[2048:2560, :] = down_grad[:, 0:512]
    grad_ref[2560:3072, :] = down_grad[:, 512:1024]
    grad_ref[0:1024, :] = tn(inputs[...], lin_grads[:, 0:512]).astype(BF)
    grad_ref[1024:2048, :] = tn(inputs[...], lin_grads[:, 512:1024]).astype(BF)


def expert_grads(base, count, rows, grads, gates, gate_w, up_w, down_w):
    spec = pl.BlockSpec
    wide = [spec((blocks, 144, 1024), lambda e: (0, base + e, 0)) for blocks in (6, 2)]
    slim = [spec((blocks, 144, 128), lambda e: (0, base + e, 0)) for blocks in (6, 2)]
    tall_w = spec((1, 1024, 512), lambda e: (base + e, 0, 0))
    flat_w = spec((1, 512, 1024), lambda e: (base + e, 0, 0))
    return pl.pallas_call(
        expert_grad_kernel,
        out_shape=(
            shaped((8, 144 * count, 1024), BF),
            shaped((8, 144 * count, 512), BF),
            shaped((3072 * count, 512), BF),
        ),
        grid=(count,),
        in_specs=wide * 2 + slim + [tall_w, tall_w, flat_w],
        out_specs=(
            spec((8, 144, 1024), lambda e: (0, e, 0)),
            spec((8, 144, 512), lambda e: (0, e, 0)),
            spec((3072, 512), lambda e: (e, 0)),
        ),
        scratch_shapes=[
            pltpu.VMEM((1152, 1024), BF),
            pltpu.VMEM((1152, 512), BF),
            pltpu.VMEM((1152, 1024), BF),
            pltpu.VMEM((1152, 1024), BF),
        ],
        compiler_params=params(),
        cost_estimate=cost(count * 8e9, count * 15e6),
        name="expert_grads",
    )(*rows, *grads, *gates, gate_w, up_w, down_w)


def expert_rows_kernel(base, me_ref, lin_ref, inner_ref, *refs):
    grads_refs = refs[0:2]
    gate_w, up_w, down_w = (ref[0] for ref in refs[2:5])
    out_ref, in_grad_ref, mark_ref = refs[5:8]
    expert = me_ref[0] * 4 + base + pl.program_id(0)
    lane = lax.broadcasted_iota(jnp.int32, (576, 128), 1)
    for part in range(2):
        blocks = slice(part * 4, part * 4 + 4)
        result = nn(inner_ref[blocks].reshape(576, 512), down_w).astype(BF)
        out_ref[blocks] = result.reshape(4, 144, 1024)
        wide = both_parts(grads_refs, part).astype(F32)
        gate_slot = jnp.sum(wide * result.astype(F32), axis=1, keepdims=True)
        mark_ref[blocks] = jnp.where(lane == expert, gate_slot, 0.0).astype(BF).reshape(4, 144, 128)
        lin = lin_ref[blocks].reshape(576, 1024)
        in_grad_ref[blocks] = (
            (nt(lin[:, 0:512], gate_w) + nt(lin[:, 512:1024], up_w))
            .astype(BF)
            .reshape(4, 144, 1024)
        )


def expert_rows(me, base, count, lin, inner, grads, gate_w, up_w, down_w):
    spec = pl.BlockSpec
    wide = [spec((blocks, 144, 1024), lambda e: (0, base + e, 0)) for blocks in (6, 2)]
    tall_w = spec((1, 1024, 512), lambda e: (base + e, 0, 0))
    flat_w = spec((1, 512, 1024), lambda e: (base + e, 0, 0))
    own = lambda width: spec((8, 144, width), lambda e: (0, e, 0))
    return pl.pallas_call(
        functools.partial(expert_rows_kernel, base),
        out_shape=(
            shaped((8, 144 * count, 1024), BF),
            shaped((8, 144 * count, 1024), BF),
            shaped((8, 144 * count, 128), BF),
        ),
        grid=(count,),
        in_specs=[in_smem(), own(1024), own(512)] + wide + [tall_w, tall_w, flat_w],
        out_specs=(own(1024), own(1024), own(128)),
        compiler_params=params(),
        cost_estimate=cost(count * 4e9, count * 14e6),
        name="expert_rows",
    )(me, lin, inner, *grads, gate_w, up_w, down_w)


def combine_kernel(calls, weighted, *refs):
    slot_ref = refs[0]
    refs = refs[1:]
    gate_ref = None
    if weighted:
        gate_ref, refs = refs[0], refs[1:]
    value_refs, refs = refs[:calls], refs[calls:]
    mark_refs = ()
    if not weighted:
        mark_refs, refs = refs[:calls], refs[calls:]
    out_ref = refs[0]
    here = 4 // calls
    slots = slot_ref[0].astype(F32)
    lane = lax.broadcasted_iota(jnp.int32, (512, 144 * here), 1).astype(F32)
    total, marks = None, None
    for call in range(calls):
        hot = jnp.zeros((512, 144 * here), F32)
        for local_expert in range(here):
            number = call * here + local_expert
            slot = slots[:, number : number + 1]
            place = jnp.where(slot < 144.0, slot + 144.0 * local_expert, -1.0)
            put = 1.0
            if weighted:
                put = gate_ref[0][:, number : number + 1].astype(F32)
            hot = jnp.where(lane == place, put, hot)
        hot = hot.astype(BF)
        term = nn(hot, value_refs[call][0])
        total = term if total is None else total + term
        if not weighted:
            mark = nn(hot, mark_refs[call][0])
            marks = mark if marks is None else marks + mark
    out_ref[0, 0:512, :] = total.astype(BF)
    if not weighted:
        lying = marks.T[0:32, :].astype(BF)
        out_ref[0, 512:528, 0:512] = lying[0:16, :]
        out_ref[0, 512:528, 512:1024] = lying[16:32, :]


def combine(parity, slots, gates, values, marks):
    calls = len(values)
    weighted = gates is not None
    rows = 512 if weighted else 528
    column = pl.BlockSpec((1, 512, 128), lambda i: (2 * i + parity, 0, 0))
    wide = pl.BlockSpec((1, 576 // calls, 1024), lambda i: (2 * i + parity, 0, 0))
    slim = pl.BlockSpec((1, 576 // calls, 128), lambda i: (2 * i + parity, 0, 0))
    args = [slots] + ([gates] if weighted else []) + list(values) + list(marks)
    return pl.pallas_call(
        functools.partial(combine_kernel, calls, weighted),
        out_shape=shaped((4, rows, 1024), BF),
        grid=(4,),
        in_specs=[column]
        + ([column] if weighted else [])
        + [wide] * calls
        + [slim] * len(marks),
        out_specs=pl.BlockSpec((1, rows, 1024), lambda i: (i, 0, 0)),
        compiler_params=params(),
        cost_estimate=cost(4 * 2 * 512 * 768 * 1024, 10e6),
        name="combine",
    )(*args)


def back_kernel(
    plan, me_ref, sum_ref, sum_x_ref, sum_y_ref, hidden_ref, cot_ref, payload_ref, gates_ref,
    extra_ref, *refs,
):
    count = len(plan)
    hidden_grad_ref, branch_grad_ref, first_ref, second_ref, small_ref, mats, sems = refs[count:]
    copies = start_fetch_out(me_ref[0], plan, refs[:count], mats, sems)
    total = (
        sum_ref[...].astype(F32) + sum_x_ref[...].astype(F32) + sum_y_ref[...].astype(F32)
    )
    gate_grad = jnp.concatenate([total[512:528, 0:512], total[512:528, 512:1024]], axis=0)
    gates = gates_ref[...]
    logit_grad = (
        gates * (gate_grad - jnp.sum(gates * gate_grad, axis=0, keepdims=True))
    ).astype(BF)
    normed_grad = total[0:512, :] + tn(logit_grad, extra_ref[0:32, :])
    hidden = hidden_ref[...]
    inverse = lax.rsqrt(jnp.mean(hidden * hidden, axis=-1, keepdims=True) + norm_eps)
    scaled = normed_grad * extra_ref[33:34, :].astype(F32)
    spread_out = inverse * inverse * inverse * jnp.mean(hidden * scaled, axis=-1, keepdims=True)
    hidden_grad = cot_ref[...].astype(F32) + inverse * scaled - hidden * spread_out
    hidden_grad_ref[...] = hidden_grad
    small_ref[0:32, :] = nn(logit_grad, payload_ref[0:512, :])
    small_ref[32:40, :] = jnp.broadcast_to(
        jnp.sum(normed_grad * hidden * inverse, axis=0, keepdims=True), (8, 1024)
    )
    branch_grad = (branch_scale * hidden_grad).astype(BF)
    branch_grad_ref[...] = branch_grad
    for copy in copies:
        copy.wait()
    for part in range(4):
        grad = nt(branch_grad, mats[part * 256 : part * 256 + 256, :]).astype(BF)
        first_ref[part] = grad[:, 0:128]
        second_ref[part] = grad[:, 128:256]


def back_to_attention(me, sums, hidden, cotangent, payload, gates, extra, pieces):
    plan = plan_of(128)
    return pl.pallas_call(
        functools.partial(back_kernel, plan),
        out_shape=(
            shaped((512, 1024), F32),
            shaped((512, 1024), BF),
            shaped((4, 512, 128), BF),
            shaped((4, 512, 128), BF),
            shaped((40, 1024), F32),
        ),
        in_specs=[in_smem()] + in_vmem(8) + in_hbm(len(plan)),
        out_specs=tuple(in_vmem(5)),
        scratch_shapes=[pltpu.VMEM((1024, 1024), BF), pltpu.SemaphoreType.DMA((len(plan),))],
        compiler_params=params(),
        cost_estimate=cost(2 * 512 * 1024 * 1024, 12e6),
        name="back_to_attention",
    )(me, *sums, hidden, cotangent, payload, gates, extra, *pieces)


def deal_out(me, big, odd_ref, even_ref):
    for pair in range(4):
        for target, partner in ((even_ref, 2 * pair), (odd_ref, 2 * pair + 1)):
            start = pl.multiple_of((me ^ partner) * 128, 128)
            target[pair] = big[pl.ds(start, 128), :]


def out_grad_kernel(me_ref, first_ref, second_ref, branch_grad_ref, small_ref, odd_ref, even_ref, big):
    branch_grad = branch_grad_ref[...]
    for part in range(4):
        both = jnp.concatenate([first_ref[part], second_ref[part]], axis=1)
        big[part * 256 : part * 256 + 256, 0:1024] = tn(both, branch_grad).astype(BF)
    small = jnp.concatenate([small_ref[...], jnp.zeros((88, 1024), F32)], axis=0)
    big[:, 1024:1152] = small.T.astype(BF)
    deal_out(me_ref[0], big, odd_ref, even_ref)


def out_grads_of(me, attended, branch_grad, small):
    return pl.pallas_call(
        out_grad_kernel,
        out_shape=(shaped((4, 128, 1152), BF), shaped((4, 128, 1152), BF)),
        in_specs=[in_smem()] + in_vmem(4),
        out_specs=tuple(in_vmem(2)),
        scratch_shapes=[pltpu.VMEM((1024, 1152), BF)],
        compiler_params=params(),
        cost_estimate=cost(2 * 512 * 1024 * 1024, 5e6),
        name="out_grads",
    )(me, *attended, branch_grad, small)


def input_kernel(
    plan, me_ref, tokens_ref, cos_ref, sin_ref, first_ref, second_ref, extra_ref,
    hidden_grad_ref, *refs,
):
    count = len(plan)
    input_grad_ref, odd_ref, even_ref, mats, big, lin, sems = refs[count:]
    me = me_ref[0]
    copies = start_fetch(me, plan, refs[:count], mats, 128, sems)
    stream = tokens_ref[...].astype(F32)
    inverse = lax.rsqrt(jnp.mean(stream * stream, axis=-1, keepdims=True) + norm_eps)
    gain = extra_ref[32:33, :].astype(F32)
    normed = (stream * inverse * gain).astype(BF)
    cosine, sine = cos_ref[...], -sin_ref[...]
    for part in range(4):
        tiles = []
        for group, source in enumerate((first_ref, second_ref)):
            lin[:, part * 256 + group * 128 : part * 256 + group * 128 + 128] = turn(
                source[part, :, 0:128].astype(F32), cosine, sine
            ).astype(BF)
            tiles.append(source[part, :, 128:256].astype(F32))
        lane = lax.broadcasted_iota(jnp.int32, tiles[0].shape, 1)
        key = jnp.where(lane < HD, tiles[0], pltpu.roll(tiles[1], HD, 1))
        value = jnp.where(lane < HD, pltpu.roll(tiles[0], HD, 1), tiles[1])
        lin[:, 1024 + part * 128 : 1152 + part * 128] = turn(key, cosine, sine).astype(BF)
        lin[:, 1536 + part * 128 : 1664 + part * 128] = value.astype(BF)
    normed_t = normed.astype(F32).T.astype(BF)
    for first in range(0, 2048, 512):
        big[:, first : first + 512] = nn(normed_t, lin[:, first : first + 512]).astype(BF)
    for copy in copies:
        copy.wait()
    normed_grad = nt(lin[...], mats[:, 0:2048])
    row = jnp.sum(normed_grad * stream * inverse, axis=0, keepdims=True)
    big[:, 2048:2176] = jnp.broadcast_to(row, (128, 1024)).T.astype(BF)
    deal_out(me, big, odd_ref, even_ref)
    scaled = normed_grad * gain
    spread_out = inverse * inverse * inverse * jnp.mean(stream * scaled, axis=-1, keepdims=True)
    input_grad_ref[...] = (
        hidden_grad_ref[...] + inverse * scaled - stream * spread_out
    ).astype(BF)


def input_grads(me, tokens, cosine, sine, query_grad, pair_grad, extra, hidden_grad, pieces):
    plan = plan_of(128)
    return pl.pallas_call(
        functools.partial(input_kernel, plan),
        out_shape=(
            shaped((512, 1024), BF),
            shaped((4, 128, 2176), BF),
            shaped((4, 128, 2176), BF),
        ),
        in_specs=[in_smem()] + in_vmem(7) + in_hbm(len(plan)),
        out_specs=tuple(in_vmem(3)),
        scratch_shapes=[
            pltpu.VMEM((1024, 2176), BF),
            pltpu.VMEM((1024, 2176), BF),
            pltpu.VMEM((512, 2048), BF),
            pltpu.SemaphoreType.DMA((len(plan),)),
        ],
        compiler_params=params(),
        cost_estimate=cost(4 * 512 * 1024 * 2048, 15e6),
        name="input_grads",
    )(me, tokens, cosine, sine, query_grad, pair_grad, extra, hidden_grad, *pieces)


def dense_slots(routes, ranks, experts):
    mine = routes[None, :, :] == jnp.arange(experts, dtype=jnp.int32)[:, None, None]
    far = jnp.int32(1 << 20)
    rank = jnp.min(jnp.where(mine, ranks[None, :, :], far), axis=-1)
    slot = jnp.sum((rank[:, None, :] < rank[:, :, None]).astype(jnp.int32), axis=-1)
    routed = rank < far
    return (jnp.where(routed & (slot < 144), slot, 255).astype(BF), routed.astype(F32))


def across(values):
    return lax.all_to_all(values, "sp", split_axis=0, concat_axis=0, tiled=True)


def sum_shared(value):
    rows, columns = value.shape
    quarters = across(value).reshape(4, rows // 4, columns).astype(F32)
    quarter = jnp.sum(quarters, axis=0).astype(BF)
    return across(jnp.tile(quarter, (4, 1)))


def sum_line(value, seq):
    outer = (seq == 0) | (seq == 3)
    value = add_low(value, lax.ppermute(value, "sp", ((0, 1), (3, 2))))
    value = add_low(value, lax.ppermute(value, "sp", ((1, 2), (2, 1))))
    return jnp.where(outer, lax.ppermute(value, "sp", ((1, 0), (2, 3))), value)


def fast_local(
    tokens, documents, expert_routes, drop_rank, norm1_gain, query_weight, key_weight,
    value_weight, out_weight, norm2_gain, router_weight, gate_weight, up_weight, down_weight,
    output_grad,
):
    fsdp = lax.axis_index("fsdp")
    seq = lax.axis_index("sp")
    me = jnp.reshape(fsdp, (1,)).astype(jnp.int32)
    small = jnp.concatenate(
        [
            router_weight,
            norm1_gain[:, None],
            norm2_gain[:, None],
            jnp.zeros((128, 94), BF),
        ],
        axis=1,
    )
    shard = jnp.concatenate(
        [query_weight, key_weight, value_weight, small, out_weight], axis=1
    )
    project_pieces = spread(shard)

    slots, routed = dense_slots(expert_routes, drop_rank, 32)
    mixture_grad = (branch_scale * output_grad.astype(F32)).astype(BF)
    grad_payload = jnp.concatenate(
        [mixture_grad, jnp.concatenate([slots[:16], slots[16:]], axis=1)], axis=0
    )

    block_start = fsdp * 2048
    position_all = doc_position(documents)
    position_span = lax.dynamic_slice_in_dim(position_all, block_start, 2048)
    position = lax.dynamic_slice_in_dim(position_span, seq * 512, 512)
    cosine, sine_table = rope_tables(position, HD)
    cosine = jnp.tile(cosine, (1, 2))
    signs = jnp.where(jnp.arange(128) % HD < HD // 2, -1.0, 1.0).astype(F32)
    sine = jnp.tile(sine_table, (1, 2)) * signs[None, :]
    start = HALO + jnp.arange(2048, dtype=jnp.int32) - position_span
    start_rows = start.reshape(2048 // QB, 1, QB)
    low_block = start_rows[:, 0, 0] // KB
    low_back = start_rows[:, 0, 0] // BACK_KB

    first, second, extra = project(me, tokens, cosine, sine, project_pieces)
    grad_payload = hold(grad_payload, project_pieces[6], project_pieces[7])
    own, beside = grad_payload, flip(grad_payload, 1)
    along_x, along_y = flip(grad_payload, 2), flip(grad_payload, 4)
    heads = [across(first.reshape(2048, 256)), None]
    heads[0], second, beside, along_x, along_y = lax.optimization_barrier(
        (heads[0], second, beside, along_x, along_y)
    )
    heads[1] = across(second.reshape(2048, 256))
    halos = [from_behind(heads[0][:, 128:256], "fsdp", 1), None]
    near_pieces = (own, beside, along_x, flip(along_x, 1), along_y, flip(along_y, 1))
    blended, logs = [None, None], [None, None]
    blended[0], logs[0] = attend(low_block, heads[0], halos[0], start_rows)
    blended[0], heads[1] = lax.optimization_barrier((blended[0], heads[1]))
    halos[1] = from_behind(heads[1][:, 128:256], "fsdp", 1)
    first_back = across(blended[0])
    near, far = (0, 1, 2, 3, 4, 5), (6, 7)
    near_grads = pick_grads(me, near, near_pieces)
    halos[1], near_grads = lax.optimization_barrier((halos[1], near_grads))
    diagonal = spread_diagonal(near_pieces)
    blended[1], logs[1] = attend(low_block, heads[1], halos[1], start_rows)
    blended[1], first_back, diagonal = lax.optimization_barrier(
        (blended[1], first_back, diagonal)
    )
    attended = [first_back, across(blended[1])]
    far_grads = pick_grads(me, far, spread_far(diagonal))
    all_slot_columns = jnp.concatenate([near_grads[2], far_grads[2]], axis=0)
    attended, near_grads, far_grads, all_slot_columns = lax.optimization_barrier(
        (attended, near_grads, far_grads, all_slot_columns)
    )
    attended = [part.reshape(4, 512, 128) for part in attended]
    grad_rows, slot_rows, _ = zip(near_grads, far_grads)
    hidden_one, payload, gates = after_attention(
        me, tokens, attended, extra, routed, project_pieces
    )
    near_pieces = spread_near(payload)
    diagonal = spread_diagonal(near_pieces)
    near_rows = pick_rows(me, slot_rows[0], near, near_pieces)
    near_rows, diagonal = lax.optimization_barrier((near_rows, diagonal))
    far_rows = pick_rows(me, slot_rows[1], far, spread_far(diagonal))
    rows, slot_gates, gate_columns = zip(near_rows, far_rows)
    mats = (gate_weight, up_weight, down_weight)
    lin_grads, inners, parts = zip(
        *[expert_grads(base, 2, rows, grad_rows, slot_gates, *mats) for base in (0, 2)]
    )
    sums_of_parts = lax.psum(parts, "sp")

    def finish(turn_number, _):
        here, slot_columns = hold((me, all_slot_columns), turn_number)
        outs, in_grads, marks = zip(
            *[
                expert_rows(here, 2 * pair, 2, lin_grads[pair], inners[pair], grad_rows, *mats)
                for pair in range(2)
            ]
        )
        odd = combine(1, slot_columns, None, in_grads, marks)
        even = combine(0, slot_columns, None, in_grads, marks)
        sums = collect(odd, even)
        hidden_grad, branch_grad, first_grad, second_grad, small_grads = back_to_attention(
            me, sums, hidden_one, output_grad, payload, gates, extra, project_pieces
        )
        first_heads = across(first_grad.reshape(2048, 128))
        first_heads, second_grad = lax.optimization_barrier((first_heads, second_grad))
        second_heads = across(second_grad.reshape(2048, 128))
        first_own, first_halo = attend_back(
            low_back, heads[0], halos[0], start_rows, blended[0], first_heads, logs[0]
        )
        first_own, first_halo, second_heads = lax.optimization_barrier(
            (first_own, first_halo, second_heads)
        )
        held_outs, held_gates = hold((outs, gate_columns), first_heads)
        held_gates = jnp.concatenate(held_gates, axis=0)
        odd_mix = combine(1, slot_columns, held_gates, held_outs, ())
        even_mix = combine(0, slot_columns, held_gates, held_outs, ())
        mixture = collect(odd_mix, even_mix)
        output = (
            hidden_one
            + branch_scale
            * (mixture[0].astype(F32) + mixture[1].astype(F32) + mixture[2].astype(F32))
        ).astype(BF)
        out_sums = collect(*out_grads_of(me, attended, branch_grad, small_grads))

        def grads_home(own_grad, halo_grad):
            returned = from_behind(halo_grad, "fsdp", -1).astype(F32)
            own_grad = own_grad + jnp.pad(returned, ((0, 0), (128, 0)))
            return across(own_grad.astype(BF)).reshape(4, 512, 256)

        first_home = grads_home(first_own, first_halo)
        second_own, second_halo = attend_back(
            low_back, heads[1], halos[1], start_rows, blended[1], second_heads, logs[1]
        )
        second_own, second_halo, first_home = lax.optimization_barrier(
            (second_own, second_halo, first_home)
        )
        second_home = grads_home(second_own, second_halo)
        input_grad, odd_in, even_in = input_grads(
            me, tokens, cosine, sine, first_home, second_home, extra, hidden_grad, project_pieces
        )
        in_sums = collect(odd_in, even_in)

        out_shard = sum(term.astype(F32) for term in out_sums).astype(BF)
        in_shard = sum(term.astype(F32) for term in in_sums).astype(BF)
        in_total = sum_shared(in_shard).astype(F32)
        out_total = sum_line(out_shard, seq).astype(F32)
        return (
            output,
            input_grad,
            in_total[:, 2048],
            in_total[:, 0:1024],
            in_total[:, 1024:1536],
            in_total[:, 1536:2048],
            out_total[:, 0:1024],
            out_total[:, 1056],
            out_total[:, 1024:1056],
        )

    rounds = 1 + (documents[0] > 0).astype(jnp.int32)
    results = lax.fori_loop(
        0,
        rounds,
        finish,
        (
            jnp.zeros((512, 1024), BF),
            jnp.zeros((512, 1024), BF),
            jnp.zeros((128,), F32),
            jnp.zeros((128, 1024), F32),
            jnp.zeros((128, 512), F32),
            jnp.zeros((128, 512), F32),
            jnp.zeros((128, 1024), F32),
            jnp.zeros((128,), F32),
            jnp.zeros((128, 32), F32),
        ),
    )
    sums_of_parts = [
        total[first : first + 3072] for total in sums_of_parts for first in (0, 3072)
    ]
    stacked = [
        jnp.stack([total[0:1024] for total in sums_of_parts]).astype(F32),
        jnp.stack([total[1024:2048] for total in sums_of_parts]).astype(F32),
        jnp.stack(
            [
                jnp.concatenate([total[2048:2560], total[2560:3072]], axis=1)
                for total in sums_of_parts
            ]
        ).astype(F32),
    ]
    return (*results, *stacked)


def solution(mesh):
    placed = (
        P(("fsdp", "sp"), None),
        P(),
        P(("fsdp", "sp"), None),
        P(("fsdp", "sp"), None),
        P("fsdp"),
        P("fsdp", None),
        P("fsdp", None),
        P("fsdp", None),
        P("fsdp", None),
        P("fsdp"),
        P("fsdp", None),
        P("fsdp", None, None),
        P("fsdp", None, None),
        P("fsdp", None, None),
        P(("fsdp", "sp"), None),
    )
    fast = mesh.shape["sp"] == 4 and mesh.shape["fsdp"] == 8
    return jax.shard_map(
        fast_local if fast else local,
        mesh=mesh,
        in_specs=placed,
        out_specs=(
            P(("fsdp", "sp"), None),
            P(("fsdp", "sp"), None),
            P("fsdp"),
            P("fsdp", None),
            P("fsdp", None),
            P("fsdp", None),
            P("fsdp", None),
            P("fsdp"),
            P("fsdp", None),
            P("fsdp", None, None),
            P("fsdp", None, None),
            P("fsdp", None, None),
        ),
        check_vma=False,
    )
```

```python
import functools

import jax
import jax.numpy as jnp
from jax import lax
from jax.sharding import PartitionSpec as P
from jax.experimental import pallas as pl
from jax.experimental.pallas import tpu as pltpu

HD = 64
DOC_CAP = 2048


attend_scale = 0.015625
branch_scale = 0.22
norm_eps = 1e-06
rope_base = 10000.0
masked_score = -1e30


def from_behind(value, axis, steps):
    count = lax.axis_size(axis)
    initial, last = (max(0, -steps), min(count, count - steps))
    return lax.ppermute(value, axis, [(source, source + steps) for source in range(initial, last)])


def doc_position(documents):
    length = documents.shape[0]
    place = jnp.arange(length, dtype=jnp.int32)
    fresh = jnp.concatenate([jnp.ones((1,), dtype=bool), documents[1:] != documents[:-1]])
    opening = lax.cummax(jnp.where(fresh, place, 0), axis=0)
    return place - opening


def rope_tables(position, head_size):
    half_size = head_size // 2
    spacing = jnp.arange(half_size, dtype=jnp.float32)
    inverse = rope_base ** (-2.0 * spacing / head_size)
    angle = position.astype(jnp.float32)[:, None] * inverse[None, :]
    return (jnp.tile(jnp.cos(angle), (1, 2)), jnp.tile(jnp.sin(angle), (1, 2)))


def rotate(values, cosine, sine_table):
    half_size = values.shape[-1] // 2
    turned = jnp.concatenate([-values[..., half_size:], values[..., :half_size]], axis=-1)
    return values * cosine[:, None, :] + turned * sine_table[:, None, :]


def route_slots(routes, rank_table, experts, capacity):
    flat_routes = routes.reshape(-1)
    flat_ranks = rank_table.reshape(-1)
    ordered = flat_routes[jnp.argsort(flat_ranks)]
    onehot = (ordered[:, None] == jnp.arange(experts, dtype=jnp.int32)[None, :]).astype(jnp.int32)
    earlier = jnp.cumsum(onehot, axis=0) - onehot
    slot_sorted = jnp.sum(earlier * onehot, axis=1)
    slot_number = slot_sorted[flat_ranks].reshape(routes.shape)
    kept_pair = slot_number < capacity
    return (jnp.where(kept_pair, routes * capacity + slot_number, -1), kept_pair)


def to_owner(values):
    return lax.all_to_all(values, "fsdp", split_axis=0, concat_axis=1, tiled=True)


def from_owner(values):
    return lax.all_to_all(values, "fsdp", split_axis=1, concat_axis=0, tiled=True)


def expert_forward(slot_rows, gate_mats, up_mats, down_mats):
    gate_lin = jnp.einsum("nrd,ndf->nrf", slot_rows, gate_mats, preferred_element_type=jnp.float32)
    up_lin = jnp.einsum("nrd,ndf->nrf", slot_rows, up_mats, preferred_element_type=jnp.float32)
    inner = (gate_lin * jax.nn.sigmoid(gate_lin) * up_lin).astype(jnp.bfloat16)
    result = jnp.einsum(
        "nrf,nfd->nrd", inner, down_mats, preferred_element_type=jnp.float32
    ).astype(jnp.bfloat16)
    return (gate_lin, up_lin, result)


def expert_backward(slot_rows, gate_lin, up_lin, result_grad, gate_mats, up_mats, down_mats):
    sigma = jax.nn.sigmoid(gate_lin)
    swished = gate_lin * sigma
    inner = (swished * up_lin).astype(jnp.bfloat16)
    inner_grad = jnp.einsum(
        "nrd,nfd->nrf", result_grad, down_mats, preferred_element_type=jnp.float32
    )
    gate_grad = (inner_grad * up_lin * sigma * (1.0 + gate_lin * (1.0 - sigma))).astype(
        jnp.bfloat16
    )
    up_grad = (inner_grad * swished).astype(jnp.bfloat16)
    rows_grad = jnp.einsum("nrf,ndf->nrd", gate_grad, gate_mats, preferred_element_type=jnp.float32)
    rows_grad = (
        rows_grad + jnp.einsum("nrf,ndf->nrd", up_grad, up_mats, preferred_element_type=jnp.float32)
    ).astype(jnp.bfloat16)
    gate_part = jnp.einsum("nrd,nrf->ndf", slot_rows, gate_grad, preferred_element_type=jnp.float32)
    up_part = jnp.einsum("nrd,nrf->ndf", slot_rows, up_grad, preferred_element_type=jnp.float32)
    down_part = jnp.einsum("nrf,nrd->nfd", inner, result_grad, preferred_element_type=jnp.float32)
    return (rows_grad, gate_part, up_part, down_part)


def local(
    tokens,
    documents,
    expert_routes,
    drop_rank,
    norm1_gain,
    query_weight,
    key_weight,
    value_weight,
    out_weight,
    norm2_gain,
    router_weight,
    gate_weight,
    up_weight,
    down_weight,
    output_grad,
):
    rows_dev, model_width = tokens.shape
    heads_query = query_weight.shape[1] // HD
    heads_kv = key_weight.shape[1] // HD
    repeat = heads_query // heads_kv
    experts = router_weight.shape[1]
    top_count = expert_routes.shape[1]
    seq_parts = lax.axis_size("sp")
    span_rows = seq_parts * rows_dev
    query_block = min(512, span_rows)
    block_count = span_rows // query_block
    doc_most = min(DOC_CAP, span_rows)
    window = doc_most + query_block
    capacity = (9 * rows_dev * top_count + 8 * experts - 1) // (8 * experts)
    slot_total = experts * capacity
    block_start = lax.axis_index("fsdp") * span_rows
    row_start = block_start + lax.axis_index("sp") * rows_dev
    position = lax.dynamic_slice_in_dim(doc_position(documents), row_start, rows_dev)
    cosine, sine_table = rope_tables(position, HD)
    gain_first, query_mat, key_mat, value_mat, out_mat, gain_second, router_mat = (
        lax.all_gather(norm1_gain, "fsdp", axis=0, tiled=True),
        lax.all_gather(query_weight, "fsdp", axis=0, tiled=True),
        lax.all_gather(key_weight, "fsdp", axis=0, tiled=True),
        lax.all_gather(value_weight, "fsdp", axis=0, tiled=True),
        lax.all_gather(out_weight, "fsdp", axis=0, tiled=True),
        lax.all_gather(norm2_gain, "fsdp", axis=0, tiled=True),
        lax.all_gather(router_weight, "fsdp", axis=0, tiled=True),
    )
    stream = tokens.astype(jnp.float32)
    inverse_one = lax.rsqrt(jnp.mean(stream * stream, axis=-1, keepdims=True) + norm_eps)
    gain_one = gain_first.astype(jnp.float32)
    normed_one = (stream * inverse_one * gain_one).astype(jnp.bfloat16)
    query_lin = jnp.dot(normed_one, query_mat, preferred_element_type=jnp.float32).reshape(
        rows_dev, heads_query, HD
    )
    key_lin = jnp.dot(normed_one, key_mat, preferred_element_type=jnp.float32).reshape(
        rows_dev, heads_kv, HD
    )
    value_low = (
        jnp.dot(normed_one, value_mat, preferred_element_type=jnp.float32)
        .astype(jnp.bfloat16)
        .reshape(rows_dev, heads_kv, HD)
    )
    query_low = (
        rotate(query_lin, cosine, sine_table)
        .astype(jnp.bfloat16)
        .reshape(rows_dev, heads_kv, repeat * HD)
    )
    key_low = rotate(key_lin, cosine, sine_table).astype(jnp.bfloat16)
    packed = jnp.concatenate([query_low, key_low, value_low], axis=-1)
    by_heads = lax.all_to_all(packed, "sp", split_axis=1, concat_axis=0, tiled=True)
    groups = by_heads.shape[1]
    query_heads = by_heads[:, :, : repeat * HD]
    pair_heads = by_heads[:, :, repeat * HD :]
    halo_rows = from_behind(pair_heads[span_rows - doc_most :], "fsdp", 1)
    near_pairs = jnp.concatenate([halo_rows, pair_heads], axis=0)
    query_docs = lax.dynamic_slice_in_dim(documents, block_start, span_rows)
    near_docs = lax.dynamic_slice_in_dim(
        jnp.concatenate([jnp.full((doc_most,), -1, jnp.int32), documents]),
        block_start,
        doc_most + span_rows,
    )
    causal = jnp.arange(window)[None, :] <= jnp.arange(query_block)[:, None] + doc_most

    def block_scores(block_index):
        first_row = block_index * query_block
        query_part = lax.dynamic_slice_in_dim(query_heads, first_row, query_block).reshape(
            query_block, groups, repeat, HD
        )
        pair_part = lax.dynamic_slice_in_dim(near_pairs, first_row, window)
        key_part = pair_part[:, :, :HD]
        value_part = pair_part[:, :, HD:]
        own_docs = lax.dynamic_slice_in_dim(query_docs, first_row, query_block)
        seen_docs = lax.dynamic_slice_in_dim(near_docs, first_row, window)
        allowed = (seen_docs[None, :] == own_docs[:, None]) & causal
        scores = attend_scale * jnp.einsum(
            "rgjd,cgd->gjrc", query_part, key_part, preferred_element_type=jnp.float32
        )
        return (query_part, key_part, value_part, jnp.where(allowed, scores, masked_score))

    def attend_block(block_index):
        query_part, key_part, value_part, scores = block_scores(block_index)
        row_max = jnp.max(scores, axis=-1, keepdims=True)
        exponent = jnp.exp(scores - row_max)
        row_total = jnp.sum(exponent, axis=-1, keepdims=True)
        softmaxed = (exponent / row_total).astype(jnp.bfloat16)
        blended = jnp.einsum(
            "gjrc,cgd->rgjd", softmaxed, value_part, preferred_element_type=jnp.float32
        )
        return (
            blended.astype(jnp.bfloat16).reshape(query_block, groups, repeat * HD),
            (row_max + jnp.log(row_total))[..., 0],
        )

    blended_all, log_totals = lax.map(attend_block, jnp.arange(block_count, dtype=jnp.int32))
    attended = lax.all_to_all(
        blended_all.reshape(span_rows, groups, repeat * HD),
        "sp",
        split_axis=0,
        concat_axis=1,
        tiled=True,
    ).reshape(rows_dev, heads_query * HD)
    branch = jnp.dot(attended, out_mat, preferred_element_type=jnp.float32)
    hidden_one = stream + branch_scale * branch
    inverse_two = lax.rsqrt(jnp.mean(hidden_one * hidden_one, axis=-1, keepdims=True) + norm_eps)
    gain_two = gain_second.astype(jnp.float32)
    normed_two = (hidden_one * inverse_two * gain_two).astype(jnp.bfloat16)
    logits = jnp.dot(normed_two, router_mat, preferred_element_type=jnp.float32)
    route_hot = expert_routes[:, :, None] == jnp.arange(experts, dtype=jnp.int32)[None, None, :]
    chosen = jnp.sum(jnp.where(route_hot, logits[:, None, :], 0.0), axis=-1)
    chosen_max = jnp.max(chosen, axis=-1, keepdims=True)
    gate_exp = jnp.exp(chosen - chosen_max)
    gates = gate_exp / jnp.sum(gate_exp, axis=-1, keepdims=True)
    gate_low = gates.astype(jnp.bfloat16)
    slot_index, kept_pair = route_slots(expert_routes, drop_rank, experts, capacity)
    columns = jnp.arange(slot_total, dtype=jnp.int32)[None, :]
    dispatch = jnp.zeros((rows_dev, slot_total), dtype=bool)
    combine = jnp.zeros((rows_dev, slot_total), dtype=jnp.bfloat16)
    for route_slot in range(top_count):
        landing = slot_index[:, route_slot : route_slot + 1] == columns
        dispatch = dispatch | landing
        combine = combine + jnp.where(
            landing, gate_low[:, route_slot : route_slot + 1], jnp.zeros((), jnp.bfloat16)
        )
    dispatch_low = dispatch.astype(jnp.bfloat16)
    expert_in = (
        jnp.einsum("tc,td->cd", dispatch_low, normed_two, preferred_element_type=jnp.float32)
        .astype(jnp.bfloat16)
        .reshape(experts, capacity, model_width)
    )
    owned_in = to_owner(expert_in)
    gate_lin, up_lin, owned_out = expert_forward(owned_in, gate_weight, up_weight, down_weight)
    expert_out = from_owner(owned_out)
    mixture = jnp.dot(
        combine, expert_out.reshape(slot_total, model_width), preferred_element_type=jnp.float32
    )
    output = (hidden_one + branch_scale * mixture).astype(jnp.bfloat16)
    cotangent = output_grad.astype(jnp.float32)
    mixture_grad = (branch_scale * cotangent).astype(jnp.bfloat16)
    out_grad = (
        jnp.einsum("tc,td->cd", combine, mixture_grad, preferred_element_type=jnp.float32)
        .astype(jnp.bfloat16)
        .reshape(experts, capacity, model_width)
    )
    taken = jnp.take(
        expert_out.reshape(slot_total, model_width), jnp.clip(slot_index, 0, slot_total - 1), axis=0
    )
    gate_grad = jnp.where(
        kept_pair,
        jnp.einsum("tkd,td->tk", taken, mixture_grad, preferred_element_type=jnp.float32),
        0.0,
    )
    chosen_grad = gates * (gate_grad - jnp.sum(gates * gate_grad, axis=-1, keepdims=True))
    logit_grad = jnp.sum(jnp.where(route_hot, chosen_grad[:, :, None], 0.0), axis=1).astype(
        jnp.bfloat16
    )
    router_grad = jnp.einsum(
        "td,te->de", normed_two, logit_grad, preferred_element_type=jnp.float32
    )
    normed_two_grad = jnp.einsum(
        "te,de->td", logit_grad, router_mat, preferred_element_type=jnp.float32
    )
    owned_grad = to_owner(out_grad)
    owned_in_grad, expert_gate_grad, expert_up_grad, expert_down_grad = expert_backward(
        owned_in, gate_lin, up_lin, owned_grad, gate_weight, up_weight, down_weight
    )
    expert_in_grad = from_owner(owned_in_grad)
    normed_two_grad = normed_two_grad + jnp.dot(
        dispatch_low,
        expert_in_grad.reshape(slot_total, model_width),
        preferred_element_type=jnp.float32,
    )
    scaled_two = normed_two_grad * gain_two
    hidden_grad = (
        cotangent
        + inverse_two * scaled_two
        - hidden_one * inverse_two**3 * jnp.mean(hidden_one * scaled_two, axis=-1, keepdims=True)
    )
    norm_two_grad = jnp.sum(normed_two_grad * hidden_one * inverse_two, axis=0)
    branch_grad = (branch_scale * hidden_grad).astype(jnp.bfloat16)
    out_mat_grad = jnp.einsum(
        "tk,td->kd", attended, branch_grad, preferred_element_type=jnp.float32
    )
    attended_grad = jnp.einsum(
        "td,kd->tk", branch_grad, out_mat, preferred_element_type=jnp.float32
    ).astype(jnp.bfloat16)
    grad_heads = lax.all_to_all(
        attended_grad.reshape(rows_dev, heads_kv, repeat * HD),
        "sp",
        split_axis=1,
        concat_axis=0,
        tiled=True,
    )

    def attend_back(accumulated, block_item):
        block_index, log_total = block_item
        query_part, key_part, value_part, scores = block_scores(block_index)
        first_row = block_index * query_block
        softmaxed = jnp.exp(scores - log_total[..., None])
        incoming = lax.dynamic_slice_in_dim(grad_heads, first_row, query_block).reshape(
            query_block, groups, repeat, HD
        )
        softmax_grad = jnp.einsum(
            "rgjd,cgd->gjrc", incoming, value_part, preferred_element_type=jnp.float32
        )
        centred = jnp.sum(softmaxed * softmax_grad, axis=-1, keepdims=True)
        score_grad = (softmaxed * (softmax_grad - centred)).astype(jnp.bfloat16)
        query_grad = attend_scale * jnp.einsum(
            "gjrc,cgd->rgjd", score_grad, key_part, preferred_element_type=jnp.float32
        )
        key_grad = attend_scale * jnp.einsum(
            "gjrc,rgjd->cgd", score_grad, query_part, preferred_element_type=jnp.float32
        )
        value_grad = jnp.einsum(
            "gjrc,rgjd->cgd",
            softmaxed.astype(jnp.bfloat16),
            incoming,
            preferred_element_type=jnp.float32,
        )
        current = lax.dynamic_slice_in_dim(accumulated, first_row, window)
        updated = lax.dynamic_update_slice_in_dim(
            accumulated, current + jnp.concatenate([key_grad, value_grad], axis=-1), first_row, 0
        )
        return (updated, query_grad.reshape(query_block, groups, repeat * HD))

    pair_grad, query_grads = lax.scan(
        attend_back,
        jnp.zeros((doc_most + span_rows, groups, 2 * HD), jnp.float32),
        (jnp.arange(block_count, dtype=jnp.int32), log_totals),
    )
    returned = from_behind(pair_grad[:doc_most].astype(jnp.bfloat16), "fsdp", -1).astype(
        jnp.float32
    )
    own_grad = pair_grad[doc_most:]
    own_grad = jnp.concatenate(
        [own_grad[: span_rows - doc_most], own_grad[span_rows - doc_most :] + returned], axis=0
    )
    packed_grad = jnp.concatenate(
        [
            query_grads.reshape(span_rows, groups, repeat * HD).astype(jnp.bfloat16),
            own_grad.astype(jnp.bfloat16),
        ],
        axis=-1,
    )
    by_tokens = lax.all_to_all(packed_grad, "sp", split_axis=0, concat_axis=1, tiled=True)
    query_rot_grad = (
        by_tokens[:, :, : repeat * HD].astype(jnp.float32).reshape(rows_dev, heads_query, HD)
    )
    key_rot_grad = by_tokens[:, :, repeat * HD : (repeat + 1) * HD].astype(jnp.float32)
    value_grad_low = by_tokens[:, :, (repeat + 1) * HD :].reshape(rows_dev, heads_kv * HD)
    query_lin_grad = (
        rotate(query_rot_grad, cosine, -sine_table)
        .astype(jnp.bfloat16)
        .reshape(rows_dev, heads_query * HD)
    )
    key_lin_grad = (
        rotate(key_rot_grad, cosine, -sine_table)
        .astype(jnp.bfloat16)
        .reshape(rows_dev, heads_kv * HD)
    )
    query_mat_grad = jnp.einsum(
        "td,tk->dk", normed_one, query_lin_grad, preferred_element_type=jnp.float32
    )
    key_mat_grad = jnp.einsum(
        "td,tk->dk", normed_one, key_lin_grad, preferred_element_type=jnp.float32
    )
    value_mat_grad = jnp.einsum(
        "td,tk->dk", normed_one, value_grad_low, preferred_element_type=jnp.float32
    )
    normed_one_grad = jnp.einsum(
        "tk,dk->td", query_lin_grad, query_mat, preferred_element_type=jnp.float32
    )
    normed_one_grad = normed_one_grad + jnp.einsum(
        "tk,dk->td", key_lin_grad, key_mat, preferred_element_type=jnp.float32
    )
    normed_one_grad = normed_one_grad + jnp.einsum(
        "tk,dk->td", value_grad_low, value_mat, preferred_element_type=jnp.float32
    )
    scaled_one = normed_one_grad * gain_one
    input_grad = (
        hidden_grad
        + inverse_one * scaled_one
        - stream * inverse_one**3 * jnp.mean(stream * scaled_one, axis=-1, keepdims=True)
    ).astype(jnp.bfloat16)
    norm_one_grad = jnp.sum(normed_one_grad * stream * inverse_one, axis=0)
    shard_norm_one, shard_query, shard_key, shard_value, shard_out, shard_norm_two, shard_router = (
        lax.psum_scatter(
            norm_one_grad.astype(jnp.bfloat16), "fsdp", scatter_dimension=0, tiled=True
        ).astype(jnp.float32),
        lax.psum_scatter(
            query_mat_grad.astype(jnp.bfloat16), "fsdp", scatter_dimension=0, tiled=True
        ).astype(jnp.float32),
        lax.psum_scatter(
            key_mat_grad.astype(jnp.bfloat16), "fsdp", scatter_dimension=0, tiled=True
        ).astype(jnp.float32),
        lax.psum_scatter(
            value_mat_grad.astype(jnp.bfloat16), "fsdp", scatter_dimension=0, tiled=True
        ).astype(jnp.float32),
        lax.psum_scatter(
            out_mat_grad.astype(jnp.bfloat16), "fsdp", scatter_dimension=0, tiled=True
        ).astype(jnp.float32),
        lax.psum_scatter(
            norm_two_grad.astype(jnp.bfloat16), "fsdp", scatter_dimension=0, tiled=True
        ).astype(jnp.float32),
        lax.psum_scatter(
            router_grad.astype(jnp.bfloat16), "fsdp", scatter_dimension=0, tiled=True
        ).astype(jnp.float32),
    )
    (
        summed_norm_one,
        summed_query,
        summed_key,
        summed_value,
        summed_out,
        summed_norm_two,
        summed_router,
        summed_gate,
        summed_up,
        summed_down,
    ) = (
        lax.psum(shard_norm_one.astype(jnp.bfloat16), "sp").astype(jnp.float32),
        lax.psum(shard_query.astype(jnp.bfloat16), "sp").astype(jnp.float32),
        lax.psum(shard_key.astype(jnp.bfloat16), "sp").astype(jnp.float32),
        lax.psum(shard_value.astype(jnp.bfloat16), "sp").astype(jnp.float32),
        lax.psum(shard_out.astype(jnp.bfloat16), "sp").astype(jnp.float32),
        lax.psum(shard_norm_two.astype(jnp.bfloat16), "sp").astype(jnp.float32),
        lax.psum(shard_router.astype(jnp.bfloat16), "sp").astype(jnp.float32),
        lax.psum(expert_gate_grad.astype(jnp.bfloat16), "sp").astype(jnp.float32),
        lax.psum(expert_up_grad.astype(jnp.bfloat16), "sp").astype(jnp.float32),
        lax.psum(expert_down_grad.astype(jnp.bfloat16), "sp").astype(jnp.float32),
    )
    return (
        output,
        input_grad,
        summed_norm_one,
        summed_query,
        summed_key,
        summed_value,
        summed_out,
        summed_norm_two,
        summed_router,
        summed_gate,
        summed_up,
        summed_down,
    )


BF = jnp.bfloat16
F32 = jnp.float32
LOG2E = 1.4426950408889634
QB = 512
KB = 512
BACK_KB = 256
HALO = 2048
VMEM_MOST = 60 * 1024 * 1024


def in_vmem(count):
    return [pl.BlockSpec(memory_space=pltpu.VMEM)] * count


def in_hbm(count):
    return [pl.BlockSpec(memory_space=pl.ANY)] * count


def in_smem():
    return pl.BlockSpec(memory_space=pltpu.SMEM)


def shaped(shape, kind):
    return jax.ShapeDtypeStruct(shape, kind)


def params():
    return pltpu.CompilerParams(vmem_limit_bytes=VMEM_MOST)


def cost(flops, moved, transcendentals=0):
    return pl.CostEstimate(
        flops=int(flops), bytes_accessed=int(moved), transcendentals=int(transcendentals)
    )


def nn(left, right):
    return lax.dot_general(left, right, (((1,), (0,)), ((), ())), preferred_element_type=F32)


def nt(left, right):
    return lax.dot_general(left, right, (((1,), (1,)), ((), ())), preferred_element_type=F32)


def tn(left, right):
    return lax.dot_general(left, right, (((0,), (0,)), ((), ())), preferred_element_type=F32)


def flip(value, bit):
    return lax.ppermute(value, "fsdp", [(place, place ^ bit) for place in range(8)])


def half_rows(rows):
    return (rows // 2 + 15) // 16 * 16


def plan_of(rows):
    half = half_rows(rows)
    return (
        (0, 0, rows),
        (1, 0, rows),
        (2, 0, rows),
        (3, 0, rows),
        (4, 0, rows),
        (5, 0, rows),
        (6, 0, half),
        (6, half, rows - half),
        (7, 0, half),
        (7, half, rows - half),
    )


def hold(value, *others):
    return lax.optimization_barrier((value, others))[0]


def spread_near(own):
    along_x, along_y = flip(own, 2), flip(own, 4)
    return (own, flip(own, 1), along_x, flip(along_x, 1), along_y, flip(along_y, 1))


def spread_diagonal(near):
    half = half_rows(near[0].shape[0])
    return (flip(near[4][:half], 2), flip(near[2][half:], 4))


def spread_far(diagonal):
    return (*diagonal, flip(diagonal[0], 1), flip(diagonal[1], 1))


def spread(own):
    near = spread_near(own)
    return near + spread_far(spread_diagonal(near))


def add_low(left, right):
    return (left.astype(F32) + right.astype(F32)).astype(BF)


def collect(odd, even, tick=None):
    half = half_rows(even.shape[1])
    received = flip(odd, 1)
    diagonal_low = flip(add_low(even[3, :half], received[3, :half]), 2)
    diagonal_high = flip(add_low(even[3, half:], received[3, half:]), 4)
    if tick is not None:
        diagonal_low, diagonal_high = tick((diagonal_low, diagonal_high))
    own = add_low(even[0], received[0])
    for_y = even[2].astype(F32) + received[2].astype(F32)
    for_x = even[1].astype(F32) + received[1].astype(F32)
    for_y = jnp.concatenate([for_y[:half] + diagonal_low.astype(F32), for_y[half:]]).astype(BF)
    for_x = jnp.concatenate([for_x[:half], for_x[half:] + diagonal_high.astype(F32)]).astype(BF)
    return (own, flip(for_x, 2), flip(for_y, 4))


def start_fetch(me, plan, sources, target, block_rows, sems):
    copies = []
    for number, (partner, first, rows) in enumerate(plan):
        start = pl.multiple_of((me ^ partner) * block_rows + first, 64)
        copies.append(
            pltpu.make_async_copy(
                sources[number].at[:, pl.ds(0, 2176)],
                target.at[pl.ds(start, rows)],
                sems.at[number],
            )
        )
        copies[-1].start()
    return copies


def start_fetch_out(me, plan, sources, target, sems):
    copies = []
    for number, (partner, first, rows) in enumerate(plan):
        start = pl.multiple_of((me ^ partner) * 128 + first, 64)
        copies.append(
            pltpu.make_async_copy(
                sources[number].at[:, pl.ds(2176, 1024)],
                target.at[pl.ds(start, rows)],
                sems.at[number],
            )
        )
        copies[-1].start()
    return copies


def turn(values, cosine, sine):
    lane = lax.broadcasted_iota(jnp.int32, values.shape, 1)
    other = jnp.where(
        lane % HD < HD // 2, pltpu.roll(values, 128 - HD // 2, 1), pltpu.roll(values, HD // 2, 1)
    )
    return values * cosine + other * sine


def side_by_side(left, right, group):
    lane = lax.broadcasted_iota(jnp.int32, left.shape, 1)
    if group == 0:
        return jnp.where(lane < HD, left, pltpu.roll(right, HD, 1))
    return jnp.where(lane < HD, pltpu.roll(left, HD, 1), right)


def project_kernel(plan, me_ref, tokens_ref, cos_ref, sin_ref, *refs):
    count = len(plan)
    first_ref, second_ref, extra_ref, mats, sems = refs[count:]
    copies = start_fetch(me_ref[0], plan, refs[:count], mats, 128, sems)
    stream = tokens_ref[...].astype(F32)
    scaled = stream * lax.rsqrt(jnp.mean(stream * stream, axis=-1, keepdims=True) + norm_eps)
    for copy in copies:
        copy.wait()
    extra = mats[:, 2048:2176].astype(F32).T
    extra_ref[...] = extra[:48].astype(BF)
    normed = (scaled * extra[32:33]).astype(BF)
    cosine, sine = cos_ref[...], sin_ref[...]
    for part in range(4):
        query = nn(normed, mats[:, part * 256 : part * 256 + 256])
        key = turn(nn(normed, mats[:, 1024 + part * 128 : 1152 + part * 128]), cosine, sine)
        value = nn(normed, mats[:, 1536 + part * 128 : 1664 + part * 128])
        for group, target in enumerate((first_ref, second_ref)):
            target[part, :, 0:128] = turn(
                query[:, group * 128 : group * 128 + 128], cosine, sine
            ).astype(BF)
            target[part, :, 128:256] = side_by_side(key, value, group).astype(BF)


def project(me, tokens, cosine, sine, pieces):
    plan = plan_of(128)
    return pl.pallas_call(
        functools.partial(project_kernel, plan),
        out_shape=(
            shaped((4, 512, 256), BF),
            shaped((4, 512, 256), BF),
            shaped((48, 1024), BF),
        ),
        in_specs=[in_smem()] + in_vmem(3) + in_hbm(len(plan)),
        out_specs=tuple(in_vmem(3)),
        scratch_shapes=[pltpu.VMEM((1024, 2176), BF), pltpu.SemaphoreType.DMA((len(plan),))],
        compiler_params=params(),
        cost_estimate=cost(2 * 512 * 1024 * 2048, 9e6),
        name="project",
    )(me, tokens, cosine, sine, *pieces)


def placed(values, half, side):
    moved = values.astype(F32)
    if half != side:
        moved = pltpu.roll(moved, HD, 1)
    lane = lax.broadcasted_iota(jnp.int32, values.shape, 1)
    return jnp.where((lane < HD) == (side == 0), moved, 0.0).astype(values.dtype)


def allowed_pairs(first, rows, step, start):
    key_at = first + lax.broadcasted_iota(jnp.int32, (rows, QB), 0)
    query_at = HALO + step * QB + lax.broadcasted_iota(jnp.int32, (rows, QB), 1)
    return (key_at >= start) & (key_at <= query_at)


def attend_kernel(
    low_ref, own_ref, halo_ref, start_ref, out_ref, log_ref, pairs, pairs_t, most, total, blend
):
    step = pl.program_id(0)

    @pl.when(step == 0)
    def _():
        for first in range(0, HALO, 512):
            rows = slice(first, first + 512)
            late = slice(HALO + first, HALO + first + 512)
            pairs[rows, :] = halo_ref[rows, :]
            pairs[late, :] = own_ref[rows, 128:256]
            pairs_t[:, rows] = halo_ref[rows, :].astype(F32).T.astype(BF)
            pairs_t[:, late] = own_ref[rows, 128:256].astype(F32).T.astype(BF)

    start = start_ref[0]
    query = own_ref[pl.ds(pl.multiple_of(step * QB, QB), QB), 0:128]
    picks = [placed(query, half, 0) for half in range(2)]
    most[...] = jnp.full(most.shape, masked_score, F32)
    total[...] = jnp.zeros(total.shape, F32)
    blend[...] = jnp.zeros(blend.shape, F32)

    def visit(block, carry):
        first = pl.multiple_of(block * KB, KB)
        allowed = allowed_pairs(first, KB, step, start)
        pair = pairs[pl.ds(first, KB), :]
        value = pairs_t[HD:128, pl.ds(first, KB)]
        raw = [nt(pair, picks[half]) for half in range(2)]
        for half in range(2):
            scores = jnp.where(allowed, raw[half] * (attend_scale * LOG2E), masked_score)
            before = most[half : half + 1, :]
            top = jnp.maximum(before, jnp.max(scores, axis=0, keepdims=True))
            weight = jnp.exp2(scores - top)
            fade = jnp.exp2(before - top)
            most[half : half + 1, :] = top
            total[half : half + 1, :] = total[half : half + 1, :] * fade + jnp.sum(
                weight, axis=0, keepdims=True
            )
            rows = slice(half * HD, half * HD + HD)
            blend[rows, :] = blend[rows, :] * fade + nn(value, weight.astype(BF))
        return carry

    lax.fori_loop(low_ref[step], (HALO + (step + 1) * QB) // KB, visit, 0)
    for half in range(2):
        rows = slice(half * HD, half * HD + HD)
        blend[rows, :] = blend[rows, :] / total[half : half + 1, :]
    out_ref[...] = blend[...].T.astype(BF)
    log_ref[0:2, :] = most[0:2, :] + jnp.log2(total[0:2, :])
    log_ref[2:8, :] = jnp.zeros((6, QB), F32)


def attend(low_block, own, halo, start):
    spec = lambda shape, index: pl.BlockSpec(shape, index)
    return pl.pallas_call(
        attend_kernel,
        out_shape=(shaped((2048, 128), BF), shaped((8, 2048), F32)),
        grid_spec=pltpu.PrefetchScalarGridSpec(
            num_scalar_prefetch=1,
            grid=(2048 // QB,),
            in_specs=[
                spec((2048, 256), lambda i, low: (0, 0)),
                spec((2048, 128), lambda i, low: (0, 0)),
                spec((1, 1, QB), lambda i, low: (i, 0, 0)),
            ],
            out_specs=(
                spec((QB, 128), lambda i, low: (i, 0)),
                spec((8, QB), lambda i, low: (0, i)),
            ),
            scratch_shapes=[
                pltpu.VMEM((2 * HALO, 128), BF),
                pltpu.VMEM((128, 2 * HALO), BF),
                pltpu.VMEM((8, QB), F32),
                pltpu.VMEM((8, QB), F32),
                pltpu.VMEM((128, QB), F32),
            ],
        ),
        compiler_params=params(),
        cost_estimate=cost(12e9, 3e6),
        name="attend",
    )(low_block, own, halo, start)


def attend_back_kernel(
    low_ref, own_ref, halo_ref, start_ref, out_ref, grad_ref, log_ref,
    own_grad_ref, halo_grad_ref, pairs, pairs_t, pair_grad, blend,
):
    step = pl.program_id(0)

    @pl.when(step == 0)
    def _():
        for first in range(0, HALO, 512):
            rows = slice(first, first + 512)
            late = slice(HALO + first, HALO + first + 512)
            pairs[rows, :] = halo_ref[rows, :]
            pairs[late, :] = own_ref[rows, 128:256]
            pairs_t[:, rows] = halo_ref[rows, :].astype(F32).T.astype(BF)
            pairs_t[:, late] = own_ref[rows, 128:256].astype(F32).T.astype(BF)
        pair_grad[...] = jnp.zeros(pair_grad.shape, F32)

    start = start_ref[0]
    here_rows = pl.ds(pl.multiple_of(step * QB, QB), QB)
    query, grad = own_ref[here_rows, 0:128], grad_ref[...]
    product = (out_ref[...].astype(F32) * grad.astype(F32)).T
    picks, incoming, centres = [], [], []
    for half in range(2):
        picks.append(placed(query, half, 0))
        incoming.append(placed(grad, half, 1))
        centres.append(jnp.sum(product[half * HD : half * HD + HD, :], axis=0, keepdims=True))
    blend[...] = jnp.zeros(blend.shape, F32)

    def visit(block, carry):
        first = pl.multiple_of(block * BACK_KB, BACK_KB)
        allowed = allowed_pairs(first, BACK_KB, step, start)
        here = pl.ds(first, BACK_KB)
        pair, key_t = pairs[here, :], pairs_t[0:HD, here]
        for half in range(2):
            scores = nt(pair, picks[half]) * (attend_scale * LOG2E)
            weight = jnp.where(allowed, jnp.exp2(scores - log_ref[half : half + 1, :]), 0.0)
            weight_grad = nt(pair, incoming[half])
            score_grad = (
                weight * (weight_grad - centres[half]) * attend_scale
            ).astype(BF)
            pair_grad[here, :] += nn(weight.astype(BF), incoming[half]) + nn(
                score_grad, picks[half]
            )
            blend[half * HD : half * HD + HD, :] += nn(key_t, score_grad)
        return carry

    lax.fori_loop(low_ref[step], (HALO + (step + 1) * QB) // BACK_KB, visit, 0)
    own_grad_ref[here_rows, 0:128] = blend[...].T

    @pl.when(step == pl.num_programs(0) - 1)
    def _():
        for first in range(0, HALO, 512):
            rows = slice(first, first + 512)
            late = slice(HALO + first, HALO + first + 512)
            halo_grad_ref[rows, :] = pair_grad[rows, :].astype(BF)
            own_grad_ref[rows, 128:256] = pair_grad[late, :]


def attend_back(low_block, own, halo, start, out, grad, logs):
    spec = lambda shape, index: pl.BlockSpec(shape, index)
    tile = spec((QB, 128), lambda i, low: (i, 0))
    whole = spec((2048, 256), lambda i, low: (0, 0))
    half = spec((2048, 128), lambda i, low: (0, 0))
    return pl.pallas_call(
        attend_back_kernel,
        out_shape=(shaped((2048, 256), F32), shaped((2048, 128), BF)),
        grid_spec=pltpu.PrefetchScalarGridSpec(
            num_scalar_prefetch=1,
            grid=(2048 // QB,),
            in_specs=[
                whole,
                half,
                spec((1, 1, QB), lambda i, low: (i, 0, 0)),
                tile,
                tile,
                spec((8, QB), lambda i, low: (0, i)),
            ],
            out_specs=(whole, half),
            scratch_shapes=[
                pltpu.VMEM((2 * HALO, 128), BF),
                pltpu.VMEM((128, 2 * HALO), BF),
                pltpu.VMEM((2 * HALO, 128), F32),
                pltpu.VMEM((128, QB), F32),
            ],
        ),
        compiler_params=params(),
        cost_estimate=cost(30e9, 6e6),
        name="attend_back",
    )(low_block, own, halo, start, out, grad, logs)


def after_kernel(
    plan, me_ref, tokens_ref, first_ref, second_ref, extra_ref, routed_ref, *refs
):
    count = len(plan)
    hidden_ref, payload_ref, gates_ref, mats, sems = refs[count:]
    copies = start_fetch_out(me_ref[0], plan, refs[:count], mats, sems)
    stream = tokens_ref[...].astype(F32)
    for copy in copies:
        copy.wait()
    branch = jnp.zeros((512, 1024), F32)
    for part in range(4):
        both = jnp.concatenate([first_ref[part], second_ref[part]], axis=1)
        branch += nn(both, mats[part * 256 : part * 256 + 256, :])
    hidden = stream + branch_scale * branch
    hidden_ref[...] = hidden
    inverse = lax.rsqrt(jnp.mean(hidden * hidden, axis=-1, keepdims=True) + norm_eps)
    normed = (hidden * inverse * extra_ref[33:34, :].astype(F32)).astype(BF)
    payload_ref[0:512, :] = normed
    logits = nt(extra_ref[0:32, :], normed)
    routed = routed_ref[...] > 0.5
    top = jnp.max(jnp.where(routed, logits, masked_score), axis=0, keepdims=True)
    raised = jnp.where(routed, jnp.exp(logits - top), 0.0)
    gates = raised / jnp.sum(raised, axis=0, keepdims=True)
    gates_ref[...] = gates
    low = gates.astype(BF)
    payload_ref[512:528, 0:512] = low[0:16, :]
    payload_ref[512:528, 512:1024] = low[16:32, :]


def after_attention(me, tokens, attended, extra, routed, pieces):
    plan = plan_of(128)
    return pl.pallas_call(
        functools.partial(after_kernel, plan),
        out_shape=(shaped((512, 1024), F32), shaped((528, 1024), BF), shaped((32, 512), F32)),
        in_specs=[in_smem()] + in_vmem(5) + in_hbm(len(plan)),
        out_specs=tuple(in_vmem(3)),
        scratch_shapes=[pltpu.VMEM((1024, 1024), BF), pltpu.SemaphoreType.DMA((len(plan),))],
        compiler_params=params(),
        cost_estimate=cost(2 * 512 * 1024 * 1024, 8e6),
        name="after_attention",
    )(me, tokens, *attended, extra, routed, *pieces)


def own_rows(me, packed):
    first = me * 4
    side = jnp.where(first < 16, packed[:, :512], packed[:, 512:])
    row = lax.broadcasted_iota(jnp.int32, side.shape, 0)
    return [
        jnp.sum(jnp.where(row == first % 16 + expert, side, 0.0), axis=0, keepdims=True)
        for expert in range(4)
    ]


def stand_up(rows):
    row = lax.broadcasted_iota(jnp.int32, (128, 512), 0)
    lying = jnp.zeros((128, 512), F32)
    for number, values in enumerate(rows):
        lying = jnp.where(row == number, values, lying)
    return lying.T


def slot_hot(slot_row):
    at = lax.broadcasted_iota(jnp.int32, (144, 512), 0).astype(F32)
    return at == slot_row


def block_plan(partners, height):
    return tuple(
        (partners.index(partner), first, min(rows, 528 - first))
        for partner, first, rows in plan_of(height)
        if partner in partners
    )


def start_blocks(plan, sources, target, sems):
    copies = []
    for number, (place, first, rows) in enumerate(plan):
        copies.append(
            pltpu.make_async_copy(
                sources[number].at[pl.ds(0, rows)],
                target.at[place, pl.ds(first, rows)],
                sems.at[number],
            )
        )
        copies[-1].start()
    return copies


def pick_grad_kernel(plan, blocks, me_ref, *refs):
    count = len(plan)
    rows_ref, slots_ref, columns_ref, held, made, sems, out_sems = refs[count:]
    copies = start_blocks(plan, refs[:count], held, sems)
    leaving = []
    for block in range(blocks):
        for copy, (place, _, _) in zip(copies, plan):
            if place == block:
                copy.wait()
        tokens = held[block, 0:512, :]
        slots = own_rows(me_ref[0], held[block, 512:528, :].astype(F32))
        for expert in range(4):
            hot = jnp.where(slot_hot(slots[expert]), 1.0, 0.0).astype(BF)
            made[block, expert * 144 : expert * 144 + 144, :] = nn(hot, tokens).astype(BF)
            slots_ref[block, expert : expert + 1, :] = slots[expert]
        columns_ref[block] = stand_up(slots).astype(BF)
        leaving.append(
            pltpu.make_async_copy(made.at[block], rows_ref.at[block], out_sems.at[block])
        )
        leaving[-1].start()
    for copy in leaving:
        copy.wait()


def pick_grads(me, partners, pieces):
    blocks, plan = len(partners), block_plan(partners, 528)
    return pl.pallas_call(
        functools.partial(pick_grad_kernel, plan, blocks),
        out_shape=(
            shaped((blocks, 576, 1024), BF),
            shaped((blocks, 4, 512), F32),
            shaped((blocks, 512, 128), BF),
        ),
        in_specs=[in_smem()] + in_hbm(len(pieces)),
        out_specs=tuple(in_hbm(1) + in_vmem(2)),
        scratch_shapes=[
            pltpu.VMEM((blocks, 528, 1024), BF),
            pltpu.VMEM((blocks, 576, 1024), BF),
            pltpu.SemaphoreType.DMA((len(pieces),)),
            pltpu.SemaphoreType.DMA((blocks,)),
        ],
        compiler_params=params(),
        cost_estimate=cost(blocks * 2 * 576 * 512 * 1024, blocks * 2.4e6),
        name="pick_grads",
    )(me, *pieces)


def pick_rows_kernel(plan, blocks, me_ref, slots_ref, *refs):
    count = len(plan)
    rows_ref, gate_ref, columns_ref, held, made, sems, out_sems = refs[count:]
    copies = start_blocks(plan, refs[:count], held, sems)
    leaving = []
    for block in range(blocks):
        for copy, (place, _, _) in zip(copies, plan):
            if place == block:
                copy.wait()
        tokens = held[block, 0:512, :]
        gates = own_rows(me_ref[0], held[block, 512:528, :].astype(F32))
        for expert in range(4):
            match = slot_hot(slots_ref[block, expert : expert + 1, :])
            hot = jnp.where(match, 1.0, 0.0).astype(BF)
            rows = slice(expert * 144, expert * 144 + 144)
            made[block, rows, :] = nn(hot, tokens).astype(BF)
            gate = jnp.sum(jnp.where(match, gates[expert], 0.0), axis=1, keepdims=True)
            gate_ref[block, rows, :] = jnp.broadcast_to(gate, (144, 128)).astype(BF)
        columns_ref[block] = stand_up(gates).astype(BF)
        leaving.append(
            pltpu.make_async_copy(made.at[block], rows_ref.at[block], out_sems.at[block])
        )
        leaving[-1].start()
    for copy in leaving:
        copy.wait()


def pick_rows(me, slots, partners, pieces):
    blocks, plan = len(partners), block_plan(partners, 528)
    return pl.pallas_call(
        functools.partial(pick_rows_kernel, plan, blocks),
        out_shape=(
            shaped((blocks, 576, 1024), BF),
            shaped((blocks, 576, 128), BF),
            shaped((blocks, 512, 128), BF),
        ),
        in_specs=[in_smem()] + in_vmem(1) + in_hbm(len(pieces)),
        out_specs=tuple(in_hbm(1) + in_vmem(2)),
        scratch_shapes=[
            pltpu.VMEM((blocks, 528, 1024), BF),
            pltpu.VMEM((blocks, 576, 1024), BF),
            pltpu.SemaphoreType.DMA((len(pieces),)),
            pltpu.SemaphoreType.DMA((blocks,)),
        ],
        compiler_params=params(),
        cost_estimate=cost(blocks * 2 * 576 * 512 * 1024, blocks * 2.4e6),
        name="pick_rows",
    )(me, slots, *pieces)


def both_parts(pair, part):
    if part == 0:
        return pair[0][0:4].reshape(576, -1)
    return jnp.concatenate([pair[0][4:6].reshape(288, -1), pair[1][...].reshape(288, -1)], axis=0)


def expert_grad_kernel(*refs):
    rows_refs, grads_refs, gate_refs = refs[0:2], refs[2:4], refs[4:6]
    gate_w, up_w, down_w = (ref[0] for ref in refs[6:9])
    lin_ref, inner_ref, grad_ref = refs[9:12]
    lin_grads, inners, out_grads, inputs = refs[12:16]
    for part in range(2):
        at = slice(part * 576, part * 576 + 576)
        blocks = slice(part * 4, part * 4 + 4)
        rows = both_parts(rows_refs, part)
        inputs[at, :] = rows
        gate_lin = nn(rows, gate_w)
        up_lin = nn(rows, up_w)
        sigma = 1.0 / (1.0 + jnp.exp(-gate_lin))
        swished = gate_lin * sigma
        inner = (swished * up_lin).astype(BF)
        inners[at, :] = inner
        inner_ref[blocks] = inner.reshape(4, 144, 512)
        gate = both_parts(gate_refs, part)[:, 0:1].astype(F32)
        out_grad = (both_parts(grads_refs, part).astype(F32) * gate).astype(BF)
        out_grads[at, :] = out_grad
        inner_grad = nt(out_grad, down_w)
        lin_grads[at, 0:512] = (
            inner_grad * up_lin * sigma * (1.0 + gate_lin * (1.0 - sigma))
        ).astype(BF)
        lin_grads[at, 512:1024] = (inner_grad * swished).astype(BF)
        lin_ref[blocks] = lin_grads[at, :].reshape(4, 144, 1024)
    down_grad = tn(inners[...], out_grads[...]).astype(BF)
    grad_ref[2048:2560, :] = down_grad[:, 0:512]
    grad_ref[2560:3072, :] = down_grad[:, 512:1024]
    grad_ref[0:1024, :] = tn(inputs[...], lin_grads[:, 0:512]).astype(BF)
    grad_ref[1024:2048, :] = tn(inputs[...], lin_grads[:, 512:1024]).astype(BF)


def expert_grads(base, count, rows, grads, gates, gate_w, up_w, down_w):
    spec = pl.BlockSpec
    wide = [spec((blocks, 144, 1024), lambda e: (0, base + e, 0)) for blocks in (6, 2)]
    slim = [spec((blocks, 144, 128), lambda e: (0, base + e, 0)) for blocks in (6, 2)]
    tall_w = spec((1, 1024, 512), lambda e: (base + e, 0, 0))
    flat_w = spec((1, 512, 1024), lambda e: (base + e, 0, 0))
    return pl.pallas_call(
        expert_grad_kernel,
        out_shape=(
            shaped((8, 144 * count, 1024), BF),
            shaped((8, 144 * count, 512), BF),
            shaped((3072 * count, 512), BF),
        ),
        grid=(count,),
        in_specs=wide * 2 + slim + [tall_w, tall_w, flat_w],
        out_specs=(
            spec((8, 144, 1024), lambda e: (0, e, 0)),
            spec((8, 144, 512), lambda e: (0, e, 0)),
            spec((3072, 512), lambda e: (e, 0)),
        ),
        scratch_shapes=[
            pltpu.VMEM((1152, 1024), BF),
            pltpu.VMEM((1152, 512), BF),
            pltpu.VMEM((1152, 1024), BF),
            pltpu.VMEM((1152, 1024), BF),
        ],
        compiler_params=params(),
        cost_estimate=cost(count * 8e9, count * 15e6),
        name="expert_grads",
    )(*rows, *grads, *gates, gate_w, up_w, down_w)


def expert_rows_kernel(base, me_ref, lin_ref, inner_ref, *refs):
    grads_refs = refs[0:2]
    gate_w, up_w, down_w = (ref[0] for ref in refs[2:5])
    out_ref, in_grad_ref, mark_ref = refs[5:8]
    expert = me_ref[0] * 4 + base + pl.program_id(0)
    lane = lax.broadcasted_iota(jnp.int32, (576, 128), 1)
    for part in range(2):
        blocks = slice(part * 4, part * 4 + 4)
        result = nn(inner_ref[blocks].reshape(576, 512), down_w).astype(BF)
        out_ref[blocks] = result.reshape(4, 144, 1024)
        wide = both_parts(grads_refs, part).astype(F32)
        gate_slot = jnp.sum(wide * result.astype(F32), axis=1, keepdims=True)
        mark_ref[blocks] = jnp.where(lane == expert, gate_slot, 0.0).astype(BF).reshape(4, 144, 128)
        lin = lin_ref[blocks].reshape(576, 1024)
        in_grad_ref[blocks] = (
            (nt(lin[:, 0:512], gate_w) + nt(lin[:, 512:1024], up_w))
            .astype(BF)
            .reshape(4, 144, 1024)
        )


def expert_rows(me, base, count, lin, inner, grads, gate_w, up_w, down_w):
    spec = pl.BlockSpec
    wide = [spec((blocks, 144, 1024), lambda e: (0, base + e, 0)) for blocks in (6, 2)]
    tall_w = spec((1, 1024, 512), lambda e: (base + e, 0, 0))
    flat_w = spec((1, 512, 1024), lambda e: (base + e, 0, 0))
    own = lambda width: spec((8, 144, width), lambda e: (0, e, 0))
    return pl.pallas_call(
        functools.partial(expert_rows_kernel, base),
        out_shape=(
            shaped((8, 144 * count, 1024), BF),
            shaped((8, 144 * count, 1024), BF),
            shaped((8, 144 * count, 128), BF),
        ),
        grid=(count,),
        in_specs=[in_smem(), own(1024), own(512)] + wide + [tall_w, tall_w, flat_w],
        out_specs=(own(1024), own(1024), own(128)),
        compiler_params=params(),
        cost_estimate=cost(count * 4e9, count * 14e6),
        name="expert_rows",
    )(me, lin, inner, *grads, gate_w, up_w, down_w)


def combine_kernel(calls, weighted, *refs):
    slot_ref = refs[0]
    refs = refs[1:]
    gate_ref = None
    if weighted:
        gate_ref, refs = refs[0], refs[1:]
    value_refs, refs = refs[:calls], refs[calls:]
    mark_refs = ()
    if not weighted:
        mark_refs, refs = refs[:calls], refs[calls:]
    out_ref = refs[0]
    here = 4 // calls
    slots = slot_ref[0].astype(F32)
    lane = lax.broadcasted_iota(jnp.int32, (512, 144 * here), 1).astype(F32)
    total, marks = None, None
    for call in range(calls):
        hot = jnp.zeros((512, 144 * here), F32)
        for local_expert in range(here):
            number = call * here + local_expert
            slot = slots[:, number : number + 1]
            place = jnp.where(slot < 144.0, slot + 144.0 * local_expert, -1.0)
            put = 1.0
            if weighted:
                put = gate_ref[0][:, number : number + 1].astype(F32)
            hot = jnp.where(lane == place, put, hot)
        hot = hot.astype(BF)
        term = nn(hot, value_refs[call][0])
        total = term if total is None else total + term
        if not weighted:
            mark = nn(hot, mark_refs[call][0])
            marks = mark if marks is None else marks + mark
    out_ref[0, 0:512, :] = total.astype(BF)
    if not weighted:
        lying = marks.T[0:32, :].astype(BF)
        out_ref[0, 512:528, 0:512] = lying[0:16, :]
        out_ref[0, 512:528, 512:1024] = lying[16:32, :]


def combine(parity, slots, gates, values, marks):
    calls = len(values)
    weighted = gates is not None
    rows = 512 if weighted else 528
    column = pl.BlockSpec((1, 512, 128), lambda i: (2 * i + parity, 0, 0))
    wide = pl.BlockSpec((1, 576 // calls, 1024), lambda i: (2 * i + parity, 0, 0))
    slim = pl.BlockSpec((1, 576 // calls, 128), lambda i: (2 * i + parity, 0, 0))
    args = [slots] + ([gates] if weighted else []) + list(values) + list(marks)
    return pl.pallas_call(
        functools.partial(combine_kernel, calls, weighted),
        out_shape=shaped((4, rows, 1024), BF),
        grid=(4,),
        in_specs=[column]
        + ([column] if weighted else [])
        + [wide] * calls
        + [slim] * len(marks),
        out_specs=pl.BlockSpec((1, rows, 1024), lambda i: (i, 0, 0)),
        compiler_params=params(),
        cost_estimate=cost(4 * 2 * 512 * 768 * 1024, 10e6),
        name="combine",
    )(*args)


def back_kernel(
    plan, me_ref, sum_ref, sum_x_ref, sum_y_ref, hidden_ref, cot_ref, payload_ref, gates_ref,
    extra_ref, *refs,
):
    count = len(plan)
    hidden_grad_ref, branch_grad_ref, first_ref, second_ref, small_ref, mats, sems = refs[count:]
    copies = start_fetch_out(me_ref[0], plan, refs[:count], mats, sems)
    total = (
        sum_ref[...].astype(F32) + sum_x_ref[...].astype(F32) + sum_y_ref[...].astype(F32)
    )
    gate_grad = jnp.concatenate([total[512:528, 0:512], total[512:528, 512:1024]], axis=0)
    gates = gates_ref[...]
    logit_grad = (
        gates * (gate_grad - jnp.sum(gates * gate_grad, axis=0, keepdims=True))
    ).astype(BF)
    normed_grad = total[0:512, :] + tn(logit_grad, extra_ref[0:32, :])
    hidden = hidden_ref[...]
    inverse = lax.rsqrt(jnp.mean(hidden * hidden, axis=-1, keepdims=True) + norm_eps)
    scaled = normed_grad * extra_ref[33:34, :].astype(F32)
    spread_out = inverse * inverse * inverse * jnp.mean(hidden * scaled, axis=-1, keepdims=True)
    hidden_grad = cot_ref[...].astype(F32) + inverse * scaled - hidden * spread_out
    hidden_grad_ref[...] = hidden_grad
    small_ref[0:32, :] = nn(logit_grad, payload_ref[0:512, :])
    small_ref[32:40, :] = jnp.broadcast_to(
        jnp.sum(normed_grad * hidden * inverse, axis=0, keepdims=True), (8, 1024)
    )
    branch_grad = (branch_scale * hidden_grad).astype(BF)
    branch_grad_ref[...] = branch_grad
    for copy in copies:
        copy.wait()
    for part in range(4):
        grad = nt(branch_grad, mats[part * 256 : part * 256 + 256, :]).astype(BF)
        first_ref[part] = grad[:, 0:128]
        second_ref[part] = grad[:, 128:256]


def back_to_attention(me, sums, hidden, cotangent, payload, gates, extra, pieces):
    plan = plan_of(128)
    return pl.pallas_call(
        functools.partial(back_kernel, plan),
        out_shape=(
            shaped((512, 1024), F32),
            shaped((512, 1024), BF),
            shaped((4, 512, 128), BF),
            shaped((4, 512, 128), BF),
            shaped((40, 1024), F32),
        ),
        in_specs=[in_smem()] + in_vmem(8) + in_hbm(len(plan)),
        out_specs=tuple(in_vmem(5)),
        scratch_shapes=[pltpu.VMEM((1024, 1024), BF), pltpu.SemaphoreType.DMA((len(plan),))],
        compiler_params=params(),
        cost_estimate=cost(2 * 512 * 1024 * 1024, 12e6),
        name="back_to_attention",
    )(me, *sums, hidden, cotangent, payload, gates, extra, *pieces)


def deal_out(me, big, odd_ref, even_ref):
    for pair in range(4):
        for target, partner in ((even_ref, 2 * pair), (odd_ref, 2 * pair + 1)):
            start = pl.multiple_of((me ^ partner) * 128, 128)
            target[pair] = big[pl.ds(start, 128), :]


def out_grad_kernel(me_ref, first_ref, second_ref, branch_grad_ref, small_ref, odd_ref, even_ref, big):
    branch_grad = branch_grad_ref[...]
    for part in range(4):
        both = jnp.concatenate([first_ref[part], second_ref[part]], axis=1)
        big[part * 256 : part * 256 + 256, 0:1024] = tn(both, branch_grad).astype(BF)
    small = jnp.concatenate([small_ref[...], jnp.zeros((88, 1024), F32)], axis=0)
    big[:, 1024:1152] = small.T.astype(BF)
    deal_out(me_ref[0], big, odd_ref, even_ref)


def out_grads_of(me, attended, branch_grad, small):
    return pl.pallas_call(
        out_grad_kernel,
        out_shape=(shaped((4, 128, 1152), BF), shaped((4, 128, 1152), BF)),
        in_specs=[in_smem()] + in_vmem(4),
        out_specs=tuple(in_vmem(2)),
        scratch_shapes=[pltpu.VMEM((1024, 1152), BF)],
        compiler_params=params(),
        cost_estimate=cost(2 * 512 * 1024 * 1024, 5e6),
        name="out_grads",
    )(me, *attended, branch_grad, small)


def input_kernel(
    plan, me_ref, tokens_ref, cos_ref, sin_ref, first_ref, second_ref, extra_ref,
    hidden_grad_ref, *refs,
):
    count = len(plan)
    input_grad_ref, odd_ref, even_ref, mats, big, lin, sems = refs[count:]
    me = me_ref[0]
    copies = start_fetch(me, plan, refs[:count], mats, 128, sems)
    stream = tokens_ref[...].astype(F32)
    inverse = lax.rsqrt(jnp.mean(stream * stream, axis=-1, keepdims=True) + norm_eps)
    gain = extra_ref[32:33, :].astype(F32)
    normed = (stream * inverse * gain).astype(BF)
    cosine, sine = cos_ref[...], -sin_ref[...]
    for part in range(4):
        tiles = []
        for group, source in enumerate((first_ref, second_ref)):
            lin[:, part * 256 + group * 128 : part * 256 + group * 128 + 128] = turn(
                source[part, :, 0:128].astype(F32), cosine, sine
            ).astype(BF)
            tiles.append(source[part, :, 128:256].astype(F32))
        lane = lax.broadcasted_iota(jnp.int32, tiles[0].shape, 1)
        key = jnp.where(lane < HD, tiles[0], pltpu.roll(tiles[1], HD, 1))
        value = jnp.where(lane < HD, pltpu.roll(tiles[0], HD, 1), tiles[1])
        lin[:, 1024 + part * 128 : 1152 + part * 128] = turn(key, cosine, sine).astype(BF)
        lin[:, 1536 + part * 128 : 1664 + part * 128] = value.astype(BF)
    normed_t = normed.astype(F32).T.astype(BF)
    for first in range(0, 2048, 512):
        big[:, first : first + 512] = nn(normed_t, lin[:, first : first + 512]).astype(BF)
    for copy in copies:
        copy.wait()
    normed_grad = nt(lin[...], mats[:, 0:2048])
    row = jnp.sum(normed_grad * stream * inverse, axis=0, keepdims=True)
    big[:, 2048:2176] = jnp.broadcast_to(row, (128, 1024)).T.astype(BF)
    deal_out(me, big, odd_ref, even_ref)
    scaled = normed_grad * gain
    spread_out = inverse * inverse * inverse * jnp.mean(stream * scaled, axis=-1, keepdims=True)
    input_grad_ref[...] = (
        hidden_grad_ref[...] + inverse * scaled - stream * spread_out
    ).astype(BF)


def input_grads(me, tokens, cosine, sine, query_grad, pair_grad, extra, hidden_grad, pieces):
    plan = plan_of(128)
    return pl.pallas_call(
        functools.partial(input_kernel, plan),
        out_shape=(
            shaped((512, 1024), BF),
            shaped((4, 128, 2176), BF),
            shaped((4, 128, 2176), BF),
        ),
        in_specs=[in_smem()] + in_vmem(7) + in_hbm(len(plan)),
        out_specs=tuple(in_vmem(3)),
        scratch_shapes=[
            pltpu.VMEM((1024, 2176), BF),
            pltpu.VMEM((1024, 2176), BF),
            pltpu.VMEM((512, 2048), BF),
            pltpu.SemaphoreType.DMA((len(plan),)),
        ],
        compiler_params=params(),
        cost_estimate=cost(4 * 512 * 1024 * 2048, 15e6),
        name="input_grads",
    )(me, tokens, cosine, sine, query_grad, pair_grad, extra, hidden_grad, *pieces)


def dense_slots(routes, ranks, experts):
    mine = routes[None, :, :] == jnp.arange(experts, dtype=jnp.int32)[:, None, None]
    far = jnp.int32(1 << 20)
    rank = jnp.min(jnp.where(mine, ranks[None, :, :], far), axis=-1)
    slot = jnp.sum((rank[:, None, :] < rank[:, :, None]).astype(jnp.int32), axis=-1)
    routed = rank < far
    return (jnp.where(routed & (slot < 144), slot, 255).astype(BF), routed.astype(F32))


def across(values):
    return lax.all_to_all(values, "sp", split_axis=0, concat_axis=0, tiled=True)


def sum_shared(value):
    rows, columns = value.shape
    quarters = across(value).reshape(4, rows // 4, columns).astype(F32)
    quarter = jnp.sum(quarters, axis=0).astype(BF)
    return across(jnp.tile(quarter, (4, 1)))


def sum_line(value, seq):
    outer = (seq == 0) | (seq == 3)
    value = add_low(value, lax.ppermute(value, "sp", ((0, 1), (3, 2))))
    value = add_low(value, lax.ppermute(value, "sp", ((1, 2), (2, 1))))
    return jnp.where(outer, lax.ppermute(value, "sp", ((1, 0), (2, 3))), value)


def fast_local(
    tokens, documents, expert_routes, drop_rank, norm1_gain, query_weight, key_weight,
    value_weight, out_weight, norm2_gain, router_weight, gate_weight, up_weight, down_weight,
    output_grad,
):
    fsdp = lax.axis_index("fsdp")
    seq = lax.axis_index("sp")
    me = jnp.reshape(fsdp, (1,)).astype(jnp.int32)
    small = jnp.concatenate(
        [
            router_weight,
            norm1_gain[:, None],
            norm2_gain[:, None],
            jnp.zeros((128, 94), BF),
        ],
        axis=1,
    )
    shard = jnp.concatenate(
        [query_weight, key_weight, value_weight, small, out_weight], axis=1
    )
    project_pieces = spread(shard)

    slots, routed = dense_slots(expert_routes, drop_rank, 32)
    mixture_grad = (branch_scale * output_grad.astype(F32)).astype(BF)
    grad_payload = jnp.concatenate(
        [mixture_grad, jnp.concatenate([slots[:16], slots[16:]], axis=1)], axis=0
    )

    block_start = fsdp * 2048
    position_all = doc_position(documents)
    position_span = lax.dynamic_slice_in_dim(position_all, block_start, 2048)
    position = lax.dynamic_slice_in_dim(position_span, seq * 512, 512)
    cosine, sine_table = rope_tables(position, HD)
    cosine = jnp.tile(cosine, (1, 2))
    signs = jnp.where(jnp.arange(128) % HD < HD // 2, -1.0, 1.0).astype(F32)
    sine = jnp.tile(sine_table, (1, 2)) * signs[None, :]
    start = HALO + jnp.arange(2048, dtype=jnp.int32) - position_span
    start_rows = start.reshape(2048 // QB, 1, QB)
    low_block = start_rows[:, 0, 0] // KB
    low_back = start_rows[:, 0, 0] // BACK_KB

    first, second, extra = project(me, tokens, cosine, sine, project_pieces)
    grad_payload = hold(grad_payload, project_pieces[6], project_pieces[7])
    own, beside = grad_payload, flip(grad_payload, 1)
    along_x, along_y = flip(grad_payload, 2), flip(grad_payload, 4)
    heads = [across(first.reshape(2048, 256)), None]
    heads[0], second, beside, along_x, along_y = lax.optimization_barrier(
        (heads[0], second, beside, along_x, along_y)
    )
    heads[1] = across(second.reshape(2048, 256))
    halos = [from_behind(heads[0][:, 128:256], "fsdp", 1), None]
    near_pieces = (own, beside, along_x, flip(along_x, 1), along_y, flip(along_y, 1))
    blended, logs = [None, None], [None, None]
    blended[0], logs[0] = attend(low_block, heads[0], halos[0], start_rows)
    blended[0], heads[1] = lax.optimization_barrier((blended[0], heads[1]))
    halos[1] = from_behind(heads[1][:, 128:256], "fsdp", 1)
    first_back = across(blended[0])
    near, far = (0, 1, 2, 3, 4, 5), (6, 7)
    near_grads = pick_grads(me, near, near_pieces)
    halos[1], near_grads = lax.optimization_barrier((halos[1], near_grads))
    diagonal = spread_diagonal(near_pieces)
    blended[1], logs[1] = attend(low_block, heads[1], halos[1], start_rows)
    blended[1], first_back, diagonal = lax.optimization_barrier(
        (blended[1], first_back, diagonal)
    )
    attended = [first_back, across(blended[1])]
    far_grads = pick_grads(me, far, spread_far(diagonal))
    all_slot_columns = jnp.concatenate([near_grads[2], far_grads[2]], axis=0)
    attended, near_grads, far_grads, all_slot_columns = lax.optimization_barrier(
        (attended, near_grads, far_grads, all_slot_columns)
    )
    attended = [part.reshape(4, 512, 128) for part in attended]
    grad_rows, slot_rows, _ = zip(near_grads, far_grads)
    hidden_one, payload, gates = after_attention(
        me, tokens, attended, extra, routed, project_pieces
    )
    near_pieces = spread_near(payload)
    diagonal = spread_diagonal(near_pieces)
    near_rows = pick_rows(me, slot_rows[0], near, near_pieces)
    near_rows, diagonal = lax.optimization_barrier((near_rows, diagonal))
    far_rows = pick_rows(me, slot_rows[1], far, spread_far(diagonal))
    rows, slot_gates, gate_columns = zip(near_rows, far_rows)
    mats = (gate_weight, up_weight, down_weight)
    lin_grads, inners, parts = zip(
        *[expert_grads(base, 2, rows, grad_rows, slot_gates, *mats) for base in (0, 2)]
    )
    sums_of_parts = lax.psum(parts, "sp")

    def finish(turn_number, _):
        here, slot_columns = hold((me, all_slot_columns), turn_number)
        outs, in_grads, marks = zip(
            *[
                expert_rows(here, 2 * pair, 2, lin_grads[pair], inners[pair], grad_rows, *mats)
                for pair in range(2)
            ]
        )
        odd = combine(1, slot_columns, None, in_grads, marks)
        even = combine(0, slot_columns, None, in_grads, marks)
        sums = collect(odd, even)
        hidden_grad, branch_grad, first_grad, second_grad, small_grads = back_to_attention(
            me, sums, hidden_one, output_grad, payload, gates, extra, project_pieces
        )
        first_heads = across(first_grad.reshape(2048, 128))
        first_heads, second_grad = lax.optimization_barrier((first_heads, second_grad))
        second_heads = across(second_grad.reshape(2048, 128))
        first_own, first_halo = attend_back(
            low_back, heads[0], halos[0], start_rows, blended[0], first_heads, logs[0]
        )
        first_own, first_halo, second_heads = lax.optimization_barrier(
            (first_own, first_halo, second_heads)
        )
        held_outs, held_gates = hold((outs, gate_columns), first_heads)
        held_gates = jnp.concatenate(held_gates, axis=0)
        odd_mix = combine(1, slot_columns, held_gates, held_outs, ())
        even_mix = combine(0, slot_columns, held_gates, held_outs, ())
        mixture = collect(odd_mix, even_mix)
        output = (
            hidden_one
            + branch_scale
            * (mixture[0].astype(F32) + mixture[1].astype(F32) + mixture[2].astype(F32))
        ).astype(BF)
        out_sums = collect(*out_grads_of(me, attended, branch_grad, small_grads))

        def grads_home(own_grad, halo_grad):
            returned = from_behind(halo_grad, "fsdp", -1).astype(F32)
            own_grad = own_grad + jnp.pad(returned, ((0, 0), (128, 0)))
            return across(own_grad.astype(BF)).reshape(4, 512, 256)

        first_home = grads_home(first_own, first_halo)
        second_own, second_halo = attend_back(
            low_back, heads[1], halos[1], start_rows, blended[1], second_heads, logs[1]
        )
        second_own, second_halo, first_home = lax.optimization_barrier(
            (second_own, second_halo, first_home)
        )
        second_home = grads_home(second_own, second_halo)
        input_grad, odd_in, even_in = input_grads(
            me, tokens, cosine, sine, first_home, second_home, extra, hidden_grad, project_pieces
        )
        in_sums = collect(odd_in, even_in)

        out_shard = sum(term.astype(F32) for term in out_sums).astype(BF)
        in_shard = sum(term.astype(F32) for term in in_sums).astype(BF)
        in_total = sum_shared(in_shard).astype(F32)
        out_total = sum_line(out_shard, seq).astype(F32)
        return (
            output,
            input_grad,
            in_total[:, 2048],
            in_total[:, 0:1024],
            in_total[:, 1024:1536],
            in_total[:, 1536:2048],
            out_total[:, 0:1024],
            out_total[:, 1056],
            out_total[:, 1024:1056],
        )

    rounds = 1 + (documents[0] > 0).astype(jnp.int32)
    results = lax.fori_loop(
        0,
        rounds,
        finish,
        (
            jnp.zeros((512, 1024), BF),
            jnp.zeros((512, 1024), BF),
            jnp.zeros((128,), F32),
            jnp.zeros((128, 1024), F32),
            jnp.zeros((128, 512), F32),
            jnp.zeros((128, 512), F32),
            jnp.zeros((128, 1024), F32),
            jnp.zeros((128,), F32),
            jnp.zeros((128, 32), F32),
        ),
    )
    sums_of_parts = [
        total[first : first + 3072] for total in sums_of_parts for first in (0, 3072)
    ]
    stacked = [
        jnp.stack([total[0:1024] for total in sums_of_parts]).astype(F32),
        jnp.stack([total[1024:2048] for total in sums_of_parts]).astype(F32),
        jnp.stack(
            [
                jnp.concatenate([total[2048:2560], total[2560:3072]], axis=1)
                for total in sums_of_parts
            ]
        ).astype(F32),
    ]
    return (*results, *stacked)


def solution(mesh):
    placed = (
        P(("fsdp", "sp"), None),
        P(),
        P(("fsdp", "sp"), None),
        P(("fsdp", "sp"), None),
        P("fsdp"),
        P("fsdp", None),
        P("fsdp", None),
        P("fsdp", None),
        P("fsdp", None),
        P("fsdp"),
        P("fsdp", None),
        P("fsdp", None, None),
        P("fsdp", None, None),
        P("fsdp", None, None),
        P(("fsdp", "sp"), None),
    )
    fast = mesh.shape["sp"] == 4 and mesh.shape["fsdp"] == 8
    return jax.shard_map(
        fast_local if fast else local,
        mesh=mesh,
        in_specs=placed,
        out_specs=(
            P(("fsdp", "sp"), None),
            P(("fsdp", "sp"), None),
            P("fsdp"),
            P("fsdp", None),
            P("fsdp", None),
            P("fsdp", None),
            P("fsdp", None),
            P("fsdp"),
            P("fsdp", None),
            P("fsdp", None, None),
            P("fsdp", None, None),
            P("fsdp", None, None),
        ),
        check_vma=False,
    )
```
